32 devices in a mesh: batch: 4 (over z), wide: 8 (over y, x, core).
Axes of the slice: x: 2, y: 2, z: 4, core: 2. Of those that a mesh axis runs over, the one named last changes fastest.
Arguments:
- activations: bfloat16 [2, 128, 64, 2048], P(None, 'batch', 'wide'), may hold values from -6 to 6
- bucket_ids: int32 [2, 128], P(None, 'batch'), may hold values from 0 to 7
- thresholds: bfloat16 [2, 128, 64, 2048], P(None, 'batch', 'wide'), may hold values from 0 to 1
- head_cot: bfloat16 [2, 128, 64, 768], P(None, 'batch', 'wide'), may hold values from -6 to 6
- w_reduce: bfloat16 [2, 2048, 512], replicated, may hold values from -0.125 to 0.125
- w_spatial: bfloat16 [2, 4608, 512], replicated, may hold values from -0.09375 to 0.09375
- w_expand: bfloat16 [2, 2048, 512], replicated, may hold values from -0.25 to 0.25
- gain_mid: float32 [2, 2, 512], replicated, may hold values from 0.5 to 1.5
- shift_mid: float32 [2, 2, 512], replicated, may hold values from -1 to 1
- gain_out: float32 [2, 2048], replicated, may hold values from 0.5 to 1.5
- shift_out: float32 [2, 2048], replicated, may hold values from -1 to 1
- w_heads: bfloat16 [768, 2048], replicated, may hold values from -0.375 to 0.375
Outputs:
- block_out: bfloat16 [2, 128, 64, 2048], P(None, 'batch', 'wide')
- input_grad: bfloat16 [2, 128, 64, 2048], P(None, 'batch', 'wide')
- gw_reduce: float32 [2, 2048, 512], P(None, 'wide')
- gw_spatial: float32 [2, 4608, 512], P(None, 'wide')
- gw_expand: float32 [2, 2048, 512], P(None, 'wide')
- g_gain_mid: float32 [2, 2, 512], replicated
- g_shift_mid: float32 [2, 2, 512], replicated
- g_gain_out: float32 [2, 2048], replicated
- g_shift_out: float32 [2, 2048], replicated
- gw_heads: float32 [768, 2048], P(None, 'wide')
The draws below stay inside these ranges and needn't reach their ends.
Inputs may be any that keep to these rules, and one draw needn't show every extreme that they name: `bucket_ids`: each image's aspect-ratio bucket, an index into the fixed tables of valid rows and columns.
All inputs are finite; a program needn't handle non-finite values.
Results may differ from the reference program's by a relative error of at most 0.025.
Values may be sent and summed in bfloat16 or wider, within the bound.
A program may use at most 192 MiB of HBM per device.

```python
import jax
import jax.numpy as jnp
from jax import lax

D = 2048
MID = 512
HEAD = 256
TASKS = 3
LAYERS = 2
MICRO = 2
FRAME = 8
BUCKETS = 8
POSITIONS = 64
HEADS_ALL = 768
IMAGES = 128
N_WIDE = 8


def draw_activations(key, part):
    key = jax.random.fold_in(key, 11)
    keys = jax.random.split(key, 6)
    full_shape = (MICRO, IMAGES, POSITIONS, D)
    base = jax.random.normal(keys[0], full_shape, jnp.float32)
    quiet_amp = 0.0
    pairing = jax.random.permutation(keys[2], N_WIDE)
    pos_block = jnp.arange(POSITIONS, dtype=jnp.int32) // (POSITIONS // N_WIDE)
    chan_block = jnp.arange(D, dtype=jnp.int32) // (D // N_WIDE)
    paired = pairing[pos_block][:, None] == chan_block[None, :]
    base = base * jnp.where(paired, 2.5, 1.0)
    odd_micro = (jnp.arange(MICRO, dtype=jnp.int32) % 2 == 1)[:, None, None, None]
    level = jnp.where(odd_micro, 1.0, 0.5)
    amplitude = jnp.where(odd_micro, 1.2, quiet_amp)
    image_part = jax.random.normal(keys[3], (MICRO, IMAGES, 1, 1), jnp.float32)
    pixel_part = jax.random.normal(keys[4], (MICRO, IMAGES, POSITIONS, 1), jnp.float32)
    direction = jax.random.normal(keys[5], (MICRO, 1, 1, D), jnp.float32)
    values = level * base + amplitude * (image_part + 0.4 * pixel_part) * direction
    return jnp.clip(values, -6.0, 6.0).astype(jnp.bfloat16)


def place_ends(drawn, rng, least, largest):
    extent = drawn.shape
    spot = [jax.random.randint(jax.random.fold_in(rng, axis), (), 0, extent[axis]) for axis in range(len(extent))]
    drawn = drawn.at[tuple(spot)].set(least)
    longest = extent.index(max(extent))
    spot[longest] = (spot[longest] + 1) % extent[longest]
    return drawn.at[tuple(spot)].set(largest)


def levels(own_key, extent, cuts, low, largest):
    def one(dim, shards_of):
        draws = jax.random.uniform(jax.random.fold_in(jax.random.fold_in(own_key, 6), dim), (shards_of,), jnp.float32, low / len(cuts), largest / len(cuts))
        return jnp.repeat(jnp.exp(draws), extent[dim] // shards_of).reshape((-1,) + (1,) * (len(extent) - dim - 1))

    loudness = one(*cuts[0])
    for cut in cuts[1:]:
        loudness = loudness * one(*cut)
    return loudness


def normal_values(rng, extent, deviation, most, cuts=(), kind=jnp.bfloat16):
    drawn = deviation * jax.random.normal(rng, extent, jnp.float32)
    if cuts:
        drawn = drawn * levels(rng, extent, cuts, -0.22, 0.18)
    return jnp.clip(drawn, -most, most).astype(kind)


def setup_inputs(seed: int = 0) -> dict:
    arg_keys = jax.random.split(jax.random.key(seed), 13)
    activations = draw_activations(jax.random.fold_in(arg_keys[12], 71), 0)
    bucket_ids = place_ends(jax.random.randint(arg_keys[1], (MICRO, IMAGES), 0, BUCKETS), jax.random.fold_in(arg_keys[1], 1), 0, BUCKETS - 1).astype(jnp.int32)
    thresholds = jnp.clip(1.0 * jax.random.uniform(arg_keys[2], (MICRO, IMAGES, POSITIONS, D), jnp.float32) ** levels(arg_keys[2], (MICRO, IMAGES, POSITIONS, D), ((1, 4), (2, 8)), -0.2, 0.2), 0.0, 1.0).astype(jnp.bfloat16)
    head_cot = normal_values(arg_keys[3], (MICRO, IMAGES, POSITIONS, HEADS_ALL), 1.0, 6.0, ((1, 4), (2, 8)))
    w_reduce = normal_values(arg_keys[4], (LAYERS, D, MID), D ** -0.5, 0.125)
    w_spatial = normal_values(arg_keys[5], (LAYERS, 9 * MID, MID), (9 * MID) ** -0.5, 0.09375)
    w_expand = normal_values(arg_keys[6], (LAYERS, D, MID), MID ** -0.5, 0.25)
    gain_mid = jnp.clip(1.0 + 0.1 * jax.random.normal(arg_keys[7], (LAYERS, 2, MID), jnp.float32), 0.5, 1.5)
    shift_mid = normal_values(arg_keys[8], (LAYERS, 2, MID), 0.3, 1.0, (), jnp.float32)
    gain_out = jnp.clip(1.0 + 0.1 * jax.random.normal(arg_keys[9], (LAYERS, D), jnp.float32), 0.5, 1.5)
    shift_out = normal_values(arg_keys[10], (LAYERS, D), 0.3, 1.0, (), jnp.float32)
    w_heads = normal_values(arg_keys[11], (HEADS_ALL, D), HEAD ** -0.5, 0.375)
    return dict(activations=activations, bucket_ids=bucket_ids, thresholds=thresholds, head_cot=head_cot, w_reduce=w_reduce, w_spatial=w_spatial, w_expand=w_expand, gain_mid=gain_mid, shift_mid=shift_mid, gain_out=gain_out, shift_out=shift_out, w_heads=w_heads)


EPS = 1e-05
SHARP = 8.0
FLOOR = 0.25
ROW_TABLE = (8, 8, 7, 6, 8, 5, 7, 8)
COL_TABLE = (8, 7, 8, 8, 6, 8, 7, 5)
HIGH = lax.Precision.HIGHEST

@jax.custom_vjp
def low(v):
    return lax.optimization_barrier(v.astype(jnp.bfloat16)).astype(jnp.float32)

@jax.custom_vjp
def low_back(v):
    return v

def low_keep(v):
    return (low(v), None)

def low_pass(kept, grad):
    return (grad,)

def back_keep(v):
    return (v, None)

def back_low(kept, grad):
    return (low(grad),)
low.defvjp(low_keep, low_pass)
low_back.defvjp(back_keep, back_low)

def frame_mask(buckets, positions):
    bucket_kinds = jnp.arange(len(ROW_TABLE), dtype=jnp.int32)
    onehot = (buckets[..., None] == bucket_kinds).astype(jnp.int32)
    heights = lax.optimization_barrier(jnp.sum(onehot * jnp.array(ROW_TABLE, dtype=jnp.int32), -1))
    widths = lax.optimization_barrier(jnp.sum(onehot * jnp.array(COL_TABLE, dtype=jnp.int32), -1))
    rowpos = positions // FRAME
    colpos = positions % FRAME
    inside = (rowpos < heights[..., None]) & (colpos < widths[..., None])
    return inside.astype(jnp.float32)

def unfold_taps(images):
    padded = jnp.pad(images, ((0, 0), (1, 1), (1, 1), (0, 0)))
    pieces = [padded[:, row_off:row_off + FRAME, col_off:col_off + FRAME, :] for row_off in range(3) for col_off in range(3)]
    return jnp.concatenate(pieces, -1)

def batch_norm(values, valid_rows, scale_vec, offset_vec):
    weighted = values * valid_rows[:, None]
    counts = jnp.sum(valid_rows)
    mean_val = lax.optimization_barrier(jnp.sum(weighted, 0)) / counts
    spread = lax.optimization_barrier(jnp.sum(weighted * values, 0)) / counts - mean_val * mean_val
    return scale_vec * ((values - mean_val) * lax.rsqrt(spread + EPS)) + offset_vec

def trunk_net(carried, valid_rows, w_in, w_mid, w_out, scale_mid, offset_mid, scale_out, offset_out):
    column = valid_rows[:, None]
    for layer_index in range(LAYERS):
        entry_low = low(carried)
        reduced = low_back(jnp.dot(entry_low, w_in[layer_index], precision=HIGH))
        normed = batch_norm(reduced, valid_rows, scale_mid[layer_index, 0], offset_mid[layer_index, 0])
        act_a = low_back(low(jax.nn.silu(normed) * column))
        columns = unfold_taps(act_a.reshape(-1, FRAME, FRAME, MID)).reshape(-1, 9 * MID)
        conv_out = low_back(jnp.dot(columns, w_mid[layer_index], precision=HIGH))
        normed = batch_norm(conv_out, valid_rows, scale_mid[layer_index, 1], offset_mid[layer_index, 1])
        act_b = low_back(low(jax.nn.silu(normed) * column))
        expanded = low_back(jnp.dot(act_b, w_out[layer_index].T, precision=HIGH))
        normed = batch_norm(expanded, valid_rows, scale_out[layer_index], offset_out[layer_index])
        carried = jax.nn.silu(normed + carried) * column
    return carried

def head_maps(values, table):
    return jnp.dot(low(values), table.T, precision=HIGH)

def grad_drop(task_values, limits):
    task_total = task_values[0]
    magnitude = jnp.abs(task_values[0])
    for task_index in range(1, len(task_values)):
        task_total = task_total + task_values[task_index]
        magnitude = magnitude + jnp.abs(task_values[task_index])
    keep_ratio = 0.5 * (1.0 + task_total / jnp.maximum(magnitude, FLOOR))
    upward = jax.nn.sigmoid(SHARP * (keep_ratio - limits))
    downward = jax.nn.sigmoid(SHARP * (limits - keep_ratio))
    merged = jnp.zeros_like(task_total)
    for task_value in task_values:
        merged = merged + jnp.where(task_value > 0, upward, downward) * task_value
    return merged

def reference(activations, bucket_ids, thresholds, head_cot, w_reduce, w_spatial, w_expand, gain_mid, shift_mid, gain_out, shift_out, w_heads):
    positions = jnp.arange(FRAME * FRAME, dtype=jnp.int32)
    valid_all = frame_mask(bucket_ids, positions)
    weights = (w_reduce.astype(jnp.float32), w_spatial.astype(jnp.float32), w_expand.astype(jnp.float32), gain_mid, shift_mid, gain_out, shift_out)
    heads_table = w_heads.astype(jnp.float32)
    lane_task = jnp.arange(HEADS_ALL, dtype=jnp.int32) // HEAD
    grad_sums = None
    heads_grad = jnp.zeros((HEADS_ALL, D), jnp.float32)
    outs_y = []
    outs_dx = []
    for micro_index in range(MICRO):
        valid_rows = valid_all[micro_index].reshape(-1)
        start_rows = activations[micro_index].reshape(-1, D).astype(jnp.float32)

        def trunk_micro(carried, w_in, w_mid, w_out, scale_mid, offset_mid, scale_out, offset_out):
            return trunk_net(carried, valid_rows, w_in, w_mid, w_out, scale_mid, offset_mid, scale_out, offset_out)
        result, pull_back = jax.vjp(trunk_micro, start_rows, *weights)
        outs_y.append(result.astype(jnp.bfloat16).reshape(IMAGES, POSITIONS, D))
        cot_rows = head_cot[micro_index].reshape(-1, HEADS_ALL).astype(jnp.float32)
        unused_out, head_pull = jax.vjp(head_maps, result, heads_table)
        task_values = []
        for task_index in range(TASKS):
            task_cot = cot_rows * (lane_task == task_index).astype(jnp.float32)[None, :]
            task_value, table_grad = head_pull(task_cot)
            task_values.append(task_value)
            heads_grad = heads_grad + table_grad
        limits = thresholds[micro_index].reshape(-1, D).astype(jnp.float32)
        merged = grad_drop(task_values, limits)
        grads = pull_back(merged)
        outs_dx.append(grads[0].astype(jnp.bfloat16).reshape(IMAGES, POSITIONS, D))
        if grad_sums is None:
            grad_sums = grads[1:]
        else:
            grad_sums = tuple((left_item + right_item for left_item, right_item in zip(grad_sums, grads[1:])))
    return (jnp.stack(outs_y), jnp.stack(outs_dx), grad_sums[0], grad_sums[1], grad_sums[2], grad_sums[3], grad_sums[4], grad_sums[5], grad_sums[6], heads_grad)
```

```python
import functools

import jax
import jax.numpy as jnp
from jax import lax
from jax.experimental import pallas as pl
from jax.experimental.pallas import tpu as pltpu
from jax.sharding import PartitionSpec as P

HEAD = 256
TASKS = 3
FRAME = 8


EPS = 1e-05
SHARP = 8.0
FLOOR = 0.25
ROW_TABLE = (8, 8, 7, 6, 8, 5, 7, 8)
COL_TABLE = (8, 7, 8, 8, 6, 8, 7, 5)


def silu_slope(values):
    gate_val = jax.nn.sigmoid(values)
    return gate_val * (1.0 + values * (1.0 - gate_val))


def frame_mask(buckets, positions):
    bucket_kinds = jnp.arange(len(ROW_TABLE), dtype=jnp.int32)
    onehot = (buckets[..., None] == bucket_kinds).astype(jnp.int32)
    heights = jnp.sum(onehot * jnp.array(ROW_TABLE, dtype=jnp.int32), -1)
    widths = jnp.sum(onehot * jnp.array(COL_TABLE, dtype=jnp.int32), -1)
    rowpos = positions // FRAME
    colpos = positions % FRAME
    inside = (rowpos < heights[..., None]) & (colpos < widths[..., None])
    return inside.astype(jnp.float32)


def unfold_taps(images):
    padded = jnp.pad(images, ((0, 0), (1, 1), (1, 1), (0, 0)))
    pieces = [
        padded[:, row_off : row_off + FRAME, col_off : col_off + FRAME, :]
        for row_off in range(3)
        for col_off in range(3)
    ]
    return jnp.concatenate(pieces, -1)


def fold_taps(columns, channels):
    total_sum = jnp.zeros(columns.shape[:-1] + (channels,), columns.dtype)
    for tap_index in range(9):
        row_off, col_off = divmod(tap_index, 3)
        tap_part = columns[..., tap_index * channels : (tap_index + 1) * channels]
        padded = jnp.pad(tap_part, ((0, 0), (1, 1), (1, 1), (0, 0)))
        total_sum = (
            total_sum
            + padded[:, 2 - row_off : 2 - row_off + FRAME, 2 - col_off : 2 - col_off + FRAME, :]
        )
    return total_sum


def sum_kernel(wide, batch, x_ref, o_ref, near, far, part, near_send, near_recv, far_send, far_recv):
    my_w = lax.axis_index("wide")
    my_b = lax.axis_index("batch")
    barrier = pltpu.get_barrier_semaphore()
    for step in range(1, wide):
        pl.semaphore_signal(
            barrier, inc=1, device_id=(my_b, lax.rem(my_w + step, wide)), device_id_type=pl.DeviceIdType.MESH
        )
    for step in range(1, batch):
        pl.semaphore_signal(
            barrier, inc=1, device_id=(lax.rem(my_b + step, batch), my_w), device_id_type=pl.DeviceIdType.MESH
        )
    pl.semaphore_wait(barrier, wide + batch - 2)

    def exchange(src, slots, send, recv, count, me, target):
        copies = []
        for step in range(1, count):
            copy = pltpu.make_async_remote_copy(
                src_ref=src,
                dst_ref=slots.at[me],
                send_sem=send.at[step],
                recv_sem=recv.at[step],
                device_id=target(lax.rem(me + step, count)),
                device_id_type=pl.DeviceIdType.MESH,
            )
            copy.start()
            copies.append(copy)
        slots[me] = src[...]
        for copy in copies:
            copy.wait()
        total = slots[0]
        for index in range(1, count):
            total = total + slots[index]
        return total

    part[...] = exchange(x_ref, near, near_send, near_recv, wide, my_w, lambda w: (my_b, w))
    o_ref[...] = exchange(part, far, far_send, far_recv, batch, my_b, lambda b: (b, my_w))


def sum_all(values):
    wide, batch = lax.axis_size("wide"), lax.axis_size("batch")
    block = values.shape
    return pl.pallas_call(
        functools.partial(sum_kernel, wide, batch),
        out_shape=jax.ShapeDtypeStruct(block, jnp.float32),
        in_specs=[pl.BlockSpec(memory_space=pltpu.VMEM)],
        out_specs=pl.BlockSpec(memory_space=pltpu.VMEM),
        scratch_shapes=[
            pltpu.VMEM((wide,) + block, jnp.float32),
            pltpu.VMEM((batch,) + block, jnp.float32),
            pltpu.VMEM(block, jnp.float32),
            pltpu.SemaphoreType.DMA((wide,)),
            pltpu.SemaphoreType.DMA((wide,)),
            pltpu.SemaphoreType.DMA((batch,)),
            pltpu.SemaphoreType.DMA((batch,)),
        ],
        compiler_params=pltpu.CompilerParams(collective_id=block[-1] // 512, has_side_effects=True),
    )(values)


def batch_norm(values, valid_rows, scale_vec, offset_vec):
    weighted = values * valid_rows[..., None]
    sum_first = jnp.sum(weighted, 1)
    sum_second = jnp.sum(weighted * values, 1)
    counts = jnp.sum(valid_rows, 1)
    count_row = jnp.broadcast_to(counts[:, None], sum_first.shape)
    summed = sum_all(jnp.concatenate([sum_first, sum_second, count_row, jnp.zeros_like(sum_first)], 0))
    sum_first, sum_second, counts = summed[0:2], summed[2:4], summed[4:6, 0]
    mean_val = sum_first / counts[:, None]
    spread = sum_second / counts[:, None] - mean_val * mean_val
    inv_std = lax.rsqrt(spread + EPS)
    normed = (values - mean_val[:, None, :]) * inv_std[:, None, :]
    return (normed, scale_vec * normed + offset_vec, inv_std, counts)


def norm_back(grad_out, normed, inv_std, counts, valid_rows, scale_vec):
    sum_grad = jnp.sum(grad_out, 1)
    sum_prod = jnp.sum(grad_out * normed, 1)
    summed = sum_all(jnp.concatenate([sum_grad, sum_prod, sum_grad, sum_prod], 0))
    sum_grad, sum_prod = summed[0:2], summed[2:4]
    centered = (
        grad_out - (sum_grad[:, None, :] + normed * sum_prod[:, None, :]) / counts[:, None, None]
    )
    grad_in = valid_rows[..., None] * scale_vec * inv_std[:, None, :] * centered
    return (grad_in, jnp.sum(sum_prod, 0), jnp.sum(sum_grad, 0))


def forward_layer(layer_in, pix_valid, img_valid, params, layout):
    w_in, w_mid, w_out, scale_a, offset_a, scale_b, offset_b, scale_c, offset_c = params
    groups, per_lane, local_imgs = layout
    span_len = layer_in.shape[0]
    channels = w_in.shape[1]
    entry_low = layer_in.astype(jnp.bfloat16)
    reduced = jnp.einsum("mrd,dc->mrc", entry_low, w_in, preferred_element_type=jnp.float32)
    normed_a, bn_a, inv_a, counts = batch_norm(reduced, pix_valid, scale_a, offset_a)
    act_a = (jax.nn.silu(bn_a) * pix_valid[..., None]).astype(jnp.bfloat16)
    arrived = lax.all_to_all(
        act_a.reshape(span_len, groups, per_lane, channels),
        "wide",
        split_axis=1,
        concat_axis=2,
        tiled=True,
    )
    count_imgs = arrived.shape[1]
    images = arrived.reshape(span_len * count_imgs, FRAME, FRAME, channels)
    columns = unfold_taps(images).reshape(span_len, count_imgs, FRAME * FRAME, 9 * channels)
    conv_out = jnp.einsum("mkpc,co->mkpo", columns, w_mid, preferred_element_type=jnp.float32)
    taps_saved, conv_out = (columns, conv_out)
    taps_saved = taps_saved.reshape(span_len, -1, taps_saved.shape[-1])
    conv_out = conv_out.reshape(span_len, -1, channels)
    normed_b, bn_b, inv_b, unused_counts = batch_norm(conv_out, img_valid, scale_b, offset_b)
    act_b = (jax.nn.silu(bn_b) * img_valid[..., None]).astype(jnp.bfloat16)
    returned = lax.all_to_all(
        act_b.reshape(span_len, local_imgs, FRAME * FRAME, channels),
        "wide",
        split_axis=2,
        concat_axis=1,
        tiled=True,
    ).reshape(span_len, -1, channels)
    expanded = jnp.einsum("mrc,oc->mro", returned, w_out, preferred_element_type=jnp.float32)
    normed_c, bn_c, inv_c, unused_again = batch_norm(expanded, pix_valid, scale_c, offset_c)
    before = bn_c + layer_in
    result = jax.nn.silu(before) * pix_valid[..., None]
    saved = (
        entry_low,
        normed_a,
        bn_a,
        inv_a,
        taps_saved,
        normed_b,
        bn_b,
        inv_b,
        returned,
        normed_c,
        before,
        inv_c,
        counts,
    )
    return (result, saved)


def backward_layer(incoming, saved, pix_valid, img_valid, params, layout):
    w_in, w_mid, w_out, scale_a, offset_a, scale_b, offset_b, scale_c, offset_c = params
    groups, per_lane, local_imgs = layout
    (
        entry_low,
        normed_a,
        bn_a,
        inv_a,
        taps_saved,
        normed_b,
        bn_b,
        inv_b,
        returned,
        normed_c,
        before,
        inv_c,
        counts,
    ) = saved
    span_len = incoming.shape[0]
    channels = w_in.shape[1]
    grad_pre = incoming * pix_valid[..., None] * silu_slope(before)
    grad_c, scale_gc, offset_gc = norm_back(grad_pre, normed_c, inv_c, counts, pix_valid, scale_c)
    grad_c_low = grad_c.astype(jnp.bfloat16)
    g_out = jnp.einsum("mro,mrc->oc", grad_c_low, returned, preferred_element_type=jnp.float32)
    d_returned = jnp.einsum(
        "mro,oc->mrc", grad_c_low, w_out, preferred_element_type=jnp.float32
    ).astype(jnp.bfloat16)
    d_images = lax.all_to_all(
        d_returned.reshape(span_len, groups, per_lane, channels),
        "wide",
        split_axis=1,
        concat_axis=2,
        tiled=True,
    ).reshape(span_len, -1, channels)
    d_bn_b = d_images.astype(jnp.float32) * img_valid[..., None] * silu_slope(bn_b)
    grad_b, scale_gb, offset_gb = norm_back(d_bn_b, normed_b, inv_b, counts, img_valid, scale_b)
    grad_b_low = grad_b.astype(jnp.bfloat16)
    g_mid = jnp.einsum("mrk,mro->ko", taps_saved, grad_b_low, preferred_element_type=jnp.float32)
    d_columns = jnp.einsum("mro,ko->mrk", grad_b_low, w_mid, preferred_element_type=jnp.float32)
    d_act = fold_taps(
        d_columns.reshape(span_len * local_imgs, FRAME, FRAME, 9 * channels), channels
    )
    d_act = d_act.astype(jnp.bfloat16).reshape(span_len, local_imgs, FRAME * FRAME, channels)
    d_pixels = lax.all_to_all(d_act, "wide", split_axis=2, concat_axis=1, tiled=True).reshape(
        span_len, -1, channels
    )
    d_bn_a = d_pixels.astype(jnp.float32) * pix_valid[..., None] * silu_slope(bn_a)
    grad_a, scale_ga, offset_ga = norm_back(d_bn_a, normed_a, inv_a, counts, pix_valid, scale_a)
    grad_a_low = grad_a.astype(jnp.bfloat16)
    g_in = jnp.einsum("mrd,mrc->dc", entry_low, grad_a_low, preferred_element_type=jnp.float32)
    d_entry = jnp.einsum("mrc,dc->mrd", grad_a_low, w_in, preferred_element_type=jnp.float32)
    return (
        d_entry + grad_pre,
        (g_in, g_mid, g_out),
        (scale_ga, offset_ga, scale_gb, offset_gb, scale_gc, offset_gc),
    )


def grad_drop(task_values, limits):
    task_total = task_values[0]
    magnitude = jnp.abs(task_values[0])
    for task_index in range(1, len(task_values)):
        task_total = task_total + task_values[task_index]
        magnitude = magnitude + jnp.abs(task_values[task_index])
    keep_ratio = 0.5 * (1.0 + task_total / jnp.maximum(magnitude, FLOOR))
    upward = jax.nn.sigmoid(SHARP * (keep_ratio - limits))
    downward = jax.nn.sigmoid(SHARP * (limits - keep_ratio))
    merged = jnp.zeros_like(task_total)
    for task_value in task_values:
        merged = merged + jnp.where(task_value > 0, upward, downward) * task_value
    return merged


def add_tuples(left, right):
    return tuple((left_item + right_item for left_item, right_item in zip(left, right)))


def shards(
    activations,
    bucket_ids,
    thresholds,
    head_cot,
    w_reduce,
    w_spatial,
    w_expand,
    gain_mid,
    shift_mid,
    gain_out,
    shift_out,
    w_heads,
):
    micro_total, groups, per_lane, features = activations.shape
    lane_count = lax.axis_size("wide")
    local_imgs = groups // lane_count
    lane_index = lax.axis_index("wide")
    layout = (groups, per_lane, local_imgs)
    pix_positions = lane_index * per_lane + jnp.arange(per_lane, dtype=jnp.int32)
    pix_valid_all = frame_mask(bucket_ids, pix_positions).reshape(micro_total, -1)
    own_ids = lax.dynamic_slice_in_dim(bucket_ids, lane_index * local_imgs, local_imgs, 1)
    img_valid_all = frame_mask(own_ids, jnp.arange(FRAME * FRAME, dtype=jnp.int32)).reshape(
        micro_total, -1
    )
    layer_total = w_reduce.shape[0]
    head_width = head_cot.shape[-1]
    layer_params = [
        (
            w_reduce[layer_index],
            w_spatial[layer_index],
            w_expand[layer_index],
            gain_mid[layer_index, 0],
            shift_mid[layer_index, 0],
            gain_mid[layer_index, 1],
            shift_mid[layer_index, 1],
            gain_out[layer_index],
            shift_out[layer_index],
        )
        for layer_index in range(layer_total)
    ]
    spans = [(0, micro_total)]
    weight_acc = [None] * layer_total
    norm_acc = [None] * layer_total
    heads_acc = jnp.zeros((features, head_width), jnp.float32)
    outs_y = []
    outs_dx = []
    for span_at, span_len in spans:

        def take_span(array):
            return lax.slice_in_dim(array, span_at, span_at + span_len, axis=0)

        pix_valid = take_span(pix_valid_all)
        img_valid = take_span(img_valid_all)
        carried = take_span(activations).reshape(span_len, -1, features).astype(jnp.float32)
        saved_layers = []
        for layer_index in range(layer_total):
            carried, saved = forward_layer(
                carried, pix_valid, img_valid, layer_params[layer_index], layout
            )
            saved_layers.append(saved)
        result_low = carried.astype(jnp.bfloat16)
        outs_y.append(result_low.reshape(span_len, groups, per_lane, features))
        head_grads = take_span(head_cot).reshape(span_len, -1, head_width)
        heads_acc = heads_acc + jnp.einsum(
            "mrd,mrh->dh", result_low, head_grads, preferred_element_type=jnp.float32
        )
        task_values = [
            jnp.einsum(
                "mrh,hd->mrd",
                head_grads[..., task_index * HEAD : (task_index + 1) * HEAD],
                w_heads[task_index * HEAD : (task_index + 1) * HEAD],
                preferred_element_type=jnp.float32,
            )
            for task_index in range(TASKS)
        ]
        limits = take_span(thresholds).reshape(span_len, -1, features).astype(jnp.float32)
        incoming = grad_drop(task_values, limits)
        for layer_index in reversed(range(layer_total)):
            incoming, weight_parts, norm_parts = backward_layer(
                incoming,
                saved_layers[layer_index],
                pix_valid,
                img_valid,
                layer_params[layer_index],
                layout,
            )
            if weight_acc[layer_index] is None:
                weight_acc[layer_index] = weight_parts
                norm_acc[layer_index] = norm_parts
            else:
                weight_acc[layer_index] = add_tuples(weight_acc[layer_index], weight_parts)
                norm_acc[layer_index] = add_tuples(norm_acc[layer_index], norm_parts)
        outs_dx.append(incoming.astype(jnp.bfloat16).reshape(span_len, groups, per_lane, features))
    stack_in = jnp.stack([layer_acc[0] for layer_acc in weight_acc])
    stack_mid = jnp.stack([layer_acc[1] for layer_acc in weight_acc])
    stack_out = jnp.stack([layer_acc[2] for layer_acc in weight_acc])
    shard_in, shard_mid, shard_out, shard_heads = (
        lax.psum_scatter(
            stack_in.astype(jnp.bfloat16), "wide", scatter_dimension=1, tiled=True
        ).astype(jnp.float32),
        lax.psum_scatter(
            stack_mid.astype(jnp.bfloat16), "wide", scatter_dimension=1, tiled=True
        ).astype(jnp.float32),
        lax.psum_scatter(
            stack_out.astype(jnp.bfloat16), "wide", scatter_dimension=1, tiled=True
        ).astype(jnp.float32),
        lax.psum_scatter(
            heads_acc[None].astype(jnp.bfloat16), "wide", scatter_dimension=1, tiled=True
        ).astype(jnp.float32),
    )
    shard_in, shard_mid, shard_out, shard_heads = (
        lax.psum(shard_in.astype(jnp.bfloat16), "batch").astype(jnp.float32),
        lax.psum(shard_mid.astype(jnp.bfloat16), "batch").astype(jnp.float32),
        lax.psum(shard_out.astype(jnp.bfloat16), "batch").astype(jnp.float32),
        lax.psum(shard_heads.astype(jnp.bfloat16), "batch").astype(jnp.float32),
    )
    g_gain_mid = jnp.stack([jnp.stack([layer_norm[0], layer_norm[2]]) for layer_norm in norm_acc])
    g_shift_mid = jnp.stack([jnp.stack([layer_norm[1], layer_norm[3]]) for layer_norm in norm_acc])
    g_gain_out = jnp.stack([layer_norm[4] for layer_norm in norm_acc])
    g_shift_out = jnp.stack([layer_norm[5] for layer_norm in norm_acc])
    return (
        jnp.concatenate(outs_y, 0),
        jnp.concatenate(outs_dx, 0),
        shard_in,
        shard_mid,
        shard_out,
        g_gain_mid,
        g_shift_mid,
        g_gain_out,
        g_shift_out,
        shard_heads[0].T,
    )


def solution(mesh):
    placed = (
        P(None, "batch", "wide", None),
        P(None, "batch"),
        P(None, "batch", "wide", None),
        P(None, "batch", "wide", None),
        P(),
        P(),
        P(),
        P(),
        P(),
        P(),
        P(),
        P(),
    )
    return jax.shard_map(
        shards,
        mesh=mesh,
        in_specs=placed,
        out_specs=(
            P(None, "batch", "wide", None),
            P(None, "batch", "wide", None),
            P(None, "wide", None),
            P(None, "wide", None),
            P(None, "wide", None),
            P(),
            P(),
            P(),
            P(),
            P(None, "wide"),
        ),
        check_vma=False,
    )
```

```python
import functools

import jax
import jax.numpy as jnp
from jax import lax
from jax.experimental import pallas as pl
from jax.experimental.pallas import tpu as pltpu
from jax.sharding import PartitionSpec as P

HEAD = 256
TASKS = 3
FRAME = 8


EPS = 1e-05
SHARP = 8.0
FLOOR = 0.25
ROW_TABLE = (8, 8, 7, 6, 8, 5, 7, 8)
COL_TABLE = (8, 7, 8, 8, 6, 8, 7, 5)


def silu_slope(values):
    gate_val = jax.nn.sigmoid(values)
    return gate_val * (1.0 + values * (1.0 - gate_val))


def frame_mask(buckets, positions):
    bucket_kinds = jnp.arange(len(ROW_TABLE), dtype=jnp.int32)
    onehot = (buckets[..., None] == bucket_kinds).astype(jnp.int32)
    heights = jnp.sum(onehot * jnp.array(ROW_TABLE, dtype=jnp.int32), -1)
    widths = jnp.sum(onehot * jnp.array(COL_TABLE, dtype=jnp.int32), -1)
    rowpos = positions // FRAME
    colpos = positions % FRAME
    inside = (rowpos < heights[..., None]) & (colpos < widths[..., None])
    return inside.astype(jnp.float32)


def unfold_taps(images):
    padded = jnp.pad(images, ((0, 0), (1, 1), (1, 1), (0, 0)))
    pieces = [
        padded[:, row_off : row_off + FRAME, col_off : col_off + FRAME, :]
        for row_off in range(3)
        for col_off in range(3)
    ]
    return jnp.concatenate(pieces, -1)


def fold_taps(columns, channels):
    total_sum = jnp.zeros(columns.shape[:-1] + (channels,), columns.dtype)
    for tap_index in range(9):
        row_off, col_off = divmod(tap_index, 3)
        tap_part = columns[..., tap_index * channels : (tap_index + 1) * channels]
        padded = jnp.pad(tap_part, ((0, 0), (1, 1), (1, 1), (0, 0)))
        total_sum = (
            total_sum
            + padded[:, 2 - row_off : 2 - row_off + FRAME, 2 - col_off : 2 - col_off + FRAME, :]
        )
    return total_sum


def sum_kernel(wide, batch, x_ref, o_ref, near, far, part, near_send, near_recv, far_send, far_recv):
    my_w = lax.axis_index("wide")
    my_b = lax.axis_index("batch")
    barrier = pltpu.get_barrier_semaphore()
    for step in range(1, wide):
        pl.semaphore_signal(
            barrier, inc=1, device_id=(my_b, lax.rem(my_w + step, wide)), device_id_type=pl.DeviceIdType.MESH
        )
    for step in range(1, batch):
        pl.semaphore_signal(
            barrier, inc=1, device_id=(lax.rem(my_b + step, batch), my_w), device_id_type=pl.DeviceIdType.MESH
        )
    pl.semaphore_wait(barrier, wide + batch - 2)

    def exchange(src, slots, send, recv, count, me, target):
        copies = []
        for step in range(1, count):
            copy = pltpu.make_async_remote_copy(
                src_ref=src,
                dst_ref=slots.at[me],
                send_sem=send.at[step],
                recv_sem=recv.at[step],
                device_id=target(lax.rem(me + step, count)),
                device_id_type=pl.DeviceIdType.MESH,
            )
            copy.start()
            copies.append(copy)
        slots[me] = src[...]
        for copy in copies:
            copy.wait()
        total = slots[0]
        for index in range(1, count):
            total = total + slots[index]
        return total

    part[...] = exchange(x_ref, near, near_send, near_recv, wide, my_w, lambda w: (my_b, w))
    o_ref[...] = exchange(part, far, far_send, far_recv, batch, my_b, lambda b: (b, my_w))


def sum_all(values):
    wide, batch = lax.axis_size("wide"), lax.axis_size("batch")
    block = values.shape
    return pl.pallas_call(
        functools.partial(sum_kernel, wide, batch),
        out_shape=jax.ShapeDtypeStruct(block, jnp.float32),
        in_specs=[pl.BlockSpec(memory_space=pltpu.VMEM)],
        out_specs=pl.BlockSpec(memory_space=pltpu.VMEM),
        scratch_shapes=[
            pltpu.VMEM((wide,) + block, jnp.float32),
            pltpu.VMEM((batch,) + block, jnp.float32),
            pltpu.VMEM(block, jnp.float32),
            pltpu.SemaphoreType.DMA((wide,)),
            pltpu.SemaphoreType.DMA((wide,)),
            pltpu.SemaphoreType.DMA((batch,)),
            pltpu.SemaphoreType.DMA((batch,)),
        ],
        compiler_params=pltpu.CompilerParams(collective_id=block[-1] // 512, has_side_effects=True),
    )(values)


def batch_norm(values, valid_rows, scale_vec, offset_vec):
    weighted = values * valid_rows[..., None]
    sum_first = jnp.sum(weighted, 1)
    sum_second = jnp.sum(weighted * values, 1)
    counts = jnp.sum(valid_rows, 1)
    count_row = jnp.broadcast_to(counts[:, None], sum_first.shape)
    summed = sum_all(jnp.concatenate([sum_first, sum_second, count_row, jnp.zeros_like(sum_first)], 0))
    sum_first, sum_second, counts = summed[0:2], summed[2:4], summed[4:6, 0]
    mean_val = sum_first / counts[:, None]
    spread = sum_second / counts[:, None] - mean_val * mean_val
    inv_std = lax.rsqrt(spread + EPS)
    normed = (values - mean_val[:, None, :]) * inv_std[:, None, :]
    return (normed, scale_vec * normed + offset_vec, inv_std, counts)


def norm_back(grad_out, normed, inv_std, counts, valid_rows, scale_vec):
    sum_grad = jnp.sum(grad_out, 1)
    sum_prod = jnp.sum(grad_out * normed, 1)
    summed = sum_all(jnp.concatenate([sum_grad, sum_prod, sum_grad, sum_prod], 0))
    sum_grad, sum_prod = summed[0:2], summed[2:4]
    centered = (
        grad_out - (sum_grad[:, None, :] + normed * sum_prod[:, None, :]) / counts[:, None, None]
    )
    grad_in = valid_rows[..., None] * scale_vec * inv_std[:, None, :] * centered
    return (grad_in, jnp.sum(sum_prod, 0), jnp.sum(sum_grad, 0))


def forward_layer(layer_in, pix_valid, img_valid, params, layout):
    w_in, w_mid, w_out, scale_a, offset_a, scale_b, offset_b, scale_c, offset_c = params
    groups, per_lane, local_imgs = layout
    span_len = layer_in.shape[0]
    channels = w_in.shape[1]
    entry_low = layer_in.astype(jnp.bfloat16)
    reduced = jnp.einsum("mrd,dc->mrc", entry_low, w_in, preferred_element_type=jnp.float32)
    normed_a, bn_a, inv_a, counts = batch_norm(reduced, pix_valid, scale_a, offset_a)
    act_a = (jax.nn.silu(bn_a) * pix_valid[..., None]).astype(jnp.bfloat16)
    arrived = lax.all_to_all(
        act_a.reshape(span_len, groups, per_lane, channels),
        "wide",
        split_axis=1,
        concat_axis=2,
        tiled=True,
    )
    count_imgs = arrived.shape[1]
    images = arrived.reshape(span_len * count_imgs, FRAME, FRAME, channels)
    columns = unfold_taps(images).reshape(span_len, count_imgs, FRAME * FRAME, 9 * channels)
    conv_out = jnp.einsum("mkpc,co->mkpo", columns, w_mid, preferred_element_type=jnp.float32)
    taps_saved, conv_out = (columns, conv_out)
    taps_saved = taps_saved.reshape(span_len, -1, taps_saved.shape[-1])
    conv_out = conv_out.reshape(span_len, -1, channels)
    normed_b, bn_b, inv_b, unused_counts = batch_norm(conv_out, img_valid, scale_b, offset_b)
    act_b = (jax.nn.silu(bn_b) * img_valid[..., None]).astype(jnp.bfloat16)
    returned = lax.all_to_all(
        act_b.reshape(span_len, local_imgs, FRAME * FRAME, channels),
        "wide",
        split_axis=2,
        concat_axis=1,
        tiled=True,
    ).reshape(span_len, -1, channels)
    expanded = jnp.einsum("mrc,oc->mro", returned, w_out, preferred_element_type=jnp.float32)
    normed_c, bn_c, inv_c, unused_again = batch_norm(expanded, pix_valid, scale_c, offset_c)
    before = bn_c + layer_in
    result = jax.nn.silu(before) * pix_valid[..., None]
    saved = (
        entry_low,
        normed_a,
        bn_a,
        inv_a,
        taps_saved,
        normed_b,
        bn_b,
        inv_b,
        returned,
        normed_c,
        before,
        inv_c,
        counts,
    )
    return (result, saved)


def backward_layer(incoming, saved, pix_valid, img_valid, params, layout):
    w_in, w_mid, w_out, scale_a, offset_a, scale_b, offset_b, scale_c, offset_c = params
    groups, per_lane, local_imgs = layout
    (
        entry_low,
        normed_a,
        bn_a,
        inv_a,
        taps_saved,
        normed_b,
        bn_b,
        inv_b,
        returned,
        normed_c,
        before,
        inv_c,
        counts,
    ) = saved
    span_len = incoming.shape[0]
    channels = w_in.shape[1]
    grad_pre = incoming * pix_valid[..., None] * silu_slope(before)
    grad_c, scale_gc, offset_gc = norm_back(grad_pre, normed_c, inv_c, counts, pix_valid, scale_c)
    grad_c_low = grad_c.astype(jnp.bfloat16)
    g_out = jnp.einsum("mro,mrc->oc", grad_c_low, returned, preferred_element_type=jnp.float32)
    d_returned = jnp.einsum(
        "mro,oc->mrc", grad_c_low, w_out, preferred_element_type=jnp.float32
    ).astype(jnp.bfloat16)
    d_images = lax.all_to_all(
        d_returned.reshape(span_len, groups, per_lane, channels),
        "wide",
        split_axis=1,
        concat_axis=2,
        tiled=True,
    ).reshape(span_len, -1, channels)
    d_bn_b = d_images.astype(jnp.float32) * img_valid[..., None] * silu_slope(bn_b)
    grad_b, scale_gb, offset_gb = norm_back(d_bn_b, normed_b, inv_b, counts, img_valid, scale_b)
    grad_b_low = grad_b.astype(jnp.bfloat16)
    g_mid = jnp.einsum("mrk,mro->ko", taps_saved, grad_b_low, preferred_element_type=jnp.float32)
    d_columns = jnp.einsum("mro,ko->mrk", grad_b_low, w_mid, preferred_element_type=jnp.float32)
    d_act = fold_taps(
        d_columns.reshape(span_len * local_imgs, FRAME, FRAME, 9 * channels), channels
    )
    d_act = d_act.astype(jnp.bfloat16).reshape(span_len, local_imgs, FRAME * FRAME, channels)
    d_pixels = lax.all_to_all(d_act, "wide", split_axis=2, concat_axis=1, tiled=True).reshape(
        span_len, -1, channels
    )
    d_bn_a = d_pixels.astype(jnp.float32) * pix_valid[..., None] * silu_slope(bn_a)
    grad_a, scale_ga, offset_ga = norm_back(d_bn_a, normed_a, inv_a, counts, pix_valid, scale_a)
    grad_a_low = grad_a.astype(jnp.bfloat16)
    g_in = jnp.einsum("mrd,mrc->dc", entry_low, grad_a_low, preferred_element_type=jnp.float32)
    d_entry = jnp.einsum("mrc,dc->mrd", grad_a_low, w_in, preferred_element_type=jnp.float32)
    return (
        d_entry + grad_pre,
        (g_in, g_mid, g_out),
        (scale_ga, offset_ga, scale_gb, offset_gb, scale_gc, offset_gc),
    )


def grad_drop(task_values, limits):
    task_total = task_values[0]
    magnitude = jnp.abs(task_values[0])
    for task_index in range(1, len(task_values)):
        task_total = task_total + task_values[task_index]
        magnitude = magnitude + jnp.abs(task_values[task_index])
    keep_ratio = 0.5 * (1.0 + task_total / jnp.maximum(magnitude, FLOOR))
    upward = jax.nn.sigmoid(SHARP * (keep_ratio - limits))
    downward = jax.nn.sigmoid(SHARP * (limits - keep_ratio))
    merged = jnp.zeros_like(task_total)
    for task_value in task_values:
        merged = merged + jnp.where(task_value > 0, upward, downward) * task_value
    return merged


def add_tuples(left, right):
    return tuple((left_item + right_item for left_item, right_item in zip(left, right)))


def shards(
    activations,
    bucket_ids,
    thresholds,
    head_cot,
    w_reduce,
    w_spatial,
    w_expand,
    gain_mid,
    shift_mid,
    gain_out,
    shift_out,
    w_heads,
):
    micro_total, groups, per_lane, features = activations.shape
    lane_count = lax.axis_size("wide")
    local_imgs = groups // lane_count
    lane_index = lax.axis_index("wide")
    layout = (groups, per_lane, local_imgs)
    pix_positions = lane_index * per_lane + jnp.arange(per_lane, dtype=jnp.int32)
    pix_valid_all = frame_mask(bucket_ids, pix_positions).reshape(micro_total, -1)
    own_ids = lax.dynamic_slice_in_dim(bucket_ids, lane_index * local_imgs, local_imgs, 1)
    img_valid_all = frame_mask(own_ids, jnp.arange(FRAME * FRAME, dtype=jnp.int32)).reshape(
        micro_total, -1
    )
    layer_total = w_reduce.shape[0]
    head_width = head_cot.shape[-1]
    layer_params = [
        (
            w_reduce[layer_index],
            w_spatial[layer_index],
            w_expand[layer_index],
            gain_mid[layer_index, 0],
            shift_mid[layer_index, 0],
            gain_mid[layer_index, 1],
            shift_mid[layer_index, 1],
            gain_out[layer_index],
            shift_out[layer_index],
        )
        for layer_index in range(layer_total)
    ]
    spans = [(0, micro_total)]
    weight_acc = [None] * layer_total
    norm_acc = [None] * layer_total
    heads_acc = jnp.zeros((features, head_width), jnp.float32)
    outs_y = []
    outs_dx = []
    for span_at, span_len in spans:

        def take_span(array):
            return lax.slice_in_dim(array, span_at, span_at + span_len, axis=0)

        pix_valid = take_span(pix_valid_all)
        img_valid = take_span(img_valid_all)
        carried = take_span(activations).reshape(span_len, -1, features).astype(jnp.float32)
        saved_layers = []
        for layer_index in range(layer_total):
            carried, saved = forward_layer(
                carried, pix_valid, img_valid, layer_params[layer_index], layout
            )
            saved_layers.append(saved)
        result_low = carried.astype(jnp.bfloat16)
        outs_y.append(result_low.reshape(span_len, groups, per_lane, features))
        head_grads = take_span(head_cot).reshape(span_len, -1, head_width)
        heads_acc = heads_acc + jnp.einsum(
            "mrd,mrh->dh", result_low, head_grads, preferred_element_type=jnp.float32
        )
        task_values = [
            jnp.einsum(
                "mrh,hd->mrd",
                head_grads[..., task_index * HEAD : (task_index + 1) * HEAD],
                w_heads[task_index * HEAD : (task_index + 1) * HEAD],
                preferred_element_type=jnp.float32,
            )
            for task_index in range(TASKS)
        ]
        limits = take_span(thresholds).reshape(span_len, -1, features).astype(jnp.float32)
        incoming = grad_drop(task_values, limits)
        for layer_index in reversed(range(layer_total)):
            incoming, weight_parts, norm_parts = backward_layer(
                incoming,
                saved_layers[layer_index],
                pix_valid,
                img_valid,
                layer_params[layer_index],
                layout,
            )
            if weight_acc[layer_index] is None:
                weight_acc[layer_index] = weight_parts
                norm_acc[layer_index] = norm_parts
            else:
                weight_acc[layer_index] = add_tuples(weight_acc[layer_index], weight_parts)
                norm_acc[layer_index] = add_tuples(norm_acc[layer_index], norm_parts)
        outs_dx.append(incoming.astype(jnp.bfloat16).reshape(span_len, groups, per_lane, features))
    stack_in = jnp.stack([layer_acc[0] for layer_acc in weight_acc])
    stack_mid = jnp.stack([layer_acc[1] for layer_acc in weight_acc])
    stack_out = jnp.stack([layer_acc[2] for layer_acc in weight_acc])
    shard_in, shard_mid, shard_out, shard_heads = (
        lax.psum_scatter(
            stack_in.astype(jnp.bfloat16), "wide", scatter_dimension=1, tiled=True
        ).astype(jnp.float32),
        lax.psum_scatter(
            stack_mid.astype(jnp.bfloat16), "wide", scatter_dimension=1, tiled=True
        ).astype(jnp.float32),
        lax.psum_scatter(
            stack_out.astype(jnp.bfloat16), "wide", scatter_dimension=1, tiled=True
        ).astype(jnp.float32),
        lax.psum_scatter(
            heads_acc[None].astype(jnp.bfloat16), "wide", scatter_dimension=1, tiled=True
        ).astype(jnp.float32),
    )
    shard_in, shard_mid, shard_out, shard_heads = (
        lax.psum(shard_in.astype(jnp.bfloat16), "batch").astype(jnp.float32),
        lax.psum(shard_mid.astype(jnp.bfloat16), "batch").astype(jnp.float32),
        lax.psum(shard_out.astype(jnp.bfloat16), "batch").astype(jnp.float32),
        lax.psum(shard_heads.astype(jnp.bfloat16), "batch").astype(jnp.float32),
    )
    g_gain_mid = jnp.stack([jnp.stack([layer_norm[0], layer_norm[2]]) for layer_norm in norm_acc])
    g_shift_mid = jnp.stack([jnp.stack([layer_norm[1], layer_norm[3]]) for layer_norm in norm_acc])
    g_gain_out = jnp.stack([layer_norm[4] for layer_norm in norm_acc])
    g_shift_out = jnp.stack([layer_norm[5] for layer_norm in norm_acc])
    return (
        jnp.concatenate(outs_y, 0),
        jnp.concatenate(outs_dx, 0),
        shard_in,
        shard_mid,
        shard_out,
        g_gain_mid,
        g_shift_mid,
        g_gain_out,
        g_shift_out,
        shard_heads[0].T,
    )


MESH = pl.DeviceIdType.MESH
F32, BF16 = jnp.float32, jnp.bfloat16
NN = (((1,), (0,)), ((), ()))
NT = (((1,), (1,)), ((), ()))
TN = (((0,), (0,)), ((), ()))
CH = 16


def dot(left, right, dims=NN):
    return lax.dot_general(left, right, dims, preferred_element_type=F32)


def along(column, lanes):
    return column if lanes == 128 else jnp.concatenate([column] * (lanes // 128), axis=1)


def fold8(block):
    total = block[0:8]
    for at in range(8, block.shape[0], 8):
        total = total + block[at : at + 8]
    return total


def shifted(block, by):
    rows, lanes = block.shape
    grouped = block.reshape(rows // FRAME, FRAME, lanes)
    pixel = lax.broadcasted_iota(jnp.int32, grouped.shape, 1)
    moved = pltpu.roll(grouped, by % FRAME, 1)
    keep = pixel > 0 if by == 1 else pixel < FRAME - 1
    return jnp.where(keep, moved, 0.0).reshape(rows, lanes)


def loop(n, body, start=0):
    def step(i, c):
        body(i)
        return c

    lax.fori_loop(start, n, step, 0)


def block_kernel(
    dims,
    act_in, thr_in, cot_in, valid_ref, wr_in, ws_in, we_in, wh_in, gm_ref, sm_ref, go_ref, so_ref,
    y_out, dx_out, gr_out, gs_out, ge_out, gh_out, ggm_ref, gsm_ref, ggo_ref, gso_ref,
    wr, ws, we, wh, entry, carry, wide_f, thr, cot, cot_t, act, za, sla, actb, zb, slb, zc, slc,
    mid_f, taps_f, dexp, dcv, dcs, dred, gia, gib, gic, count, pay, part, near, far, stage,
    load_sem, near_send, near_recv, far_send, far_recv, halo_send, halo_recv, stage_sem, out_sem,
):
    wide, batch, rows, D, C = dims
    my_w = lax.axis_index("wide")
    my_b = lax.axis_index("batch")
    Q = D // 4

    def span(m):
        return pl.ds(pl.multiple_of(m * rows, rows), rows)

    def chunk(m, i):
        return pl.ds(pl.multiple_of(m * rows + i * CH, CH), CH)

    def load(src, dst, index):
        return pltpu.make_async_copy(src, dst, load_sem.at[index])

    def load_wr(l):
        return load(wr_in.at[l], wr, 0)

    def load_ws(l):
        return load(ws_in.at[l], ws, 1)

    def load_we(l):
        return load(we_in.at[l], we, 2)

    load_act = load(act_in, entry.at[0], 3)
    load_wh = load(wh_in, wh, 4)
    load_thr = load(thr_in, thr, 5)
    load_cot = load(cot_in, cot, 6)
    load_act.start()
    load_wr(0).start()
    load_ws(0).start()
    load_we(0).start()
    load_cot.start()
    load_wh.start()
    load_thr.start()

    for side in (0, 2):
        for l in range(2):
            act[l, side] = jnp.zeros(act.shape[2:], BF16)
        dcv[side] = jnp.zeros(dcv.shape[1:], BF16)

    barrier = pltpu.get_barrier_semaphore()
    for step in range(1, wide):
        pl.semaphore_signal(barrier, inc=1, device_id=(my_b, lax.rem(my_w + step, wide)), device_id_type=MESH)
    for step in range(1, batch):
        pl.semaphore_signal(barrier, inc=1, device_id=(lax.rem(my_b + step, batch), my_w), device_id_type=MESH)
    pl.semaphore_wait(barrier, wide + batch - 2)

    def near_copy(k, m, step, lanes):
        return pltpu.make_async_remote_copy(
            src_ref=pay.at[k, m, :, pl.ds(0, lanes)],
            dst_ref=near.at[k, m, my_w, :, pl.ds(0, lanes)],
            send_sem=near_send.at[k, m, step],
            recv_sem=near_recv.at[k, m, step],
            device_id=(my_b, lax.rem(my_w + step, wide)),
            device_id_type=MESH,
        )

    def far_copy(k, m, step, lanes):
        return pltpu.make_async_remote_copy(
            src_ref=part.at[k, m, :, pl.ds(0, lanes)],
            dst_ref=far.at[k, m, my_b, :, pl.ds(0, lanes)],
            send_sem=far_send.at[k, m, step],
            recv_sem=far_recv.at[k, m, step],
            device_id=(lax.rem(my_b + step, batch), my_w),
            device_id_type=MESH,
        )

    def sum_start(k, m, lanes):
        for step in range(1, wide):
            near_copy(k, m, step, lanes).start()
        near[k, m, my_w, :, 0:lanes] = pay[k, m, :, 0:lanes]

    def sum_middle(k, m, lanes):
        for step in range(1, wide):
            near_copy(k, m, step, lanes).wait()
        total = near[k, m, 0, :, 0:lanes]
        for index in range(1, wide):
            total = total + near[k, m, index, :, 0:lanes]
        part[k, m, :, 0:lanes] = total
        for step in range(1, batch):
            far_copy(k, m, step, lanes).start()
        far[k, m, my_b, :, 0:lanes] = total

    def sum_end(k, m, lanes):
        for step in range(1, batch):
            far_copy(k, m, step, lanes).wait()
        total = far[k, m, 0, :, 0:lanes]
        for index in range(1, batch):
            total = total + far[k, m, index, :, 0:lanes]
        return total

    def pack(k, m, which, at, width, sums):
        row = jnp.sum(sums, 0, keepdims=True)
        for j in range(row.shape[1] // width):
            index = which * 4 + at // width + j
            pay[k, m, index : index + 1, 0:width] = row[:, j * width : (j + 1) * width]

    def unpack_mid(total, which):
        return jnp.concatenate([total[which * 4 + j : which * 4 + j + 1, 0 : C // 4] for j in range(4)], axis=1)

    W4 = C // 4
    FWD = 2 * W4

    def zero(width):
        return jnp.zeros((8, width), F32)

    def mid_stats(k, m):
        def body(i, c):
            z = mid_f[chunk(m, i), :]
            v = valid_ref[chunk(m, i), :]
            zw = z * along(v, C)
            return c[0] + fold8(zw), c[1] + fold8(zw * z), c[2] + fold8(v)

        first, second, seen = lax.fori_loop(0, rows // CH, body, (zero(C), zero(C), zero(128)))
        pack(k, m, 0, 0, W4, first)
        pack(k, m, 1, 0, W4, second)
        pay[k, m, :, W4:FWD] = jnp.broadcast_to(jnp.sum(seen, 0, keepdims=True), (8, W4))
        sum_start(k, m, FWD)

    def mid_forward(k, l, which, m, zhat_ref, slope_ref, store, gi_ref):
        total = sum_end(k, m, FWD)
        n = total[0:1, W4:FWD]
        count[m] = jnp.broadcast_to(1.0 / n, (8, 128))
        rn = along(1.0 / n, C)
        mean = unpack_mid(total, 0) * rn
        inv = lax.rsqrt(unpack_mid(total, 1) * rn - mean * mean + EPS)
        gain = gm_ref[2 * l + which]
        shift = sm_ref[2 * l + which]
        gi_ref[l, m, 0:1, :] = gain * inv

        def body(i):
            at = chunk(m, i)
            v = along(valid_ref[at, :], C)
            zhat = (mid_f[at, :] - mean) * inv
            value = gain * zhat + shift
            s = jax.nn.sigmoid(value)
            zhat_ref[l, at, :] = zhat.astype(BF16)
            slope_ref[l, at, :] = (s * (1.0 + value * (1.0 - s)) * v).astype(BF16)
            store(at, (value * s * v).astype(BF16))

        loop(rows // CH, body)

    def mid_back_sums(k, l, m, zhat_ref, slope_ref):
        def body(i, c):
            at = chunk(m, i)
            d = mid_f[at, :].astype(BF16).astype(F32) * slope_ref[l, at, :].astype(F32)
            mid_f[at, :] = d
            return c[0] + fold8(d), c[1] + fold8(d * zhat_ref[l, at, :].astype(F32))

        first, second = lax.fori_loop(0, rows // CH, body, (zero(C), zero(C)))
        pack(k, m, 0, 0, W4, first)
        pack(k, m, 1, 0, W4, second)
        sum_start(k, m, W4)

    def mid_back(k, l, which, m, zhat_ref, gi_ref, store):
        total = sum_end(k, m, W4)
        sd, sz = unpack_mid(total, 0), unpack_mid(total, 1)
        gsm_ref[2 * l + which] += sd
        ggm_ref[2 * l + which] += sz
        rn = along(count[m, 0:1, :], C)
        sd, sz = sd * rn, sz * rn
        gi = gi_ref[l, m, 0:1, :]

        def body(i):
            at = chunk(m, i)
            v = along(valid_ref[at, :], C)
            zhat = zhat_ref[l, at, :].astype(F32)
            store(at, v * gi * (mid_f[at, :] - (sd + zhat * sz)))

        loop(rows // CH, body)

    def halo(buffer, m, down):
        to = my_w + 1 if down else my_w - 1
        side = 0 if down else 1
        return pltpu.make_async_remote_copy(
            src_ref=buffer.at[1, span(m), :],
            dst_ref=buffer.at[0 if down else 2, span(m), :],
            send_sem=halo_send.at[m, side],
            recv_sem=halo_recv.at[m, side],
            device_id=(my_b, to),
            device_id_type=MESH,
        )

    def halo_start(buffer, m):
        @pl.when(my_w < wide - 1)
        def _():
            halo(buffer, m, True).start()

        @pl.when(my_w > 0)
        def _():
            halo(buffer, m, False).start()

    def halo_wait(buffer, m):
        @pl.when(my_w < wide - 1)
        def _():
            halo(buffer, m, True).wait_send()
            halo(buffer, m, False).wait_recv()

        @pl.when(my_w > 0)
        def _():
            halo(buffer, m, False).wait_send()
            halo(buffer, m, True).wait_recv()

    HB = 256

    def heads(j):
        cols = pl.ds(pl.multiple_of(j * HB, HB), HB)
        for t in range(TASKS):
            taps_f[t, :, 0:HB] = dot(cot[:, t * HEAD : (t + 1) * HEAD], wh[t * HEAD : (t + 1) * HEAD, cols])

        def body(i):
            at = pl.ds(pl.multiple_of(i * CH, CH), CH)
            values = [taps_f[t, at, 0:HB] for t in range(TASKS)]
            total = values[0] + values[1] + values[2]
            size = jnp.abs(values[0]) + jnp.abs(values[1]) + jnp.abs(values[2])
            keep = 0.5 * (1.0 + total / jnp.maximum(size, FLOOR))
            offset = SHARP * (keep - thr[at, cols].astype(F32))
            up = jax.nn.sigmoid(offset)
            down = jax.nn.sigmoid(-offset)
            merged = jnp.zeros_like(total)
            for value in values:
                merged = merged + jnp.where(value > 0, up, down) * value
            thr[at, cols] = merged.astype(BF16)

        loop(2 * rows // CH, body)

    def staged(slot, dst):
        return pltpu.make_async_copy(stage.at[slot], dst, stage_sem.at[slot])

    def put(index, slot, value, dst):
        @pl.when(index >= 2)
        def _():
            staged(slot, dst).wait()

        stage[slot] = value.astype(BF16)
        staged(slot, dst).start()

    def put_end(dst):
        staged(0, dst).wait()
        staged(1, dst).wait()

    T = 256

    def grad_tiles(lhs, rhs, dst, begin, end):
        def body(i):
            for slot in range(2):
                at = pl.ds(pl.multiple_of((2 * i + slot) * T, T), T)
                put(2 * (i - begin // 2) + slot, slot, dot(lhs[:, at], rhs, TN), dst.at[at, :])

        loop(end // 2, body, begin // 2)
        put_end(dst.at[pl.ds(0, T), :])

    def grad_spatial(l, row_offset):
        for half in range(C // T):
            product = dot(act[l, row_offset, :, half * T : (half + 1) * T], dcs[...], TN)
            for c in range(3):
                index = half * 3 + c
                base = (3 * row_offset + c) * C + half * T
                put(index, index % 2, product[:, c * C : (c + 1) * C], gs_out.at[l, pl.ds(base, T), :])
        put_end(gs_out.at[l, pl.ds(0, T), :])

    def grad_heads(begin, end):
        def body(s):
            cols = pl.ds(pl.multiple_of(s * HB, HB), HB)
            wh[:, cols] = dot(cot_t[...], entry[2, :, cols]).astype(BF16)
            pltpu.make_async_copy(wh.at[:, cols], gh_out.at[s], out_sem.at[2]).start()

        loop(end, body, begin)

    ggm_ref[...] = jnp.zeros_like(ggm_ref)
    gsm_ref[...] = jnp.zeros_like(gsm_ref)
    ggo_ref[...] = jnp.zeros_like(ggo_ref)
    gso_ref[...] = jnp.zeros_like(gso_ref)
    load_act.wait()

    for l in range(2):
        load_wr(l).wait()

        def reduce_in(m):
            mid_f[span(m), :] = dot(entry[l, span(m), :], wr[...])
            mid_stats(0, m)

        loop(2, reduce_in)
        if l == 0:
            load_wr(1).start()
            load_cot.wait()
            load_wh.wait()
            load_thr.wait()
            cot_t[...] = cot[...].T
        heads(4 * l)
        loop(2, lambda m: sum_middle(0, m, FWD))
        heads(4 * l + 1)
        load_ws(l).wait()

        def conv_own(m):
            def store(at, value):
                act[l, 1, at, :] = value

            mid_forward(0, l, 0, m, za, sla, store, gia)
            halo_start(act.at[l], m)
            for c in range(3):
                taps_f[c, span(m), :] = dot(act[l, 1, span(m), :], ws[(3 + c) * C : (4 + c) * C, :])

        loop(2, conv_own)

        def conv_rest(m):
            halo_wait(act.at[l], m)
            for c in range(3):
                taps_f[c, span(m), :] += dot(act[l, 0, span(m), :], ws[c * C : (c + 1) * C, :]) + dot(
                    act[l, 2, span(m), :], ws[(6 + c) * C : (7 + c) * C, :]
                )

            def body(i):
                at = chunk(m, i)
                mid_f[at, :] = taps_f[1, at, :] + shifted(taps_f[0, at, :], 1) + shifted(taps_f[2, at, :], -1)

            loop(rows // CH, body)
            mid_stats(1, m)

        loop(2, conv_rest)
        if l == 0:
            load_ws(1).start()
        heads(4 * l + 2)
        loop(2, lambda m: sum_middle(1, m, FWD))
        heads(4 * l + 3)
        load_we(l).wait()

        def expand(m):
            def store(at, value):
                actb[l, at, :] = value

            mid_forward(1, l, 1, m, zb, slb, store, gib)
            for q in range(4):
                lanes = slice(q * Q, (q + 1) * Q)
                wide_f[span(m), lanes] = dot(actb[l, span(m), :], we[lanes, :], NT)

                def body(i, c):
                    z = wide_f[chunk(m, i), lanes]
                    zw = z * along(valid_ref[chunk(m, i), :], Q)
                    return c[0] + fold8(zw), c[1] + fold8(zw * z)

                first, second = lax.fori_loop(0, rows // CH, body, (zero(Q), zero(Q)))
                pack(2, m, 0, q * Q, Q, first)
                pack(2, m, 1, q * Q, Q, second)
            sum_start(2, m, Q)

        loop(2, expand)
        if l == 0:
            load_we(1).start()
        loop(2, lambda m: sum_middle(2, m, Q))

        def output(m):
            total = sum_end(2, m, Q)
            rn = along(count[m, 0:1, :], Q)
            for q in range(4):
                lanes = slice(q * Q, (q + 1) * Q)
                mean = total[q : q + 1] * rn
                inv = lax.rsqrt(total[4 + q : 5 + q] * rn - mean * mean + EPS)
                gain = go_ref[l, :, lanes]
                shift = so_ref[l, :, lanes]
                gic[l, m, 0:1, lanes] = gain * inv

                def body(i, c):
                    at = chunk(m, i)
                    v = along(valid_ref[at, :], Q)
                    zhat = (wide_f[at, lanes] - mean) * inv
                    below = entry[0, at, lanes].astype(F32) if l == 0 else carry[at, lanes]
                    before = gain * zhat + shift + below
                    s = jax.nn.sigmoid(before)
                    value = before * s * v
                    slope = s * (1.0 + before * (1.0 - s)) * v
                    zc[l, at, lanes] = zhat.astype(BF16)
                    slc[l, at, lanes] = slope.astype(BF16)
                    entry[l + 1, at, lanes] = value.astype(BF16)
                    if l == 0:
                        carry[at, lanes] = value
                        return c
                    d = thr[at, lanes].astype(F32) * slope
                    wide_f[at, lanes] = d
                    return c[0] + fold8(d), c[1] + fold8(d * zhat)

                if l == 0:
                    lax.fori_loop(0, rows // CH, body, 0)
                else:
                    first, second = lax.fori_loop(0, rows // CH, body, (zero(Q), zero(Q)))
                    pack(0, m, 0, q * Q, Q, first)
                    pack(0, m, 1, q * Q, Q, second)
            if l == 1:
                sum_start(0, m, Q)

        loop(2, output)

    store_y = pltpu.make_async_copy(entry.at[2], y_out, out_sem.at[0])
    store_y.start()
    half = wide // 2
    grad_heads(0, half)
    loop(2, lambda m: sum_middle(0, m, Q))
    grad_heads(half, wide)

    for l in (1, 0):
        if l == 0:
            load_we(0).wait()

        def back_out(m):
            total = sum_end(0, m, Q)
            rn = along(count[m, 0:1, :], Q)
            for q in range(4):
                lanes = slice(q * Q, (q + 1) * Q)
                sd, sz = total[q : q + 1], total[4 + q : 5 + q]
                gso_ref[l, :, lanes] += sd
                ggo_ref[l, :, lanes] += sz
                sd, sz = sd * rn, sz * rn
                gi = gic[l, m, 0:1, lanes]

                def body(i):
                    at = chunk(m, i)
                    v = along(valid_ref[at, :], Q)
                    zhat = zc[l, at, lanes].astype(F32)
                    dexp[at, lanes] = (v * gi * (wide_f[at, lanes] - (sd + zhat * sz))).astype(BF16)

                loop(rows // CH, body)
            mid_f[span(m), :] = dot(dexp[span(m), :], we[...])
            mid_back_sums(1, l, m, zb, slb)

        loop(2, back_out)
        if l == 1:
            load_we(0).start()
        grad_tiles(dexp, actb[l], ge_out.at[l], 0, 4)
        loop(2, lambda m: sum_middle(1, m, W4))
        grad_tiles(dexp, actb[l], ge_out.at[l], 4, 8)
        if l == 0:
            load_ws(0).wait()

        def back_conv(m):
            def store(at, value):
                low = value.astype(BF16)
                dcv[1, at, :] = low
                dcs[at, C : 2 * C] = low
                dcs[at, 0:C] = shifted(value, -1).astype(BF16)
                dcs[at, 2 * C : 3 * C] = shifted(value, 1).astype(BF16)

            mid_back(1, l, 1, m, zb, gib, store)
            halo_start(dcv, m)
            for c in range(3):
                taps_f[c, span(m), :] = dot(dcv[1, span(m), :], ws[(3 + c) * C : (4 + c) * C, :], NT)

        loop(2, back_conv)
        grad_spatial(l, 1)

        def back_rest(m):
            halo_wait(dcv, m)
            for c in range(3):
                taps_f[c, span(m), :] += dot(dcv[0, span(m), :], ws[(6 + c) * C : (7 + c) * C, :], NT) + dot(
                    dcv[2, span(m), :], ws[c * C : (c + 1) * C, :], NT
                )

            def body(i):
                at = chunk(m, i)
                mid_f[at, :] = taps_f[1, at, :] + shifted(taps_f[0, at, :], -1) + shifted(taps_f[2, at, :], 1)

            loop(rows // CH, body)
            mid_back_sums(2, l, m, za, sla)

        loop(2, back_rest)
        if l == 1:
            load_ws(0).start()
        grad_spatial(l, 0)
        loop(2, lambda m: sum_middle(2, m, W4))
        grad_spatial(l, 2)
        if l == 0:
            load_wr(0).wait()

        def back_in(m):
            def store(at, value):
                dred[at, :] = value.astype(BF16)

            mid_back(2, l, 0, m, za, gia, store)
            for q in range(4):
                lanes = slice(q * Q, (q + 1) * Q)
                taps_f[0, span(m), 0:Q] = dot(dred[span(m), :], wr[lanes, :], NT)

                def body(i, c):
                    at = chunk(m, i)
                    d = taps_f[0, at, 0:Q] + wide_f[at, lanes]
                    if l == 0:
                        dexp[at, lanes] = d.astype(BF16)
                        return c
                    d = d * slc[0, at, lanes].astype(F32)
                    wide_f[at, lanes] = d
                    return c[0] + fold8(d), c[1] + fold8(d * zc[0, at, lanes].astype(F32))

                if l == 0:
                    lax.fori_loop(0, rows // CH, body, 0)
                else:
                    first, second = lax.fori_loop(0, rows // CH, body, (zero(Q), zero(Q)))
                    pack(0, m, 0, q * Q, Q, first)
                    pack(0, m, 1, q * Q, Q, second)
            if l == 1:
                sum_start(0, m, Q)

        loop(2, back_in)
        if l == 1:
            load_wr(0).start()
            grad_tiles(entry.at[1], dred[...], gr_out.at[1], 0, 4)
            loop(2, lambda m: sum_middle(0, m, Q))
            grad_tiles(entry.at[1], dred[...], gr_out.at[1], 4, 8)
        else:
            store_dx = pltpu.make_async_copy(dexp, dx_out, out_sem.at[1])
            store_dx.start()
            grad_tiles(entry.at[0], dred[...], gr_out.at[0], 0, 8)

    store_y.wait()
    store_dx.wait()
    pltpu.make_async_copy(wh, wh, out_sem.at[2]).wait()


def run_block(act, thr, cot, valid, w_reduce, w_spatial, w_expand, w_heads, gm, sm, go, so):
    wide, batch = lax.axis_size("wide"), lax.axis_size("batch")
    M, D = act.shape
    C = w_reduce.shape[2]
    H = w_heads.shape[0]
    rows = M // 2
    Q = D // 4
    hbm = pl.BlockSpec(memory_space=pl.ANY)
    vmem = pl.BlockSpec(memory_space=pltpu.VMEM)
    V, DMA = pltpu.VMEM, pltpu.SemaphoreType.DMA
    scratch = [
        V((D, C), BF16), V((9 * C, C), BF16), V((D, C), BF16), V((H, D), BF16),
        V((3, M, D), BF16), V((M, D), F32), V((M, D), F32), V((M, D), BF16),
        V((M, H), BF16), V((H, M), BF16),
        V((2, 3, M, C), BF16), V((2, M, C), BF16), V((2, M, C), BF16),
        V((2, M, C), BF16), V((2, M, C), BF16), V((2, M, C), BF16),
        V((2, M, D), BF16), V((2, M, D), BF16),
        V((M, C), F32), V((3, M, C), F32),
        V((M, D), BF16), V((3, M, C), BF16), V((M, 3 * C), BF16), V((M, C), BF16),
        V((2, 2, 8, C), F32), V((2, 2, 8, C), F32), V((2, 2, 8, D), F32), V((2, 8, 128), F32),
        V((3, 2, 8, Q), F32), V((3, 2, 8, Q), F32),
        V((3, 2, wide, 8, Q), F32), V((3, 2, batch, 8, Q), F32),
        V((2, 256, C), BF16),
        DMA((7,)), DMA((3, 2, wide)), DMA((3, 2, wide)), DMA((3, 2, batch)), DMA((3, 2, batch)),
        DMA((2, 2)), DMA((2, 2)), DMA((2,)), DMA((3,)),
    ]
    shape = jax.ShapeDtypeStruct
    return pl.pallas_call(
        functools.partial(block_kernel, (wide, batch, rows, D, C)),
        out_shape=[
            shape((M, D), BF16), shape((M, D), BF16),
            shape((2, D, C), BF16), shape((2, 9 * C, C), BF16), shape((2, D, C), BF16), shape((wide, H, D // wide), BF16),
            shape((4, 1, C), F32), shape((4, 1, C), F32), shape((2, 1, D), F32), shape((2, 1, D), F32),
        ],
        in_specs=[hbm, hbm, hbm, vmem, hbm, hbm, hbm, hbm, vmem, vmem, vmem, vmem],
        out_specs=[hbm] * 6 + [vmem] * 4,
        scratch_shapes=scratch,
        compiler_params=pltpu.CompilerParams(
            collective_id=7, has_side_effects=True, vmem_limit_bytes=62 * 1024 * 1024
        ),
    )(act, thr, cot, valid, w_reduce, w_spatial, w_expand, w_heads, gm, sm, go, so)


def shards_rows(
    activations, bucket_ids, thresholds, head_cot, w_reduce, w_spatial, w_expand,
    gain_mid, shift_mid, gain_out, shift_out, w_heads,
):
    micro, images, pixels, D = activations.shape
    M = micro * images * pixels
    L, _, C = w_reduce.shape
    H = head_cot.shape[-1]
    wide = lax.axis_size("wide")
    positions = lax.axis_index("wide") * pixels + jnp.arange(pixels, dtype=jnp.int32)
    valid = jnp.broadcast_to(frame_mask(bucket_ids, positions).reshape(M, 1), (M, 128))
    y, dx, gr, gs, ge, gh, ggm, gsm, ggo, gso = run_block(
        activations.reshape(M, D), thresholds.reshape(M, D), head_cot.reshape(M, H), valid,
        w_reduce, w_spatial, w_expand, w_heads,
        gain_mid.reshape(2 * L, 1, C), shift_mid.reshape(2 * L, 1, C),
        gain_out.reshape(L, 1, D), shift_out.reshape(L, 1, D),
    )

    def total(array, dim):
        part = lax.psum_scatter(array, "wide", scatter_dimension=dim, tiled=True)
        return lax.psum(part, "batch").astype(F32)

    return (
        y.reshape(activations.shape),
        dx.reshape(activations.shape),
        total(gr, 1),
        total(gs, 1),
        total(ge, 1),
        ggm.reshape(L, 2, C),
        gsm.reshape(L, 2, C),
        ggo.reshape(L, D),
        gso.reshape(L, D),
        total(gh, 0)[0],
    )


def solution(mesh):
    placed = (
        P(None, "batch", "wide", None),
        P(None, "batch"),
        P(None, "batch", "wide", None),
        P(None, "batch", "wide", None),
        P(),
        P(),
        P(),
        P(),
        P(),
        P(),
        P(),
        P(),
    )
    def split(*arrays):
        micro, images, pixels, features = arrays[0].shape
        whole_rows = pixels == FRAME and FRAME == lax.axis_size("wide") and micro == 2 and (images * pixels) % 256 == 0
        return (shards_rows if whole_rows else shards)(*arrays)

    return jax.shard_map(
        split,
        mesh=mesh,
        in_specs=placed,
        out_specs=(
            P(None, "batch", "wide", None),
            P(None, "batch", "wide", None),
            P(None, "wide", None),
            P(None, "wide", None),
            P(None, "wide", None),
            P(),
            P(),
            P(),
            P(),
            P(None, "wide"),
        ),
        check_vma=False,
    )
```

```python
import functools

import jax
import jax.numpy as jnp
from jax import lax
from jax.experimental import pallas as pl
from jax.experimental.pallas import tpu as pltpu
from jax.sharding import PartitionSpec as P

HEAD = 256
TASKS = 3
FRAME = 8


EPS = 1e-05
SHARP = 8.0
FLOOR = 0.25
ROW_TABLE = (8, 8, 7, 6, 8, 5, 7, 8)
COL_TABLE = (8, 7, 8, 8, 6, 8, 7, 5)


def silu_slope(values):
    gate_val = jax.nn.sigmoid(values)
    return gate_val * (1.0 + values * (1.0 - gate_val))


def frame_mask(buckets, positions):
    bucket_kinds = jnp.arange(len(ROW_TABLE), dtype=jnp.int32)
    onehot = (buckets[..., None] == bucket_kinds).astype(jnp.int32)
    heights = jnp.sum(onehot * jnp.array(ROW_TABLE, dtype=jnp.int32), -1)
    widths = jnp.sum(onehot * jnp.array(COL_TABLE, dtype=jnp.int32), -1)
    rowpos = positions // FRAME
    colpos = positions % FRAME
    inside = (rowpos < heights[..., None]) & (colpos < widths[..., None])
    return inside.astype(jnp.float32)


def unfold_taps(images):
    padded = jnp.pad(images, ((0, 0), (1, 1), (1, 1), (0, 0)))
    pieces = [
        padded[:, row_off : row_off + FRAME, col_off : col_off + FRAME, :]
        for row_off in range(3)
        for col_off in range(3)
    ]
    return jnp.concatenate(pieces, -1)


def fold_taps(columns, channels):
    total_sum = jnp.zeros(columns.shape[:-1] + (channels,), columns.dtype)
    for tap_index in range(9):
        row_off, col_off = divmod(tap_index, 3)
        tap_part = columns[..., tap_index * channels : (tap_index + 1) * channels]
        padded = jnp.pad(tap_part, ((0, 0), (1, 1), (1, 1), (0, 0)))
        total_sum = (
            total_sum
            + padded[:, 2 - row_off : 2 - row_off + FRAME, 2 - col_off : 2 - col_off + FRAME, :]
        )
    return total_sum


def sum_kernel(wide, batch, x_ref, o_ref, near, far, part, near_send, near_recv, far_send, far_recv):
    my_w = lax.axis_index("wide")
    my_b = lax.axis_index("batch")
    barrier = pltpu.get_barrier_semaphore()
    for step in range(1, wide):
        pl.semaphore_signal(
            barrier, inc=1, device_id=(my_b, lax.rem(my_w + step, wide)), device_id_type=pl.DeviceIdType.MESH
        )
    for step in range(1, batch):
        pl.semaphore_signal(
            barrier, inc=1, device_id=(lax.rem(my_b + step, batch), my_w), device_id_type=pl.DeviceIdType.MESH
        )
    pl.semaphore_wait(barrier, wide + batch - 2)

    def exchange(src, slots, send, recv, count, me, target):
        copies = []
        for step in range(1, count):
            copy = pltpu.make_async_remote_copy(
                src_ref=src,
                dst_ref=slots.at[me],
                send_sem=send.at[step],
                recv_sem=recv.at[step],
                device_id=target(lax.rem(me + step, count)),
                device_id_type=pl.DeviceIdType.MESH,
            )
            copy.start()
            copies.append(copy)
        slots[me] = src[...]
        for copy in copies:
            copy.wait()
        total = slots[0]
        for index in range(1, count):
            total = total + slots[index]
        return total

    part[...] = exchange(x_ref, near, near_send, near_recv, wide, my_w, lambda w: (my_b, w))
    o_ref[...] = exchange(part, far, far_send, far_recv, batch, my_b, lambda b: (b, my_w))


def sum_all(values):
    wide, batch = lax.axis_size("wide"), lax.axis_size("batch")
    block = values.shape
    return pl.pallas_call(
        functools.partial(sum_kernel, wide, batch),
        out_shape=jax.ShapeDtypeStruct(block, jnp.float32),
        in_specs=[pl.BlockSpec(memory_space=pltpu.VMEM)],
        out_specs=pl.BlockSpec(memory_space=pltpu.VMEM),
        scratch_shapes=[
            pltpu.VMEM((wide,) + block, jnp.float32),
            pltpu.VMEM((batch,) + block, jnp.float32),
            pltpu.VMEM(block, jnp.float32),
            pltpu.SemaphoreType.DMA((wide,)),
            pltpu.SemaphoreType.DMA((wide,)),
            pltpu.SemaphoreType.DMA((batch,)),
            pltpu.SemaphoreType.DMA((batch,)),
        ],
        compiler_params=pltpu.CompilerParams(collective_id=block[-1] // 512, has_side_effects=True),
    )(values)


def batch_norm(values, valid_rows, scale_vec, offset_vec):
    weighted = values * valid_rows[..., None]
    sum_first = jnp.sum(weighted, 1)
    sum_second = jnp.sum(weighted * values, 1)
    counts = jnp.sum(valid_rows, 1)
    count_row = jnp.broadcast_to(counts[:, None], sum_first.shape)
    summed = sum_all(jnp.concatenate([sum_first, sum_second, count_row, jnp.zeros_like(sum_first)], 0))
    sum_first, sum_second, counts = summed[0:2], summed[2:4], summed[4:6, 0]
    mean_val = sum_first / counts[:, None]
    spread = sum_second / counts[:, None] - mean_val * mean_val
    inv_std = lax.rsqrt(spread + EPS)
    normed = (values - mean_val[:, None, :]) * inv_std[:, None, :]
    return (normed, scale_vec * normed + offset_vec, inv_std, counts)


def norm_back(grad_out, normed, inv_std, counts, valid_rows, scale_vec):
    sum_grad = jnp.sum(grad_out, 1)
    sum_prod = jnp.sum(grad_out * normed, 1)
    summed = sum_all(jnp.concatenate([sum_grad, sum_prod, sum_grad, sum_prod], 0))
    sum_grad, sum_prod = summed[0:2], summed[2:4]
    centered = (
        grad_out - (sum_grad[:, None, :] + normed * sum_prod[:, None, :]) / counts[:, None, None]
    )
    grad_in = valid_rows[..., None] * scale_vec * inv_std[:, None, :] * centered
    return (grad_in, jnp.sum(sum_prod, 0), jnp.sum(sum_grad, 0))


def forward_layer(layer_in, pix_valid, img_valid, params, layout):
    w_in, w_mid, w_out, scale_a, offset_a, scale_b, offset_b, scale_c, offset_c = params
    groups, per_lane, local_imgs = layout
    span_len = layer_in.shape[0]
    channels = w_in.shape[1]
    entry_low = layer_in.astype(jnp.bfloat16)
    reduced = jnp.einsum("mrd,dc->mrc", entry_low, w_in, preferred_element_type=jnp.float32)
    normed_a, bn_a, inv_a, counts = batch_norm(reduced, pix_valid, scale_a, offset_a)
    act_a = (jax.nn.silu(bn_a) * pix_valid[..., None]).astype(jnp.bfloat16)
    arrived = lax.all_to_all(
        act_a.reshape(span_len, groups, per_lane, channels),
        "wide",
        split_axis=1,
        concat_axis=2,
        tiled=True,
    )
    count_imgs = arrived.shape[1]
    images = arrived.reshape(span_len * count_imgs, FRAME, FRAME, channels)
    columns = unfold_taps(images).reshape(span_len, count_imgs, FRAME * FRAME, 9 * channels)
    conv_out = jnp.einsum("mkpc,co->mkpo", columns, w_mid, preferred_element_type=jnp.float32)
    taps_saved, conv_out = (columns, conv_out)
    taps_saved = taps_saved.reshape(span_len, -1, taps_saved.shape[-1])
    conv_out = conv_out.reshape(span_len, -1, channels)
    normed_b, bn_b, inv_b, unused_counts = batch_norm(conv_out, img_valid, scale_b, offset_b)
    act_b = (jax.nn.silu(bn_b) * img_valid[..., None]).astype(jnp.bfloat16)
    returned = lax.all_to_all(
        act_b.reshape(span_len, local_imgs, FRAME * FRAME, channels),
        "wide",
        split_axis=2,
        concat_axis=1,
        tiled=True,
    ).reshape(span_len, -1, channels)
    expanded = jnp.einsum("mrc,oc->mro", returned, w_out, preferred_element_type=jnp.float32)
    normed_c, bn_c, inv_c, unused_again = batch_norm(expanded, pix_valid, scale_c, offset_c)
    before = bn_c + layer_in
    result = jax.nn.silu(before) * pix_valid[..., None]
    saved = (
        entry_low,
        normed_a,
        bn_a,
        inv_a,
        taps_saved,
        normed_b,
        bn_b,
        inv_b,
        returned,
        normed_c,
        before,
        inv_c,
        counts,
    )
    return (result, saved)


def backward_layer(incoming, saved, pix_valid, img_valid, params, layout):
    w_in, w_mid, w_out, scale_a, offset_a, scale_b, offset_b, scale_c, offset_c = params
    groups, per_lane, local_imgs = layout
    (
        entry_low,
        normed_a,
        bn_a,
        inv_a,
        taps_saved,
        normed_b,
        bn_b,
        inv_b,
        returned,
        normed_c,
        before,
        inv_c,
        counts,
    ) = saved
    span_len = incoming.shape[0]
    channels = w_in.shape[1]
    grad_pre = incoming * pix_valid[..., None] * silu_slope(before)
    grad_c, scale_gc, offset_gc = norm_back(grad_pre, normed_c, inv_c, counts, pix_valid, scale_c)
    grad_c_low = grad_c.astype(jnp.bfloat16)
    g_out = jnp.einsum("mro,mrc->oc", grad_c_low, returned, preferred_element_type=jnp.float32)
    d_returned = jnp.einsum(
        "mro,oc->mrc", grad_c_low, w_out, preferred_element_type=jnp.float32
    ).astype(jnp.bfloat16)
    d_images = lax.all_to_all(
        d_returned.reshape(span_len, groups, per_lane, channels),
        "wide",
        split_axis=1,
        concat_axis=2,
        tiled=True,
    ).reshape(span_len, -1, channels)
    d_bn_b = d_images.astype(jnp.float32) * img_valid[..., None] * silu_slope(bn_b)
    grad_b, scale_gb, offset_gb = norm_back(d_bn_b, normed_b, inv_b, counts, img_valid, scale_b)
    grad_b_low = grad_b.astype(jnp.bfloat16)
    g_mid = jnp.einsum("mrk,mro->ko", taps_saved, grad_b_low, preferred_element_type=jnp.float32)
    d_columns = jnp.einsum("mro,ko->mrk", grad_b_low, w_mid, preferred_element_type=jnp.float32)
    d_act = fold_taps(
        d_columns.reshape(span_len * local_imgs, FRAME, FRAME, 9 * channels), channels
    )
    d_act = d_act.astype(jnp.bfloat16).reshape(span_len, local_imgs, FRAME * FRAME, channels)
    d_pixels = lax.all_to_all(d_act, "wide", split_axis=2, concat_axis=1, tiled=True).reshape(
        span_len, -1, channels
    )
    d_bn_a = d_pixels.astype(jnp.float32) * pix_valid[..., None] * silu_slope(bn_a)
    grad_a, scale_ga, offset_ga = norm_back(d_bn_a, normed_a, inv_a, counts, pix_valid, scale_a)
    grad_a_low = grad_a.astype(jnp.bfloat16)
    g_in = jnp.einsum("mrd,mrc->dc", entry_low, grad_a_low, preferred_element_type=jnp.float32)
    d_entry = jnp.einsum("mrc,dc->mrd", grad_a_low, w_in, preferred_element_type=jnp.float32)
    return (
        d_entry + grad_pre,
        (g_in, g_mid, g_out),
        (scale_ga, offset_ga, scale_gb, offset_gb, scale_gc, offset_gc),
    )


def grad_drop(task_values, limits):
    task_total = task_values[0]
    magnitude = jnp.abs(task_values[0])
    for task_index in range(1, len(task_values)):
        task_total = task_total + task_values[task_index]
        magnitude = magnitude + jnp.abs(task_values[task_index])
    keep_ratio = 0.5 * (1.0 + task_total / jnp.maximum(magnitude, FLOOR))
    upward = jax.nn.sigmoid(SHARP * (keep_ratio - limits))
    downward = jax.nn.sigmoid(SHARP * (limits - keep_ratio))
    merged = jnp.zeros_like(task_total)
    for task_value in task_values:
        merged = merged + jnp.where(task_value > 0, upward, downward) * task_value
    return merged


def add_tuples(left, right):
    return tuple((left_item + right_item for left_item, right_item in zip(left, right)))


def shards(
    activations,
    bucket_ids,
    thresholds,
    head_cot,
    w_reduce,
    w_spatial,
    w_expand,
    gain_mid,
    shift_mid,
    gain_out,
    shift_out,
    w_heads,
):
    micro_total, groups, per_lane, features = activations.shape
    lane_count = lax.axis_size("wide")
    local_imgs = groups // lane_count
    lane_index = lax.axis_index("wide")
    layout = (groups, per_lane, local_imgs)
    pix_positions = lane_index * per_lane + jnp.arange(per_lane, dtype=jnp.int32)
    pix_valid_all = frame_mask(bucket_ids, pix_positions).reshape(micro_total, -1)
    own_ids = lax.dynamic_slice_in_dim(bucket_ids, lane_index * local_imgs, local_imgs, 1)
    img_valid_all = frame_mask(own_ids, jnp.arange(FRAME * FRAME, dtype=jnp.int32)).reshape(
        micro_total, -1
    )
    layer_total = w_reduce.shape[0]
    head_width = head_cot.shape[-1]
    layer_params = [
        (
            w_reduce[layer_index],
            w_spatial[layer_index],
            w_expand[layer_index],
            gain_mid[layer_index, 0],
            shift_mid[layer_index, 0],
            gain_mid[layer_index, 1],
            shift_mid[layer_index, 1],
            gain_out[layer_index],
            shift_out[layer_index],
        )
        for layer_index in range(layer_total)
    ]
    spans = [(0, micro_total)]
    weight_acc = [None] * layer_total
    norm_acc = [None] * layer_total
    heads_acc = jnp.zeros((features, head_width), jnp.float32)
    outs_y = []
    outs_dx = []
    for span_at, span_len in spans:

        def take_span(array):
            return lax.slice_in_dim(array, span_at, span_at + span_len, axis=0)

        pix_valid = take_span(pix_valid_all)
        img_valid = take_span(img_valid_all)
        carried = take_span(activations).reshape(span_len, -1, features).astype(jnp.float32)
        saved_layers = []
        for layer_index in range(layer_total):
            carried, saved = forward_layer(
                carried, pix_valid, img_valid, layer_params[layer_index], layout
            )
            saved_layers.append(saved)
        result_low = carried.astype(jnp.bfloat16)
        outs_y.append(result_low.reshape(span_len, groups, per_lane, features))
        head_grads = take_span(head_cot).reshape(span_len, -1, head_width)
        heads_acc = heads_acc + jnp.einsum(
            "mrd,mrh->dh", result_low, head_grads, preferred_element_type=jnp.float32
        )
        task_values = [
            jnp.einsum(
                "mrh,hd->mrd",
                head_grads[..., task_index * HEAD : (task_index + 1) * HEAD],
                w_heads[task_index * HEAD : (task_index + 1) * HEAD],
                preferred_element_type=jnp.float32,
            )
            for task_index in range(TASKS)
        ]
        limits = take_span(thresholds).reshape(span_len, -1, features).astype(jnp.float32)
        incoming = grad_drop(task_values, limits)
        for layer_index in reversed(range(layer_total)):
            incoming, weight_parts, norm_parts = backward_layer(
                incoming,
                saved_layers[layer_index],
                pix_valid,
                img_valid,
                layer_params[layer_index],
                layout,
            )
            if weight_acc[layer_index] is None:
                weight_acc[layer_index] = weight_parts
                norm_acc[layer_index] = norm_parts
            else:
                weight_acc[layer_index] = add_tuples(weight_acc[layer_index], weight_parts)
                norm_acc[layer_index] = add_tuples(norm_acc[layer_index], norm_parts)
        outs_dx.append(incoming.astype(jnp.bfloat16).reshape(span_len, groups, per_lane, features))
    stack_in = jnp.stack([layer_acc[0] for layer_acc in weight_acc])
    stack_mid = jnp.stack([layer_acc[1] for layer_acc in weight_acc])
    stack_out = jnp.stack([layer_acc[2] for layer_acc in weight_acc])
    shard_in, shard_mid, shard_out, shard_heads = (
        lax.psum_scatter(
            stack_in.astype(jnp.bfloat16), "wide", scatter_dimension=1, tiled=True
        ).astype(jnp.float32),
        lax.psum_scatter(
            stack_mid.astype(jnp.bfloat16), "wide", scatter_dimension=1, tiled=True
        ).astype(jnp.float32),
        lax.psum_scatter(
            stack_out.astype(jnp.bfloat16), "wide", scatter_dimension=1, tiled=True
        ).astype(jnp.float32),
        lax.psum_scatter(
            heads_acc[None].astype(jnp.bfloat16), "wide", scatter_dimension=1, tiled=True
        ).astype(jnp.float32),
    )
    shard_in, shard_mid, shard_out, shard_heads = (
        lax.psum(shard_in.astype(jnp.bfloat16), "batch").astype(jnp.float32),
        lax.psum(shard_mid.astype(jnp.bfloat16), "batch").astype(jnp.float32),
        lax.psum(shard_out.astype(jnp.bfloat16), "batch").astype(jnp.float32),
        lax.psum(shard_heads.astype(jnp.bfloat16), "batch").astype(jnp.float32),
    )
    g_gain_mid = jnp.stack([jnp.stack([layer_norm[0], layer_norm[2]]) for layer_norm in norm_acc])
    g_shift_mid = jnp.stack([jnp.stack([layer_norm[1], layer_norm[3]]) for layer_norm in norm_acc])
    g_gain_out = jnp.stack([layer_norm[4] for layer_norm in norm_acc])
    g_shift_out = jnp.stack([layer_norm[5] for layer_norm in norm_acc])
    return (
        jnp.concatenate(outs_y, 0),
        jnp.concatenate(outs_dx, 0),
        shard_in,
        shard_mid,
        shard_out,
        g_gain_mid,
        g_shift_mid,
        g_gain_out,
        g_shift_out,
        shard_heads[0].T,
    )


MESH = pl.DeviceIdType.MESH
F32, BF16 = jnp.float32, jnp.bfloat16
NN = (((1,), (0,)), ((), ()))
NT = (((1,), (1,)), ((), ()))
TN = (((0,), (0,)), ((), ()))
CH = 16
HB = 256

VMEM_BYTES = 63 * 1024 * 1024
SUB_H, SUB_E, SUB_S, SUB_R = 2, 2, 3, 2
SUBS = 3
AGENDA = {
    "1_0": ("H_p0", "H_b0", "H_p1"),
    "1_0b": ("H_b1",),
    "1_1": ("E1_p0",),
    "1_2": ("E1_b0", "E1_p1"),
    "1_3": ("E1_b1",),
    "1_3b": ("H_c",),
    "1_4": ("E1_c",),
    "1_5": ("S1_p0", "S1_b0", "S1_p1", "S1_b1"),
    "1_5b": ("S1_p2", "H_d0", "E1_d", "H_d1"),
    "1_6": ("R1_p", "S1_b2"),
    "0_0": ("R1_b0", "E1_e0", "S1_c", "E1_e1"),
    "0_0b": ("E1_f",),
    "0_1": ("H_e",),
    "0_2": ("R1_b1", "S1_d0", "H_f0", "S1_d1", "S1_d2", "R1_c0"),
    "0_2b": ("S1_e0", "E0_p"),
    "0_3": ("E0_b", "S1_f0", "R1_c1", "R1_d0", "S1_e1"),
    "0_3b": (
        "E0_c0", "H_g0", "E0_c1", "R1_d1", "S0_p0", "S0_b0", "R1_e0", "S1_e2", "S1_f1", "S0_p1", "H_f1", "S0_p2",
        "S0_b1", "E0_d", "R1_e1",
    ),
    "0_4": ("S0_c0", "E0_e0", "S0_c1", "S0_b2", "R1_f0", "E0_e1", "E1_g", "S0_d0", "R1_f1", "S1_f2"),
    "0_5": (
        "S0_d1", "D_1", "E0_f0", "S0_c2", "R0_p0", "S0_e0", "R0_p1", "R0_b0", "E0_f1", "R0_b1", "S0_d2", "S0_e1",
        "D_0", "R1_g", "S1_g", "S0_f0", "R0_c", "S0_e2", "R0_d0", "S0_f1", "R0_d1", "E0_g0", "D_3", "R0_e0",
        "S0_f2", "R0_e1", "E0_g1", "R0_f", "D_2", "H_g1", "S0_g", "R0_g",
    ),
}


def dot(left, right, dims=NN):
    return lax.dot_general(left, right, dims, preferred_element_type=F32)


def along(column, lanes):
    return column if lanes == 128 else jnp.concatenate([column] * (lanes // 128), axis=1)


def sigmoid(v):
    return 0.5 * jnp.tanh(0.5 * v) + 0.5


def fold8(block):
    total = block[0:8]
    for at in range(8, block.shape[0], 8):
        total = total + block[at : at + 8]
    return total


def shifted(block, by):
    rows, lanes = block.shape
    grouped = block.reshape(rows // FRAME, FRAME, lanes)
    pixel = lax.broadcasted_iota(jnp.int32, grouped.shape, 1)
    moved = pltpu.roll(grouped, by % FRAME, 1)
    keep = pixel > 0 if by == 1 else pixel < FRAME - 1
    return jnp.where(keep, moved, 0.0).reshape(rows, lanes)


def loop(n, body, start=0):
    def step(i, c):
        body(i)
        return c

    lax.fori_loop(start, n, step, 0)


def block_kernel(
    dims,
    act_in, thr_in, cot_in, valid_ref, wr_in, ws_in, we_in, wh_in, gm_ref, sm_ref, go_ref, so_ref,
    y_out, dx_out, gr_out, gs_out, ge_out, gh_out, ggm_ref, gsm_ref, ggo_ref, gso_ref, zc_far, slc_far,
    wr, ws, we, wh, entry, wide_f, thr, cot, cot_t, act, za, sla, actb, zb, slb, zc, slc,
    mid_f, taps_f, dcv, dcs, dred, gia, gib, gic, count, pay, part, near, far,
    ger, gs, recv_h, recv_s, recv_e, recv_r,
    load_sem, near_send, near_recv, far_send, far_recv, halo_send, halo_recv, out_sem, rs_send, rs_recv, emit_sem,
):
    wide, batch, rows, D, C, H = dims
    my_w = lax.axis_index("wide")
    my_b = lax.axis_index("batch")
    Q = D // 4
    M = 2 * rows
    dexp = thr

    def span(m):
        return pl.ds(pl.multiple_of(m * rows, rows), rows)

    def chunk(m, i):
        return pl.ds(pl.multiple_of(m * rows + i * CH, CH), CH)

    def load(src, dst, index):
        return pltpu.make_async_copy(src, dst, load_sem.at[index])

    def load_wr(l):
        return load(wr_in.at[l], wr, 0)

    def load_ws(l):
        return load(ws_in.at[l], ws, 1)

    def load_we(l):
        return load(we_in.at[l], we, 2)

    load_act = load(act_in, entry.at[0], 3)
    load_wh = load(wh, wh, 4)
    load_thr = load(thr_in, thr, 5)
    load_cot = load(cot_in, cot, 6)
    load_act.start()
    load_wr(0).start()
    load_ws(0).start()
    load_we(0).start()
    load_cot.start()
    for j in range(D // HB):
        load(wh_in.at[:, pl.ds(j * HB, HB)], wh.at[j], 4).start()
    load_thr.start()

    for side in (0, 2):
        for l in range(2):
            act[l, side] = jnp.zeros(act.shape[2:], BF16)
        dcv[side // 2] = jnp.zeros(dcv.shape[1:], BF16)

    barrier = pltpu.get_barrier_semaphore()
    for step in range(1, wide):
        pl.semaphore_signal(barrier, inc=1, device_id=(my_b, lax.rem(my_w + step, wide)), device_id_type=MESH)
    for step in range(1, batch):
        pl.semaphore_signal(barrier, inc=1, device_id=(lax.rem(my_b + step, batch), my_w), device_id_type=MESH)

    def near_copy(k, m, step, lanes):
        return pltpu.make_async_remote_copy(
            src_ref=pay.at[k, m, :, pl.ds(0, lanes)],
            dst_ref=near.at[k, m, my_w, :, pl.ds(0, lanes)],
            send_sem=near_send.at[k, m, step],
            recv_sem=near_recv.at[k, m, step],
            device_id=(my_b, lax.rem(my_w + step, wide)),
            device_id_type=MESH,
        )

    def far_copy(k, m, step, lanes):
        return pltpu.make_async_remote_copy(
            src_ref=part.at[k, m, :, pl.ds(0, lanes)],
            dst_ref=far.at[k, m, my_b, :, pl.ds(0, lanes)],
            send_sem=far_send.at[k, m, step],
            recv_sem=far_recv.at[k, m, step],
            device_id=(lax.rem(my_b + step, batch), my_w),
            device_id_type=MESH,
        )

    def sum_start(k, m, lanes):
        for step in range(1, wide):
            near_copy(k, m, step, lanes).start()
        near[k, m, my_w, :, 0:lanes] = pay[k, m, :, 0:lanes]

    def sum_middle(k, m, lanes):
        for step in range(1, wide):
            near_copy(k, m, step, lanes).wait()
        total = near[k, m, 0, :, 0:lanes]
        for index in range(1, wide):
            total = total + near[k, m, index, :, 0:lanes]
        part[k, m, :, 0:lanes] = total
        for step in range(1, batch):
            far_copy(k, m, step, lanes).start()
        far[k, m, my_b, :, 0:lanes] = total

    def sum_end(k, m, lanes):
        for step in range(1, batch):
            far_copy(k, m, step, lanes).wait()
        total = far[k, m, 0, :, 0:lanes]
        for index in range(1, batch):
            total = total + far[k, m, index, :, 0:lanes]
        return total

    def pack(k, m, which, at, width, sums):
        row = jnp.sum(sums, 0, keepdims=True)
        for j in range(row.shape[1] // width):
            index = which * 4 + at // width + j
            pay[k, m, index : index + 1, 0:width] = row[:, j * width : (j + 1) * width]

    def unpack_mid(total, which):
        return jnp.concatenate([total[which * 4 + j : which * 4 + j + 1, 0 : C // 4] for j in range(4)], axis=1)

    W4 = C // 4
    FWD = 2 * W4

    def zero(width):
        return jnp.zeros((8, width), F32)

    def mid_stats(k, m):
        def body(i, c):
            z = mid_f[chunk(m, i), :]
            v = valid_ref[chunk(m, i), :]
            zw = z * along(v, C)
            return c[0] + fold8(zw), c[1] + fold8(zw * z), c[2] + fold8(v)

        first, second, seen = lax.fori_loop(0, rows // CH, body, (zero(C), zero(C), zero(128)))
        pack(k, m, 0, 0, W4, first)
        pack(k, m, 1, 0, W4, second)
        pay[k, m, :, W4:FWD] = jnp.broadcast_to(jnp.sum(seen, 0, keepdims=True), (8, W4))
        sum_start(k, m, FWD)

    def mid_forward(k, l, which, m, zhat_ref, slope_ref, store, gi_ref):
        total = sum_end(k, m, FWD)
        n = total[0:1, W4:FWD]
        count[m] = jnp.broadcast_to(1.0 / n, (8, 128))
        rn = along(1.0 / n, C)
        mean = unpack_mid(total, 0) * rn
        inv = lax.rsqrt(unpack_mid(total, 1) * rn - mean * mean + EPS)
        gain = gm_ref[l, which : which + 1, :]
        shift = sm_ref[l, which : which + 1, :]
        gi_ref[l, m, 0:1, :] = gain * inv

        def body(i):
            at = chunk(m, i)
            v = along(valid_ref[at, :], C)
            zhat = (mid_f[at, :] - mean) * inv
            value = gain * zhat + shift
            s = sigmoid(value)
            zhat_ref[l, at, :] = zhat.astype(BF16)
            slope_ref[l, at, :] = (s * (1.0 + value * (1.0 - s)) * v).astype(BF16)
            store(at, (value * s * v).astype(BF16))

        loop(rows // CH, body)

    def mid_back_sums(k, l, m, zhat_ref, slope_ref):
        def body(i, c):
            at = chunk(m, i)
            d = mid_f[at, :].astype(BF16).astype(F32) * slope_ref[l, at, :].astype(F32)
            mid_f[at, :] = d
            return c[0] + fold8(d), c[1] + fold8(d * zhat_ref[l, at, :].astype(F32))

        first, second = lax.fori_loop(0, rows // CH, body, (zero(C), zero(C)))
        pack(k, m, 0, 0, W4, first)
        pack(k, m, 1, 0, W4, second)
        sum_start(k, m, W4)

    def mid_back(k, l, which, m, zhat_ref, gi_ref, store):
        total = sum_end(k, m, W4)
        sd, sz = unpack_mid(total, 0), unpack_mid(total, 1)
        gsm_ref[l, which : which + 1, :] += sd
        ggm_ref[l, which : which + 1, :] += sz
        rn = along(count[m, 0:1, :], C)
        sd, sz = sd * rn, sz * rn
        gi = gi_ref[l, m, 0:1, :]

        def body(i):
            at = chunk(m, i)
            v = along(valid_ref[at, :], C)
            zhat = zhat_ref[l, at, :].astype(F32)
            store(at, v * gi * (mid_f[at, :] - (sd + zhat * sz)))

        loop(rows // CH, body)

    def halo(buffers, m, down):
        to = my_w + 1 if down else my_w - 1
        side = 0 if down else 1
        return pltpu.make_async_remote_copy(
            src_ref=buffers[1].at[span(m), :],
            dst_ref=buffers[0 if down else 2].at[span(m), :],
            send_sem=halo_send.at[m, side],
            recv_sem=halo_recv.at[m, side],
            device_id=(my_b, to),
            device_id_type=MESH,
        )

    def halo_start(buffer, m):
        @pl.when(my_w < wide - 1)
        def _():
            halo(buffer, m, True).start()

        @pl.when(my_w > 0)
        def _():
            halo(buffer, m, False).start()

    def halo_wait(buffer, m):
        @pl.when(my_w < wide - 1)
        def _():
            halo(buffer, m, True).wait_send()
            halo(buffer, m, False).wait_recv()

        @pl.when(my_w > 0)
        def _():
            halo(buffer, m, False).wait_send()
            halo(buffer, m, True).wait_recv()

    def heads(j):
        cols = pl.ds(pl.multiple_of(j * HB, HB), HB)
        for t in range(TASKS):
            taps_f[t, :, 0:HB] = dot(cot[:, t * HEAD : (t + 1) * HEAD], wh[j, t * HEAD : (t + 1) * HEAD, :])

        def body(i):
            at = pl.ds(pl.multiple_of(i * CH, CH), CH)
            values = [taps_f[t, at, 0:HB] for t in range(TASKS)]
            total = values[0] + values[1] + values[2]
            size = jnp.abs(values[0]) + jnp.abs(values[1]) + jnp.abs(values[2])
            keep = 0.5 * (1.0 + total / jnp.maximum(size, FLOOR))
            offset = SHARP * (keep - thr[at, cols].astype(F32))
            up = sigmoid(offset)
            down = 1.0 - up
            merged = jnp.zeros_like(total)
            for value in values:
                merged = merged + jnp.where(value > 0, up, down) * value
            thr[at, cols] = merged.astype(BF16)

        loop(2 * rows // CH, body)

    T = 256
    core, my_x, my_y = lax.rem(my_w, 2), lax.rem(my_w // 2, 2), my_w // 4
    to_core, to_x, to_y = 1 - 2 * core, 2 - 4 * my_x, 4 - 8 * my_y
    first = to_x * (1 - core) + to_y * core
    second = to_x * core + to_y * (1 - core)
    twin = my_w + to_core
    own = [my_w + to_x + to_y, my_w + first, my_w + second, my_w]
    theirs = [twin + to_x + to_y, twin + second, twin + first, twin]
    inner = (my_b == 1) | (my_b == 2)
    outer = (my_b == 0) | (my_b == 3)

    def tall(s):
        return pl.ds(pl.multiple_of(s * T, T), T)

    def grad_tall(held, lhs, rhs, mine):
        def body(i):
            s = 2 * i + (core if mine else 1 - core)
            held[tall(s), :] = dot(lhs[:, tall(s)], rhs, TN).astype(BF16)

        loop(wide // 2, body)

    def grad_heads(mine):
        def body(i):
            s = 2 * i + (core if mine else 1 - core)
            wh[s] = dot(cot_t[...], entry[2, :, tall(s)]).astype(BF16)

        loop(wide // 2, body)

    def grad_spatial(l, row_offset):
        def body(half):
            product = dot(act[l, row_offset, :, tall(half)], dcs[...], TN).astype(BF16)
            for c in range(3):
                base = pl.multiple_of((3 * row_offset + c) * C + half * T, T)
                gs[pl.ds(base, T), :] = product[:, c * C : (c + 1) * C]

        loop(C // T, body)

    def add_into(dst, src, n):
        step = 32

        def body(i):
            at = pl.ds(pl.multiple_of(i * step, step), step)
            dst[at, :] = dst[at, :] + src[at, :]

        loop(n // step, body)

    emitted = []

    def emit(kind, j, src_inner, src_outer, dst):
        pl.when(inner)(lambda: pltpu.make_async_copy(src_inner, dst, emit_sem.at[kind, j]).start())
        pl.when(outer)(lambda: pltpu.make_async_copy(src_outer, dst, emit_sem.at[kind, j]).start())
        emitted.append(pltpu.make_async_copy(src_inner, dst, emit_sem.at[kind, j]))

    class Reduce:
        def __init__(self, kind, piece, recv_a, recv, final, n, lanes, sub, out):
            self.kind, self.piece, self.recv_a, self.recv, self.final = kind, piece, recv_a, recv, final
            self.n, self.lanes, self.sub, self.out = n, lanes, sub, out
            self.size = n // sub

        def rows_of(self, ref, j):
            return ref.at[pl.ds(j * self.size, self.size), :]

        def copy(self, j, index, src, dst, where):
            return pltpu.make_async_remote_copy(
                src_ref=src,
                dst_ref=dst,
                send_sem=rs_send.at[self.kind, j, index],
                recv_sem=rs_recv.at[self.kind, j, index],
                device_id=where,
                device_id_type=MESH,
            )

        def a_copy(self, p):
            return self.copy(0, p, self.piece(theirs[p]), self.recv_a(p), (my_b, twin))

        def b_copy(self, j, i):
            src, dst = self.rows_of(self.piece(own[i]), j), self.recv(i, j)
            return self.copy(j, 4 + i, src, dst, (my_b, my_w + first))

        def c_copy(self, j):
            src, dst = self.rows_of(self.piece(own[2]), j), self.recv(2, j)
            return self.copy(j, 6, src, dst, (my_b, my_w + second))

        def z_copy(self, j, step):
            dst = self.recv(4 if step == 1 else 3, j)
            to = (1 + my_b // 2, 3 - my_b, 3 * (my_b - 1))[step]
            return self.copy(j, 7 + step, self.final(j), dst, (to, my_w))

        def a(self):
            for p in range(4):
                self.a_copy(p).start()

        def p(self, j):
            if j == 0:
                for p in range(4):
                    self.a_copy(p).wait()
            for p in range(4):
                add_into(self.rows_of(self.piece(own[p]), j), self.rows_of(self.recv_a(p), j), self.size)

        def b(self, j):
            for p in range(2):
                self.b_copy(j, p).start()

        def c(self, j):
            for i in range(2):
                self.b_copy(j, i).wait()
                add_into(self.rows_of(self.piece(own[2 + i]), j), self.recv(i, j), self.size)
                if i == 0:
                    self.c_copy(j).start()

        def d(self, j):
            self.c_copy(j).wait()
            final, mine, other = self.final(j), self.rows_of(self.piece(own[3]), j), self.recv(2, j)

            def body(i):
                at = pl.ds(pl.multiple_of(i * 32, 32), 32)
                final[at, :] = mine[at, :] + other[at, :]

            loop(self.size // 32, body)

            @pl.when(outer)
            def _():
                self.z_copy(j, 0).start()

        def e(self, j):
            @pl.when(inner)
            def _():
                self.z_copy(j, 0).wait_recv()
                add_into(self.final(j), self.recv(3, j), self.size)
                self.z_copy(j, 1).start()

        def f(self, j):
            @pl.when(inner)
            def _():
                self.z_copy(j, 1).wait()
                add_into(self.final(j), self.recv(4, j), self.size)
                self.z_copy(j, 2).start()

        def g(self, j):
            @pl.when(outer)
            def _():
                self.z_copy(j, 2).wait_recv()
                self.z_copy(j, 0).wait_send()

            @pl.when(inner)
            def _():
                self.z_copy(j, 2).wait_send()

            dst = self.out.at[pl.ds(j * self.size, self.size), :]
            emit(self.kind, j, self.final(j), self.recv(3, j), dst)

    def block(ref, index, n):
        begin, size = n
        return ref.at[pl.ds((index // 4) * T + begin, size), pl.ds((index % 4) * C, C)]

    def make_heads():
        def recv(index, j):
            return recv_h.at[index, pl.ds(j * (H // SUB_H), H // SUB_H), :]

        def recv_a(p):
            return gs.at[pl.ds(p * H, H), pl.ds(0, HB)]

        return Reduce(0, lambda s: wh.at[s], recv_a, recv, lambda j: recv(2, j), H, HB, SUB_H, gh_out)

    def make_spatial(l):
        n = 9 * C // wide
        size = n // SUB_S

        def recv(index, j):
            if l == 1 or index < 2:
                return recv_s.at[4 + index, pl.ds(j * size, size), :]
            if index == 2:
                return block(zc, 5 + j, (0, size))
            return slc.at[pl.ds((index - 3) * size, size), pl.ds(j * C, C)]

        def piece(s):
            return gs.at[pl.ds(pl.multiple_of(s * n, 64), n), :]

        return Reduce(
            1 + l, piece, lambda p: recv_s.at[p], recv, lambda j: recv(2, j), n, C, SUB_S, gs_out.at[l]
        )

    def make_tall(kind, held, l, recv_a, recv, final, sub, out):
        def rows_of(j):
            return (j * (T // sub), T // sub)

        return Reduce(
            kind,
            lambda s: held.at[tall(s), :],
            recv_a,
            lambda index, j: recv(index, rows_of(j)),
            lambda j: final(rows_of(j)),
            T, C, sub, out.at[l],
        )

    def shared_a(p):
        return block(entry.at[2], p, (0, T))

    def recv_a_reduce1(p):
        return act.at[1, p // 2, pl.ds((p % 2) * T, T), :]

    def recv_expand1(index, n):
        return block(entry.at[2], 4 + index, n) if index < 3 else recv_e.at[index - 3, pl.ds(*n), :]

    def recv_expand0(index, n):
        return block(entry.at[2], 4 + index, n) if index < 3 else zb.at[1, pl.ds((index - 3) * T + n[0], n[1]), :]

    def recv_reduce1(index, n):
        if index < 2:
            return slc.at[pl.ds(index * T + n[0], n[1]), pl.ds(3 * C, C)]
        return block(entry.at[2], 7, n) if index == 2 else recv_r.at[index - 3, pl.ds(*n), :]

    def recv_reduce0(index, n):
        return block(zc, index, n)

    table = {"H": make_heads(), "S1": make_spatial(1), "S0": make_spatial(0)}
    table["E1"] = make_tall(4, ger, 1, shared_a, recv_expand1, lambda n: recv_e.at[2, pl.ds(*n), :], SUB_E, ge_out)
    table["E0"] = make_tall(3, ger, 0, shared_a, recv_expand0, lambda n: slb.at[1, pl.ds(*n), :], SUB_E, ge_out)
    table["R1"] = make_tall(5, wr, 1, recv_a_reduce1, recv_reduce1, lambda n: recv_reduce1(2, n), SUB_R, gr_out)
    table["R0"] = make_tall(6, we, 0, shared_a, recv_reduce0, lambda n: recv_reduce0(2, n), SUB_R, gr_out)

    def input_grad(q):
        lanes = slice(q * Q, (q + 1) * Q)
        for m in range(2):
            taps_f[0, span(m), 0:Q] = dot(dred[span(m), :], wr[lanes, :], NT)

        def body(i):
            at = pl.ds(pl.multiple_of(i * CH, CH), CH)
            dexp[at, lanes] = (taps_f[0, at, 0:Q] + wide_f[at, lanes]).astype(BF16)

        loop(M // CH, body)

    def point(name):
        for event in AGENDA.get(name, ()):
            item, step = event.split("_")
            if item == "D":
                input_grad(int(step))
                continue
            reduce, index = table[item], step[1:]
            if step == "a":
                reduce.a()
            elif index:
                getattr(reduce, step[0])(int(index))
            else:
                for j in range(reduce.sub):
                    getattr(reduce, step)(j)

    spill_zc = pltpu.make_async_copy(zc, zc_far, out_sem.at[2])
    spill_slc = pltpu.make_async_copy(slc, slc_far, out_sem.at[3])
    back_zc = pltpu.make_async_copy(zc_far, zc, out_sem.at[2])
    back_slc = pltpu.make_async_copy(slc_far, slc, out_sem.at[3])
    ggm_ref[...] = jnp.zeros_like(ggm_ref)
    gsm_ref[...] = jnp.zeros_like(gsm_ref)
    ggo_ref[...] = jnp.zeros_like(ggo_ref)
    gso_ref[...] = jnp.zeros_like(gso_ref)
    load_act.wait()

    for l in range(2):
        load_wr(l).wait()

        def reduce_in(m):
            mid_f[span(m), :] = dot(entry[l, span(m), :], wr[...])
            if l == 0:
                pl.when(m == 0)(lambda: pl.semaphore_wait(barrier, wide + batch - 2))
            mid_stats(0, m)

        loop(2, reduce_in)
        if l == 0:
            load_wr(1).start()
            load_cot.wait()
            load_wh.wait()
            load_thr.wait()
            cot_t[...] = cot[...].T
        heads(4 * l)
        loop(2, lambda m: sum_middle(0, m, FWD))
        heads(4 * l + 1)
        load_ws(l).wait()

        def conv_own(m):
            def store(at, value):
                act[l, 1, at, :] = value

            mid_forward(0, l, 0, m, za, sla, store, gia)
            halo_start([act.at[l, r] for r in range(3)], m)
            for c in range(3):
                taps_f[c, span(m), :] = dot(act[l, 1, span(m), :], ws[(3 + c) * C : (4 + c) * C, :])

        loop(2, conv_own)

        def conv_rest(m):
            halo_wait([act.at[l, r] for r in range(3)], m)
            for c in range(3):
                taps_f[c, span(m), :] += dot(act[l, 0, span(m), :], ws[c * C : (c + 1) * C, :]) + dot(
                    act[l, 2, span(m), :], ws[(6 + c) * C : (7 + c) * C, :]
                )

            def body(i):
                at = chunk(m, i)
                mid_f[at, :] = taps_f[1, at, :] + shifted(taps_f[0, at, :], 1) + shifted(taps_f[2, at, :], -1)

            loop(rows // CH, body)
            mid_stats(1, m)

        loop(2, conv_rest)
        if l == 0:
            load_ws(1).start()
        heads(4 * l + 2)
        loop(2, lambda m: sum_middle(1, m, FWD))
        heads(4 * l + 3)
        load_we(l).wait()

        def expand(m):
            def store(at, value):
                actb[l, at, :] = value

            mid_forward(1, l, 1, m, zb, slb, store, gib)
            for q in range(4):
                lanes = slice(q * Q, (q + 1) * Q)
                wide_f[span(m), lanes] = dot(actb[l, span(m), :], we[lanes, :], NT)

                def body(i, c):
                    z = wide_f[chunk(m, i), lanes]
                    zw = z * along(valid_ref[chunk(m, i), :], Q)
                    return c[0] + fold8(zw), c[1] + fold8(zw * z)

                first, second = lax.fori_loop(0, rows // CH, body, (zero(Q), zero(Q)))
                pack(2, m, 0, q * Q, Q, first)
                pack(2, m, 1, q * Q, Q, second)
            sum_start(2, m, Q)

        loop(2, expand)
        if l == 0:
            load_we(1).start()
        loop(2, lambda m: sum_middle(2, m, Q))

        def output(m):
            total = sum_end(2, m, Q)
            rn = along(count[m, 0:1, :], Q)
            for q in range(4):
                lanes = slice(q * Q, (q + 1) * Q)
                mean = total[q : q + 1] * rn
                inv = lax.rsqrt(total[4 + q : 5 + q] * rn - mean * mean + EPS)
                gain = go_ref[l : l + 1, lanes]
                shift = so_ref[l : l + 1, lanes]
                gic[l, m, 0:1, lanes] = gain * inv

                def body(i, c):
                    at = chunk(m, i)
                    v = along(valid_ref[at, :], Q)
                    zhat = (wide_f[at, lanes] - mean) * inv
                    kept = pl.ds(pl.multiple_of(q * M + m * rows + i * CH, CH), CH)
                    below = entry[l, at, lanes].astype(F32)
                    if l == 1:
                        below = below + ger[kept, :].astype(F32)
                    before = gain * zhat + shift + below
                    s = sigmoid(before)
                    value = before * s * v
                    slope = s * (1.0 + before * (1.0 - s)) * v
                    zc[at, lanes] = zhat.astype(BF16)
                    slc[at, lanes] = slope.astype(BF16)
                    low = value.astype(BF16)
                    entry[l + 1, at, lanes] = low
                    if l == 0:
                        ger[kept, :] = (value - low.astype(F32)).astype(BF16)
                        return c
                    d = thr[at, lanes].astype(F32) * slope
                    wide_f[at, lanes] = d
                    return c[0] + fold8(d), c[1] + fold8(d * zhat)

                if l == 0:
                    lax.fori_loop(0, rows // CH, body, 0)
                else:
                    first, second = lax.fori_loop(0, rows // CH, body, (zero(Q), zero(Q)))
                    pack(0, m, 0, q * Q, Q, first)
                    pack(0, m, 1, q * Q, Q, second)
            if l == 1:
                sum_start(0, m, Q)

        if l == 1:
            spill_zc.wait()
            spill_slc.wait()
        loop(2, output)
        if l == 0:
            spill_zc.start()
            spill_slc.start()

    store_y = pltpu.make_async_copy(entry.at[2], y_out, out_sem.at[0])
    store_y.start()
    back_slc.start()
    grad_heads(False)
    loop(2, lambda m: sum_middle(0, m, Q))
    table["H"].a()
    grad_heads(True)
    store_y.wait()
    point("1_h")

    for l in (1, 0):
        if l == 0:
            load_we(0).wait()

        def back_out(m):
            total = sum_end(0, m, Q)
            rn = along(count[m, 0:1, :], Q)
            for q in range(4):
                lanes = slice(q * Q, (q + 1) * Q)
                sd, sz = total[q : q + 1], total[4 + q : 5 + q]
                gso_ref[l : l + 1, lanes] += sd
                ggo_ref[l : l + 1, lanes] += sz
                sd, sz = sd * rn, sz * rn
                gi = gic[l, m, 0:1, lanes]

                def body(i):
                    at = chunk(m, i)
                    v = along(valid_ref[at, :], Q)
                    zhat = zc[at, lanes].astype(F32)
                    dexp[at, lanes] = (v * gi * (wide_f[at, lanes] - (sd + zhat * sz))).astype(BF16)

                loop(rows // CH, body)
            mid_f[span(m), :] = dot(dexp[span(m), :], we[...])
            mid_back_sums(1, l, m, zb, slb)

        loop(2, back_out)
        if l == 1:
            load_we(0).start()
            back_zc.start()
        point(f"{l}_0")
        grad_tall(ger, dexp, actb[l], False)
        loop(2, lambda m: sum_middle(1, m, W4))
        point(f"{l}_0b")
        table[f"E{l}"].a()
        grad_tall(ger, dexp, actb[l], True)
        point(f"{l}_1")
        if l == 0:
            load_ws(0).wait()

        grad_rows = [dcv.at[0], dcs.at[:, pl.ds(C, C)], dcv.at[1]]

        def back_conv(m):
            def store(at, value):
                low = value.astype(BF16)
                dcs[at, C : 2 * C] = low
                dcs[at, 0:C] = shifted(value, -1).astype(BF16)
                dcs[at, 2 * C : 3 * C] = shifted(value, 1).astype(BF16)

            mid_back(1, l, 1, m, zb, gib, store)
            halo_start(grad_rows, m)
            for c in range(3):
                taps_f[c, span(m), :] = dot(dcs[span(m), C : 2 * C], ws[(3 + c) * C : (4 + c) * C, :], NT)

        loop(2, back_conv)
        point(f"{l}_2")
        grad_spatial(l, 1)
        point(f"{l}_2b")

        def back_rest(m):
            halo_wait(grad_rows, m)
            for c in range(3):
                taps_f[c, span(m), :] += dot(dcv[0, span(m), :], ws[(6 + c) * C : (7 + c) * C, :], NT) + dot(
                    dcv[1, span(m), :], ws[c * C : (c + 1) * C, :], NT
                )

            def body(i):
                at = chunk(m, i)
                mid_f[at, :] = taps_f[1, at, :] + shifted(taps_f[0, at, :], -1) + shifted(taps_f[2, at, :], 1)

            loop(rows // CH, body)
            mid_back_sums(2, l, m, za, sla)

        loop(2, back_rest)
        if l == 1:
            load_ws(0).start()
        point(f"{l}_3")
        grad_spatial(l, 0)
        if l == 0:
            grad_spatial(l, 2)
            table["S0"].a()
        loop(2, lambda m: sum_middle(2, m, W4))
        point(f"{l}_3b")
        if l == 0:
            load_wr(0).start()
        if l == 1:
            grad_spatial(l, 2)
            table["S1"].a()
        point(f"{l}_4")
        if l == 0:
            load_wr(0).wait()

        if l == 1:
            back_zc.wait()
            back_slc.wait()

        def back_in(m):
            def store(at, value):
                dred[at, :] = value.astype(BF16)

            mid_back(2, l, 0, m, za, gia, store)
            for q in range(4 if l == 1 else 0):
                lanes = slice(q * Q, (q + 1) * Q)
                taps_f[0, span(m), 0:Q] = dot(dred[span(m), :], wr[lanes, :], NT)

                def body(i, c):
                    at = chunk(m, i)
                    d = (taps_f[0, at, 0:Q] + wide_f[at, lanes]) * slc[at, lanes].astype(F32)
                    wide_f[at, lanes] = d
                    return c[0] + fold8(d), c[1] + fold8(d * zc[at, lanes].astype(F32))

                first, second = lax.fori_loop(0, rows // CH, body, (zero(Q), zero(Q)))
                pack(0, m, 0, q * Q, Q, first)
                pack(0, m, 1, q * Q, Q, second)
            if l == 1:
                sum_start(0, m, Q)

        loop(2, back_in)
        if l == 1:
            point("1_5")
            grad_tall(wr, entry.at[1], dred[...], False)
            loop(2, lambda m: sum_middle(0, m, Q))
            point("1_5b")
            table["R1"].a()
            grad_tall(wr, entry.at[1], dred[...], True)
            point("1_6")
        else:
            grad_tall(we, entry.at[0], dred[...], False)
            table["R0"].a()
            grad_tall(we, entry.at[0], dred[...], True)
            point("0_5")

    store_dx = pltpu.make_async_copy(dexp, dx_out, out_sem.at[1])
    store_dx.start()
    store_dx.wait()
    for copy in emitted:
        copy.wait()


def run_block(act, thr, cot, valid, w_reduce, w_spatial, w_expand, w_heads, gm, sm, go, so):
    wide, batch = lax.axis_size("wide"), lax.axis_size("batch")
    M, D = act.shape
    C = w_reduce.shape[2]
    H = w_heads.shape[0]
    rows = M // 2
    Q = D // 4
    hbm = pl.BlockSpec(memory_space=pl.ANY)
    vmem = pl.BlockSpec(memory_space=pltpu.VMEM)
    V, DMA = pltpu.VMEM, pltpu.SemaphoreType.DMA
    scratch = [
        V((D, C), BF16), V((9 * C, C), BF16), V((D, C), BF16), V((D // HB, H, HB), BF16),
        V((3, M, D), BF16), V((M, D), F32), V((M, D), BF16),
        V((M, H), BF16), V((H, M), BF16),
        V((2, 3, M, C), BF16), V((2, M, C), BF16), V((2, M, C), BF16),
        V((2, M, C), BF16), V((2, M, C), BF16), V((2, M, C), BF16),
        V((M, D), BF16), V((M, D), BF16),
        V((M, C), F32), V((3, M, C), F32),
        V((2, M, C), BF16), V((M, 3 * C), BF16), V((M, C), BF16),
        V((2, 2, 8, C), F32), V((2, 2, 8, C), F32), V((2, 2, 8, D), F32), V((2, 8, 128), F32),
        V((3, 2, 8, Q), F32), V((3, 2, 8, Q), F32),
        V((3, 2, wide, 8, Q), F32), V((3, 2, batch, 8, Q), F32),
        V((D, C), BF16), V((9 * C, C), BF16),
        V((5, H, HB), BF16), V((9, 9 * C // wide, C), BF16), V((3, 256, C), BF16), V((2, 256, C), BF16),
        DMA((7,)), DMA((3, 2, wide)), DMA((3, 2, wide)), DMA((3, 2, batch)), DMA((3, 2, batch)),
        DMA((2, 2)), DMA((2, 2)), DMA((4,)), DMA((7, SUBS, 10)), DMA((7, SUBS, 10)), DMA((7, SUBS)),
    ]
    shape = jax.ShapeDtypeStruct
    return pl.pallas_call(
        functools.partial(block_kernel, (wide, batch, rows, D, C, H)),
        out_shape=[
            shape((M, D), BF16), shape((M, D), BF16),
            shape((2, D // wide, C), BF16), shape((2, 9 * C // wide, C), BF16), shape((2, D // wide, C), BF16), shape((H, D // wide), BF16),
            shape((2, 2, C), F32), shape((2, 2, C), F32), shape((2, D), F32), shape((2, D), F32),
            shape((M, D), BF16), shape((M, D), BF16),
        ],
        in_specs=[hbm, hbm, hbm, vmem, hbm, hbm, hbm, hbm, vmem, vmem, vmem, vmem],
        out_specs=[hbm] * 6 + [vmem] * 4 + [hbm] * 2,
        scratch_shapes=scratch,
        compiler_params=pltpu.CompilerParams(
            collective_id=7, has_side_effects=True, vmem_limit_bytes=VMEM_BYTES
        ),
    )(act, thr, cot, valid, w_reduce, w_spatial, w_expand, w_heads, gm, sm, go, so)


def finish_kernel(n, *refs):
    ins, outs, held, wide, sems, out_sems = refs[:n], refs[n : 2 * n], refs[2 * n : 3 * n], refs[3 * n : -2], refs[-2], refs[-1]
    loads = [pltpu.make_async_copy(ins[i], held[i], sems.at[i]) for i in range(n)]
    for copy in loads:
        copy.start()
    stores = []
    w = 0
    for i in range(n):
        loads[i].wait()
        src = held[i]
        if ins[i].dtype != outs[i].dtype:
            src = wide[w]
            w += 1
            rows = 64
            if len(src.shape) == 2:
                def body(r, src=src, i=i):
                    at = pl.ds(pl.multiple_of(r * rows, rows), rows)
                    src[at, :] = held[i][at, :].astype(F32)

                loop(src.shape[0] // rows, body)
            else:
                for l in range(src.shape[0]):
                    def body(r, src=src, i=i, l=l):
                        at = pl.ds(pl.multiple_of(r * rows, rows), rows)
                        src[l, at, :] = held[i][l, at, :].astype(F32)

                    loop(src.shape[1] // rows, body)
        stores.append(pltpu.make_async_copy(src, outs[i], out_sems.at[i]))
        stores[-1].start()
    for copy in stores:
        copy.wait()


def finish(*arrays):
    hbm = pl.BlockSpec(memory_space=pl.ANY)
    n = len(arrays)
    widened = [a.dtype == BF16 and 2 <= i < 6 for i, a in enumerate(arrays)]
    out = [jax.ShapeDtypeStruct(a.shape, F32 if w else a.dtype) for a, w in zip(arrays, widened)]
    scratch = [pltpu.VMEM(a.shape, a.dtype) for a in arrays]
    scratch += [pltpu.VMEM(a.shape, F32) for a, w in zip(arrays, widened) if w]
    return pl.pallas_call(
        functools.partial(finish_kernel, n),
        out_shape=out,
        in_specs=[hbm] * n,
        out_specs=[hbm] * n,
        scratch_shapes=scratch + [pltpu.SemaphoreType.DMA((n,)), pltpu.SemaphoreType.DMA((n,))],
        compiler_params=pltpu.CompilerParams(vmem_limit_bytes=VMEM_BYTES),
    )(*arrays)


def shards_rows(
    activations, bucket_ids, thresholds, head_cot, w_reduce, w_spatial, w_expand,
    gain_mid, shift_mid, gain_out, shift_out, w_heads,
):
    micro, images, pixels, D = activations.shape
    M = micro * images * pixels
    L, _, C = w_reduce.shape
    H = head_cot.shape[-1]
    wide = lax.axis_size("wide")
    positions = lax.axis_index("wide") * pixels + jnp.arange(pixels, dtype=jnp.int32)
    valid = jnp.broadcast_to(frame_mask(bucket_ids, positions).reshape(M, 1), (M, 128))
    y, dx, gr, gs, ge, gh, ggm, gsm, ggo, gso, _, _ = run_block(
        activations.reshape(M, D), thresholds.reshape(M, D), head_cot.reshape(M, H), valid,
        w_reduce, w_spatial, w_expand, w_heads,
        gain_mid, shift_mid, gain_out, shift_out,
    )
    y, dx, gr, gs, ge, gh, ggm, gsm, ggo, gso = finish(y, dx, gr, gs, ge, gh, ggm, gsm, ggo, gso)

    return (
        y.reshape(activations.shape),
        dx.reshape(activations.shape),
        gr,
        gs,
        ge,
        ggm,
        gsm,
        ggo,
        gso,
        gh,
    )


def solution(mesh):
    placed = (
        P(None, "batch", "wide", None),
        P(None, "batch"),
        P(None, "batch", "wide", None),
        P(None, "batch", "wide", None),
        P(),
        P(),
        P(),
        P(),
        P(),
        P(),
        P(),
        P(),
    )
    def split(*arrays):
        micro, images, pixels, features = arrays[0].shape
        whole_rows = pixels == FRAME and FRAME == lax.axis_size("wide") and lax.axis_size("batch") == 4
        fits = micro == 2 and images * pixels == 256 and features == 2048 and arrays[4].shape[2] == 512
        return (shards_rows if whole_rows and fits else shards)(*arrays)

    return jax.shard_map(
        split,
        mesh=mesh,
        in_specs=placed,
        out_specs=(
            P(None, "batch", "wide", None),
            P(None, "batch", "wide", None),
            P(None, "wide", None),
            P(None, "wide", None),
            P(None, "wide", None),
            P(),
            P(),
            P(),
            P(),
            P(None, "wide"),
        ),
        check_vma=False,
    )
```

```python
import functools

import jax
import jax.numpy as jnp
from jax import lax
from jax.experimental import pallas as pl
from jax.experimental.pallas import tpu as pltpu
from jax.sharding import PartitionSpec as P

HEAD = 256
TASKS = 3
FRAME = 8


EPS = 1e-05
SHARP = 8.0
FLOOR = 0.25
ROW_TABLE = (8, 8, 7, 6, 8, 5, 7, 8)
COL_TABLE = (8, 7, 8, 8, 6, 8, 7, 5)


def silu_slope(values):
    gate_val = jax.nn.sigmoid(values)
    return gate_val * (1.0 + values * (1.0 - gate_val))


def frame_mask(buckets, positions):
    bucket_kinds = jnp.arange(len(ROW_TABLE), dtype=jnp.int32)
    onehot = (buckets[..., None] == bucket_kinds).astype(jnp.int32)
    heights = jnp.sum(onehot * jnp.array(ROW_TABLE, dtype=jnp.int32), -1)
    widths = jnp.sum(onehot * jnp.array(COL_TABLE, dtype=jnp.int32), -1)
    rowpos = positions // FRAME
    colpos = positions % FRAME
    inside = (rowpos < heights[..., None]) & (colpos < widths[..., None])
    return inside.astype(jnp.float32)


def unfold_taps(images):
    padded = jnp.pad(images, ((0, 0), (1, 1), (1, 1), (0, 0)))
    pieces = [
        padded[:, row_off : row_off + FRAME, col_off : col_off + FRAME, :]
        for row_off in range(3)
        for col_off in range(3)
    ]
    return jnp.concatenate(pieces, -1)


def fold_taps(columns, channels):
    total_sum = jnp.zeros(columns.shape[:-1] + (channels,), columns.dtype)
    for tap_index in range(9):
        row_off, col_off = divmod(tap_index, 3)
        tap_part = columns[..., tap_index * channels : (tap_index + 1) * channels]
        padded = jnp.pad(tap_part, ((0, 0), (1, 1), (1, 1), (0, 0)))
        total_sum = (
            total_sum
            + padded[:, 2 - row_off : 2 - row_off + FRAME, 2 - col_off : 2 - col_off + FRAME, :]
        )
    return total_sum


def sum_kernel(wide, batch, x_ref, o_ref, near, far, part, near_send, near_recv, far_send, far_recv):
    my_w = lax.axis_index("wide")
    my_b = lax.axis_index("batch")
    barrier = pltpu.get_barrier_semaphore()
    for step in range(1, wide):
        pl.semaphore_signal(
            barrier, inc=1, device_id=(my_b, lax.rem(my_w + step, wide)), device_id_type=pl.DeviceIdType.MESH
        )
    for step in range(1, batch):
        pl.semaphore_signal(
            barrier, inc=1, device_id=(lax.rem(my_b + step, batch), my_w), device_id_type=pl.DeviceIdType.MESH
        )
    pl.semaphore_wait(barrier, wide + batch - 2)

    def exchange(src, slots, send, recv, count, me, target):
        copies = []
        for step in range(1, count):
            copy = pltpu.make_async_remote_copy(
                src_ref=src,
                dst_ref=slots.at[me],
                send_sem=send.at[step],
                recv_sem=recv.at[step],
                device_id=target(lax.rem(me + step, count)),
                device_id_type=pl.DeviceIdType.MESH,
            )
            copy.start()
            copies.append(copy)
        slots[me] = src[...]
        for copy in copies:
            copy.wait()
        total = slots[0]
        for index in range(1, count):
            total = total + slots[index]
        return total

    part[...] = exchange(x_ref, near, near_send, near_recv, wide, my_w, lambda w: (my_b, w))
    o_ref[...] = exchange(part, far, far_send, far_recv, batch, my_b, lambda b: (b, my_w))


def sum_all(values):
    wide, batch = lax.axis_size("wide"), lax.axis_size("batch")
    block = values.shape
    return pl.pallas_call(
        functools.partial(sum_kernel, wide, batch),
        out_shape=jax.ShapeDtypeStruct(block, jnp.float32),
        in_specs=[pl.BlockSpec(memory_space=pltpu.VMEM)],
        out_specs=pl.BlockSpec(memory_space=pltpu.VMEM),
        scratch_shapes=[
            pltpu.VMEM((wide,) + block, jnp.float32),
            pltpu.VMEM((batch,) + block, jnp.float32),
            pltpu.VMEM(block, jnp.float32),
            pltpu.SemaphoreType.DMA((wide,)),
            pltpu.SemaphoreType.DMA((wide,)),
            pltpu.SemaphoreType.DMA((batch,)),
            pltpu.SemaphoreType.DMA((batch,)),
        ],
        compiler_params=pltpu.CompilerParams(collective_id=block[-1] // 512, has_side_effects=True),
    )(values)


def batch_norm(values, valid_rows, scale_vec, offset_vec):
    weighted = values * valid_rows[..., None]
    sum_first = jnp.sum(weighted, 1)
    sum_second = jnp.sum(weighted * values, 1)
    counts = jnp.sum(valid_rows, 1)
    count_row = jnp.broadcast_to(counts[:, None], sum_first.shape)
    summed = sum_all(jnp.concatenate([sum_first, sum_second, count_row, jnp.zeros_like(sum_first)], 0))
    sum_first, sum_second, counts = summed[0:2], summed[2:4], summed[4:6, 0]
    mean_val = sum_first / counts[:, None]
    spread = sum_second / counts[:, None] - mean_val * mean_val
    inv_std = lax.rsqrt(spread + EPS)
    normed = (values - mean_val[:, None, :]) * inv_std[:, None, :]
    return (normed, scale_vec * normed + offset_vec, inv_std, counts)


def norm_back(grad_out, normed, inv_std, counts, valid_rows, scale_vec):
    sum_grad = jnp.sum(grad_out, 1)
    sum_prod = jnp.sum(grad_out * normed, 1)
    summed = sum_all(jnp.concatenate([sum_grad, sum_prod, sum_grad, sum_prod], 0))
    sum_grad, sum_prod = summed[0:2], summed[2:4]
    centered = (
        grad_out - (sum_grad[:, None, :] + normed * sum_prod[:, None, :]) / counts[:, None, None]
    )
    grad_in = valid_rows[..., None] * scale_vec * inv_std[:, None, :] * centered
    return (grad_in, jnp.sum(sum_prod, 0), jnp.sum(sum_grad, 0))


def forward_layer(layer_in, pix_valid, img_valid, params, layout):
    w_in, w_mid, w_out, scale_a, offset_a, scale_b, offset_b, scale_c, offset_c = params
    groups, per_lane, local_imgs = layout
    span_len = layer_in.shape[0]
    channels = w_in.shape[1]
    entry_low = layer_in.astype(jnp.bfloat16)
    reduced = jnp.einsum("mrd,dc->mrc", entry_low, w_in, preferred_element_type=jnp.float32)
    normed_a, bn_a, inv_a, counts = batch_norm(reduced, pix_valid, scale_a, offset_a)
    act_a = (jax.nn.silu(bn_a) * pix_valid[..., None]).astype(jnp.bfloat16)
    arrived = lax.all_to_all(
        act_a.reshape(span_len, groups, per_lane, channels),
        "wide",
        split_axis=1,
        concat_axis=2,
        tiled=True,
    )
    count_imgs = arrived.shape[1]
    images = arrived.reshape(span_len * count_imgs, FRAME, FRAME, channels)
    columns = unfold_taps(images).reshape(span_len, count_imgs, FRAME * FRAME, 9 * channels)
    conv_out = jnp.einsum("mkpc,co->mkpo", columns, w_mid, preferred_element_type=jnp.float32)
    taps_saved, conv_out = (columns, conv_out)
    taps_saved = taps_saved.reshape(span_len, -1, taps_saved.shape[-1])
    conv_out = conv_out.reshape(span_len, -1, channels)
    normed_b, bn_b, inv_b, unused_counts = batch_norm(conv_out, img_valid, scale_b, offset_b)
    act_b = (jax.nn.silu(bn_b) * img_valid[..., None]).astype(jnp.bfloat16)
    returned = lax.all_to_all(
        act_b.reshape(span_len, local_imgs, FRAME * FRAME, channels),
        "wide",
        split_axis=2,
        concat_axis=1,
        tiled=True,
    ).reshape(span_len, -1, channels)
    expanded = jnp.einsum("mrc,oc->mro", returned, w_out, preferred_element_type=jnp.float32)
    normed_c, bn_c, inv_c, unused_again = batch_norm(expanded, pix_valid, scale_c, offset_c)
    before = bn_c + layer_in
    result = jax.nn.silu(before) * pix_valid[..., None]
    saved = (
        entry_low,
        normed_a,
        bn_a,
        inv_a,
        taps_saved,
        normed_b,
        bn_b,
        inv_b,
        returned,
        normed_c,
        before,
        inv_c,
        counts,
    )
    return (result, saved)


def backward_layer(incoming, saved, pix_valid, img_valid, params, layout):
    w_in, w_mid, w_out, scale_a, offset_a, scale_b, offset_b, scale_c, offset_c = params
    groups, per_lane, local_imgs = layout
    (
        entry_low,
        normed_a,
        bn_a,
        inv_a,
        taps_saved,
        normed_b,
        bn_b,
        inv_b,
        returned,
        normed_c,
        before,
        inv_c,
        counts,
    ) = saved
    span_len = incoming.shape[0]
    channels = w_in.shape[1]
    grad_pre = incoming * pix_valid[..., None] * silu_slope(before)
    grad_c, scale_gc, offset_gc = norm_back(grad_pre, normed_c, inv_c, counts, pix_valid, scale_c)
    grad_c_low = grad_c.astype(jnp.bfloat16)
    g_out = jnp.einsum("mro,mrc->oc", grad_c_low, returned, preferred_element_type=jnp.float32)
    d_returned = jnp.einsum(
        "mro,oc->mrc", grad_c_low, w_out, preferred_element_type=jnp.float32
    ).astype(jnp.bfloat16)
    d_images = lax.all_to_all(
        d_returned.reshape(span_len, groups, per_lane, channels),
        "wide",
        split_axis=1,
        concat_axis=2,
        tiled=True,
    ).reshape(span_len, -1, channels)
    d_bn_b = d_images.astype(jnp.float32) * img_valid[..., None] * silu_slope(bn_b)
    grad_b, scale_gb, offset_gb = norm_back(d_bn_b, normed_b, inv_b, counts, img_valid, scale_b)
    grad_b_low = grad_b.astype(jnp.bfloat16)
    g_mid = jnp.einsum("mrk,mro->ko", taps_saved, grad_b_low, preferred_element_type=jnp.float32)
    d_columns = jnp.einsum("mro,ko->mrk", grad_b_low, w_mid, preferred_element_type=jnp.float32)
    d_act = fold_taps(
        d_columns.reshape(span_len * local_imgs, FRAME, FRAME, 9 * channels), channels
    )
    d_act = d_act.astype(jnp.bfloat16).reshape(span_len, local_imgs, FRAME * FRAME, channels)
    d_pixels = lax.all_to_all(d_act, "wide", split_axis=2, concat_axis=1, tiled=True).reshape(
        span_len, -1, channels
    )
    d_bn_a = d_pixels.astype(jnp.float32) * pix_valid[..., None] * silu_slope(bn_a)
    grad_a, scale_ga, offset_ga = norm_back(d_bn_a, normed_a, inv_a, counts, pix_valid, scale_a)
    grad_a_low = grad_a.astype(jnp.bfloat16)
    g_in = jnp.einsum("mrd,mrc->dc", entry_low, grad_a_low, preferred_element_type=jnp.float32)
    d_entry = jnp.einsum("mrc,dc->mrd", grad_a_low, w_in, preferred_element_type=jnp.float32)
    return (
        d_entry + grad_pre,
        (g_in, g_mid, g_out),
        (scale_ga, offset_ga, scale_gb, offset_gb, scale_gc, offset_gc),
    )


def grad_drop(task_values, limits):
    task_total = task_values[0]
    magnitude = jnp.abs(task_values[0])
    for task_index in range(1, len(task_values)):
        task_total = task_total + task_values[task_index]
        magnitude = magnitude + jnp.abs(task_values[task_index])
    keep_ratio = 0.5 * (1.0 + task_total / jnp.maximum(magnitude, FLOOR))
    upward = jax.nn.sigmoid(SHARP * (keep_ratio - limits))
    downward = jax.nn.sigmoid(SHARP * (limits - keep_ratio))
    merged = jnp.zeros_like(task_total)
    for task_value in task_values:
        merged = merged + jnp.where(task_value > 0, upward, downward) * task_value
    return merged


def add_tuples(left, right):
    return tuple((left_item + right_item for left_item, right_item in zip(left, right)))


def shards(
    activations,
    bucket_ids,
    thresholds,
    head_cot,
    w_reduce,
    w_spatial,
    w_expand,
    gain_mid,
    shift_mid,
    gain_out,
    shift_out,
    w_heads,
):
    micro_total, groups, per_lane, features = activations.shape
    lane_count = lax.axis_size("wide")
    local_imgs = groups // lane_count
    lane_index = lax.axis_index("wide")
    layout = (groups, per_lane, local_imgs)
    pix_positions = lane_index * per_lane + jnp.arange(per_lane, dtype=jnp.int32)
    pix_valid_all = frame_mask(bucket_ids, pix_positions).reshape(micro_total, -1)
    own_ids = lax.dynamic_slice_in_dim(bucket_ids, lane_index * local_imgs, local_imgs, 1)
    img_valid_all = frame_mask(own_ids, jnp.arange(FRAME * FRAME, dtype=jnp.int32)).reshape(
        micro_total, -1
    )
    layer_total = w_reduce.shape[0]
    head_width = head_cot.shape[-1]
    layer_params = [
        (
            w_reduce[layer_index],
            w_spatial[layer_index],
            w_expand[layer_index],
            gain_mid[layer_index, 0],
            shift_mid[layer_index, 0],
            gain_mid[layer_index, 1],
            shift_mid[layer_index, 1],
            gain_out[layer_index],
            shift_out[layer_index],
        )
        for layer_index in range(layer_total)
    ]
    spans = [(0, micro_total)]
    weight_acc = [None] * layer_total
    norm_acc = [None] * layer_total
    heads_acc = jnp.zeros((features, head_width), jnp.float32)
    outs_y = []
    outs_dx = []
    for span_at, span_len in spans:

        def take_span(array):
            return lax.slice_in_dim(array, span_at, span_at + span_len, axis=0)

        pix_valid = take_span(pix_valid_all)
        img_valid = take_span(img_valid_all)
        carried = take_span(activations).reshape(span_len, -1, features).astype(jnp.float32)
        saved_layers = []
        for layer_index in range(layer_total):
            carried, saved = forward_layer(
                carried, pix_valid, img_valid, layer_params[layer_index], layout
            )
            saved_layers.append(saved)
        result_low = carried.astype(jnp.bfloat16)
        outs_y.append(result_low.reshape(span_len, groups, per_lane, features))
        head_grads = take_span(head_cot).reshape(span_len, -1, head_width)
        heads_acc = heads_acc + jnp.einsum(
            "mrd,mrh->dh", result_low, head_grads, preferred_element_type=jnp.float32
        )
        task_values = [
            jnp.einsum(
                "mrh,hd->mrd",
                head_grads[..., task_index * HEAD : (task_index + 1) * HEAD],
                w_heads[task_index * HEAD : (task_index + 1) * HEAD],
                preferred_element_type=jnp.float32,
            )
            for task_index in range(TASKS)
        ]
        limits = take_span(thresholds).reshape(span_len, -1, features).astype(jnp.float32)
        incoming = grad_drop(task_values, limits)
        for layer_index in reversed(range(layer_total)):
            incoming, weight_parts, norm_parts = backward_layer(
                incoming,
                saved_layers[layer_index],
                pix_valid,
                img_valid,
                layer_params[layer_index],
                layout,
            )
            if weight_acc[layer_index] is None:
                weight_acc[layer_index] = weight_parts
                norm_acc[layer_index] = norm_parts
            else:
                weight_acc[layer_index] = add_tuples(weight_acc[layer_index], weight_parts)
                norm_acc[layer_index] = add_tuples(norm_acc[layer_index], norm_parts)
        outs_dx.append(incoming.astype(jnp.bfloat16).reshape(span_len, groups, per_lane, features))
    stack_in = jnp.stack([layer_acc[0] for layer_acc in weight_acc])
    stack_mid = jnp.stack([layer_acc[1] for layer_acc in weight_acc])
    stack_out = jnp.stack([layer_acc[2] for layer_acc in weight_acc])
    shard_in, shard_mid, shard_out, shard_heads = (
        lax.psum_scatter(
            stack_in.astype(jnp.bfloat16), "wide", scatter_dimension=1, tiled=True
        ).astype(jnp.float32),
        lax.psum_scatter(
            stack_mid.astype(jnp.bfloat16), "wide", scatter_dimension=1, tiled=True
        ).astype(jnp.float32),
        lax.psum_scatter(
            stack_out.astype(jnp.bfloat16), "wide", scatter_dimension=1, tiled=True
        ).astype(jnp.float32),
        lax.psum_scatter(
            heads_acc[None].astype(jnp.bfloat16), "wide", scatter_dimension=1, tiled=True
        ).astype(jnp.float32),
    )
    shard_in, shard_mid, shard_out, shard_heads = (
        lax.psum(shard_in.astype(jnp.bfloat16), "batch").astype(jnp.float32),
        lax.psum(shard_mid.astype(jnp.bfloat16), "batch").astype(jnp.float32),
        lax.psum(shard_out.astype(jnp.bfloat16), "batch").astype(jnp.float32),
        lax.psum(shard_heads.astype(jnp.bfloat16), "batch").astype(jnp.float32),
    )
    g_gain_mid = jnp.stack([jnp.stack([layer_norm[0], layer_norm[2]]) for layer_norm in norm_acc])
    g_shift_mid = jnp.stack([jnp.stack([layer_norm[1], layer_norm[3]]) for layer_norm in norm_acc])
    g_gain_out = jnp.stack([layer_norm[4] for layer_norm in norm_acc])
    g_shift_out = jnp.stack([layer_norm[5] for layer_norm in norm_acc])
    return (
        jnp.concatenate(outs_y, 0),
        jnp.concatenate(outs_dx, 0),
        shard_in,
        shard_mid,
        shard_out,
        g_gain_mid,
        g_shift_mid,
        g_gain_out,
        g_shift_out,
        shard_heads[0].T,
    )


MESH = pl.DeviceIdType.MESH
F32, BF16 = jnp.float32, jnp.bfloat16
NN = (((1,), (0,)), ((), ()))
NT = (((1,), (1,)), ((), ()))
TN = (((0,), (0,)), ((), ()))
CH = 16
HB = 256

VMEM_BYTES = 63 * 1024 * 1024
PIECES = {"H": 4, "S0": 6, "S1": 3, "E0": 2, "E1": 2, "R1": 2, "R0": 4}
AGENDA = {
    101: (110, 111, 120, 121),
    103: (112, 130, 113),
    104: (131, 210),
    105: (211, 140, 220),
    106: (221, 122),
    107: (123,),
    108: (141, 132, 239, 310, 311, 320),
    109: (249, 133, 312, 321),
    110: (250, 142, 330),
    111: (322, 410, 143, 251),
    1: (340, 411, 331, 420, 150),
    2: (151, 152, 153, 341, 332, 260),
    3: (261, 430),
    4: (160, 342, 510, 440, 161),
    5: (511, 359, 421),
    6: (162, 163, 529, 360, 450),
    7: (431, 270, 530, 361, 362, 610, 271, 620, 611, 441, 621, 540, 630, 531, 612, 451, 622, 613, 614, 631, 640),
    8: (623, 615, 632, 469, 541, 170, 379, 624, 550, 650, 625, 641),
    9: (
        642, 633, 551, 560, 651, 634, 710, 720, 635, 660, 643, 711, 644, 712, 561, 570, 721, 652, 713, 722, 645,
        661, 730, 723, 653, 812, 731, 654, 662, 810, 732, 663, 740, 479, 733, 655, 571, 741, 664, 742, 813, 743,
        750, 665, 751, 752, 760, 753, 761, 762, 670, 770, 763, 171, 811, 172, 173, 771, 671, 672, 673, 674, 675,
        772, 773,
    ),
}


def dot(left, right, dims=NN):
    return lax.dot_general(left, right, dims, preferred_element_type=F32)


def along(column, lanes):
    return column if lanes == 128 else jnp.concatenate([column] * (lanes // 128), axis=1)


def sigmoid(v):
    return 0.5 * jnp.tanh(0.5 * v) + 0.5


def fold8(block):
    total = block[0:8]
    for at in range(8, block.shape[0], 8):
        total = total + block[at : at + 8]
    return total


def shifted(block, by):
    rows, lanes = block.shape
    grouped = block.reshape(rows // FRAME, FRAME, lanes)
    pixel = lax.broadcasted_iota(jnp.int32, grouped.shape, 1)
    moved = pltpu.roll(grouped, by % FRAME, 1)
    keep = pixel > 0 if by == 1 else pixel < FRAME - 1
    return jnp.where(keep, moved, 0.0).reshape(rows, lanes)


def loop(n, body, start=0):
    def step(i, c):
        body(i)
        return c

    lax.fori_loop(start, n, step, 0, unroll=4 if n % 4 == 0 and n >= 8 else 1)


def block_kernel(
    dims,
    act_in, thr_in, cot_in, valid_in, wr_in, ws_in, we_in, wh_in, gm_in, sm_in, go_in, so_in,
    y_out, dx_out, gr_out, gs_out, ge_out, gh_out, ggm_out, gsm_out, ggo_out, gso_out, zc_far, slc_far,
    wr, ws, we, wh, entry, wide_f, thr, cot, cot_t, act, za, sla, actb, zb, slb, zc, slc,
    mid_f, taps_f, dcv, dcs, dred, gia, gib, gic, count, pay, part, near, far,
    ger, gs, recv_h, recv_s, recv_e, recv_r, relay,
    gm_ref, sm_ref, go_ref, so_ref, valid_ref, ggm_ref, gsm_ref, ggo_ref, gso_ref,
    load_sem, near_send, near_recv, far_send, far_recv, halo_send, halo_recv, relay_send, relay_recv,
    out_sem, rs_sem,
):
    wide, batch, rows, D, C, H = dims
    my_w = lax.axis_index("wide")
    my_b = lax.axis_index("batch")
    Q = D // 4
    M = 2 * rows
    dexp = thr

    def span(m):
        return pl.ds(pl.multiple_of(m * rows, rows), rows)

    def chunk(m, i):
        return pl.ds(pl.multiple_of(m * rows + i * CH, CH), CH)

    def load(src, dst, index):
        return pltpu.make_async_copy(src, dst, load_sem.at[index])

    def load_wr(l):
        return load(wr_in.at[l], wr, 0)

    def load_ws(l):
        return load(ws_in.at[l], ws, 1)

    def load_we(l):
        return load(we_in.at[l], we, 2)

    load_act = load(act_in, entry.at[0], 3)
    load_wh = load(wh, wh, 4)
    load_thr = load(thr_in, thr, 5)
    load_cot = load(cot_in, cot, 6)
    load_small = [
        load(src, dst, 7 + i)
        for i, (src, dst) in enumerate(
            ((valid_in, valid_ref), (gm_in, gm_ref), (sm_in, sm_ref), (go_in, go_ref), (so_in, so_ref))
        )
    ]
    load_act.start()
    load_wr(0).start()
    for copy in load_small:
        copy.start()
    load_ws(0).start()
    load_we(0).start()
    load_cot.start()
    for j in range(D // HB):
        load(wh_in.at[:, pl.ds(j * HB, HB)], wh.at[j], 4).start()
    load_thr.start()

    for side in (0, 2):
        for l in range(2):
            act[l, side] = jnp.zeros(act.shape[2:], BF16)
        dcv[side // 2] = jnp.zeros(dcv.shape[1:], BF16)

    barrier = pltpu.get_barrier_semaphore()
    for step in range(1, wide):
        pl.semaphore_signal(barrier, inc=1, device_id=(my_b, lax.rem(my_w + step, wide)), device_id_type=MESH)
    for step in range(1, batch):
        pl.semaphore_signal(barrier, inc=1, device_id=(lax.rem(my_b + step, batch), my_w), device_id_type=MESH)

    def near_copy(k, m, step, lanes):
        return pltpu.make_async_remote_copy(
            src_ref=pay.at[k, m, :, pl.ds(0, lanes)],
            dst_ref=near.at[k, m, my_w, :, pl.ds(0, lanes)],
            send_sem=near_send.at[k, m],
            recv_sem=near_recv.at[k, m],
            device_id=(my_b, lax.rem(my_w + step, wide)),
            device_id_type=MESH,
        )

    def far_copy(k, m, step, lanes):
        return pltpu.make_async_remote_copy(
            src_ref=part.at[k, m, :, pl.ds(0, lanes)],
            dst_ref=far.at[k, m, my_b, :, pl.ds(0, lanes)],
            send_sem=far_send.at[k, m],
            recv_sem=far_recv.at[k, m],
            device_id=(lax.rem(my_b + step, batch), my_w),
            device_id_type=MESH,
        )

    def whole_sum(block, *sems):
        for sem in sems:
            pltpu.make_async_copy(block, block, sem).wait()

    def sum_start(k, m, lanes):
        for step in range(1, wide):
            near_copy(k, m, step, lanes).start()
        near[k, m, my_w, :, 0:lanes] = pay[k, m, :, 0:lanes]

    def sum_middle(k, m, lanes):
        whole_sum(near.at[k, m, pl.ds(0, wide - 1), :, pl.ds(0, lanes)], near_send.at[k, m], near_recv.at[k, m])
        total = near[k, m, 0, :, 0:lanes]
        for index in range(1, wide):
            total = total + near[k, m, index, :, 0:lanes]
        part[k, m, :, 0:lanes] = total
        for step in range(1, batch):
            far_copy(k, m, step, lanes).start()
        far[k, m, my_b, :, 0:lanes] = total

    def sum_end(k, m, lanes):
        whole_sum(far.at[k, m, pl.ds(0, batch - 1), :, pl.ds(0, lanes)], far_send.at[k, m], far_recv.at[k, m])
        total = far[k, m, 0, :, 0:lanes]
        for index in range(1, batch):
            total = total + far[k, m, index, :, 0:lanes]
        return total

    def pack(k, m, which, at, width, sums):
        row = jnp.sum(sums, 0, keepdims=True)
        for j in range(row.shape[1] // width):
            index = which * 4 + at // width + j
            pay[k, m, index : index + 1, 0:width] = row[:, j * width : (j + 1) * width]

    def unpack_mid(total, which):
        return jnp.concatenate([total[which * 4 + j : which * 4 + j + 1, 0 : C // 4] for j in range(4)], axis=1)

    W4 = C // 4
    FWD = 2 * W4

    def zero(width):
        return jnp.zeros((8, width), F32)

    def mid_stats(k, m, lanes):
        def body(i, c):
            z = mid_f[chunk(m, i), :]
            v = valid_ref[chunk(m, i), :]
            zw = z * along(v, C)
            return c[0] + fold8(zw), c[1] + fold8(zw * z), c[2] + fold8(v)

        first, second, seen = lax.fori_loop(0, rows // CH, body, (zero(C), zero(C), zero(128)), unroll=4)
        pack(k, m, 0, 0, W4, first)
        pack(k, m, 1, 0, W4, second)
        if lanes == FWD:
            pay[k, m, :, W4:FWD] = jnp.broadcast_to(jnp.sum(seen, 0, keepdims=True), (8, W4))
        sum_start(k, m, lanes)

    def mid_forward(k, l, which, m, lanes, zhat_ref, slope_ref, store, gi_ref):
        total = sum_end(k, m, lanes)
        if lanes == FWD:
            count[m] = jnp.broadcast_to(1.0 / total[0:1, W4:FWD], (8, 128))
        rn = along(count[m, 0:1, :], C)
        mean = unpack_mid(total, 0) * rn
        inv = lax.rsqrt(unpack_mid(total, 1) * rn - mean * mean + EPS)
        gain = gm_ref[l, which : which + 1, :]
        shift = sm_ref[l, which : which + 1, :]
        gi_ref[l, m, 0:1, :] = gain * inv

        def body(i):
            at = chunk(m, i)
            v = along(valid_ref[at, :], C)
            zhat = (mid_f[at, :] - mean) * inv
            value = gain * zhat + shift
            s = sigmoid(value)
            zhat_ref[l, at, :] = zhat.astype(BF16)
            slope_ref[l, at, :] = (s * (1.0 + value * (1.0 - s)) * v).astype(BF16)
            store(at, (value * s * v).astype(BF16))

        loop(rows // CH, body)

    def mid_back_sums(k, l, m, zhat_ref, slope_ref):
        def body(i, c):
            at = chunk(m, i)
            d = mid_f[at, :].astype(BF16).astype(F32) * slope_ref[l, at, :].astype(F32)
            mid_f[at, :] = d
            return c[0] + fold8(d), c[1] + fold8(d * zhat_ref[l, at, :].astype(F32))

        first, second = lax.fori_loop(0, rows // CH, body, (zero(C), zero(C)), unroll=4)
        pack(k, m, 0, 0, W4, first)
        pack(k, m, 1, 0, W4, second)
        sum_start(k, m, W4)

    def mid_back(k, l, which, m, zhat_ref, gi_ref, store):
        total = sum_end(k, m, W4)
        sd, sz = unpack_mid(total, 0), unpack_mid(total, 1)
        gsm_ref[l, which : which + 1, :] += sd
        ggm_ref[l, which : which + 1, :] += sz
        rn = along(count[m, 0:1, :], C)
        sd, sz = sd * rn, sz * rn
        gi = gi_ref[l, m, 0:1, :]

        def body(i):
            at = chunk(m, i)
            v = along(valid_ref[at, :], C)
            zhat = zhat_ref[l, at, :].astype(F32)
            store(at, v * gi * (mid_f[at, :] - (sd + zhat * sz)))

        loop(rows // CH, body)

    low, high = wide // 2 - 1, wide // 2

    def halo(buffers, m, down):
        side = 0 if down else 1
        return pltpu.make_async_remote_copy(
            src_ref=buffers[1].at[span(m), :],
            dst_ref=buffers[0 if down else 2].at[span(m), :],
            send_sem=halo_send.at[m, side],
            recv_sem=halo_recv.at[m, side],
            device_id=(my_b, my_w + 1 if down else my_w - 1),
            device_id_type=MESH,
        )

    def halo_out(buffers, down):
        side = 0 if down else 1
        return pltpu.make_async_remote_copy(
            src_ref=buffers[1].at[span(1), :],
            dst_ref=relay,
            send_sem=halo_send.at[1, side],
            recv_sem=relay_recv,
            device_id=(my_b, wide - 1 if down else 0),
            device_id_type=MESH,
        )

    def halo_on(buffers, down):
        side = 0 if down else 1
        return pltpu.make_async_remote_copy(
            src_ref=relay,
            dst_ref=buffers[0 if down else 2].at[span(1), :],
            send_sem=relay_send,
            recv_sem=halo_recv.at[1, side],
            device_id=(my_b, high if down else low),
            device_id_type=MESH,
        )

    def halo_start(buffers, m):
        around_down = (my_w == low) & (m == 1)
        around_up = (my_w == high) & (m == 1)

        @pl.when((my_w < wide - 1) & jnp.logical_not(around_down))
        def _():
            halo(buffers, m, True).start()

        @pl.when(around_down)
        def _():
            halo_out(buffers, True).start()

        @pl.when((my_w > 0) & jnp.logical_not(around_up))
        def _():
            halo(buffers, m, False).start()

        @pl.when(around_up)
        def _():
            halo_out(buffers, False).start()

    def halo_pass(buffers):
        @pl.when(my_w == wide - 1)
        def _():
            halo_out(buffers, True).wait_recv()
            halo_on(buffers, True).start()

        @pl.when(my_w == 0)
        def _():
            halo_out(buffers, False).wait_recv()
            halo_on(buffers, False).start()

    def halo_wait(buffers, m):
        @pl.when(my_w < wide - 1)
        def _():
            halo(buffers, m, True).wait_send()
            halo(buffers, m, False).wait_recv()

        @pl.when(my_w > 0)
        def _():
            halo(buffers, m, False).wait_send()
            halo(buffers, m, True).wait_recv()

        @pl.when((m == 1) & ((my_w == 0) | (my_w == wide - 1)))
        def _():
            halo_on(buffers, True).wait_send()

    def heads(j):
        cols = pl.ds(pl.multiple_of(j * HB, HB), HB)
        for t in range(TASKS):
            taps_f[t, :, 0:HB] = dot(cot[:, t * HEAD : (t + 1) * HEAD], wh[j, t * HEAD : (t + 1) * HEAD, :])

        def body(i):
            at = pl.ds(pl.multiple_of(i * CH, CH), CH)
            values = [taps_f[t, at, 0:HB] for t in range(TASKS)]
            total = values[0] + values[1] + values[2]
            size = jnp.abs(values[0]) + jnp.abs(values[1]) + jnp.abs(values[2])
            keep = 0.5 * (1.0 + total / jnp.maximum(size, FLOOR))
            offset = SHARP * (keep - thr[at, cols].astype(F32))
            up = sigmoid(offset)
            down = 1.0 - up
            merged = jnp.zeros_like(total)
            for value in values:
                merged = merged + jnp.where(value > 0, up, down) * value
            thr[at, cols] = merged.astype(BF16)

        loop(2 * rows // CH, body)

    T = 256
    core, my_x, my_y = lax.rem(my_w, 2), lax.rem(my_w // 2, 2), my_w // 4
    to_core, to_x, to_y = 1 - 2 * core, 2 - 4 * my_x, 4 - 8 * my_y
    first = to_x * (1 - core) + to_y * core
    second = to_x * core + to_y * (1 - core)
    twin = my_w + to_core
    own = [my_w + to_x + to_y, my_w + first, my_w + second, my_w]
    theirs = [twin + to_x + to_y, twin + second, twin + first, twin]
    inner = (my_b == 1) | (my_b == 2)
    outer = (my_b == 0) | (my_b == 3)

    def tall(s):
        return pl.ds(pl.multiple_of(s * T, T), T)

    def grad_tall(held, lhs, rhs, mine):
        def body(i):
            s = 2 * i + (core if mine else 1 - core)
            held[tall(s), :] = dot(lhs[:, tall(s)], rhs, TN).astype(BF16)

        loop(wide // 2, body)

    def grad_heads(mine):
        def body(i):
            s = 2 * i + (core if mine else 1 - core)
            wh[s] = dot(cot_t[...], entry[2, :, tall(s)]).astype(BF16)

        loop(wide // 2, body)

    def grad_spatial(l, row_offset):
        def body(half):
            product = dot(act[l, row_offset, :, tall(half)], dcs[...], TN).astype(BF16)
            for c in range(3):
                base = pl.multiple_of((3 * row_offset + c) * C + half * T, T)
                gs[pl.ds(base, T), :] = product[:, c * C : (c + 1) * C]

        loop(C // T, body)

    def add_into(dst, src, n):
        step = 32

        def body(i):
            at = pl.ds(pl.multiple_of(i * step, step), step)
            dst[at, :] = dst[at, :] + src[at, :]

        loop(n // step, body)

    class Reduce:
        def __init__(self, kind, piece, some, recv_a, recv, final, n, sub, out):
            self.kind, self.piece, self.some, self.recv_a, self.recv, self.final = kind, piece, some, recv_a, recv, final
            self.n, self.sub, self.out = n, sub, out
            self.size = n // sub
            self.sem = rs_sem.at[pl.ds(sum(4 + 5 * k for k in list(PIECES.values())[:kind]), 4 + 5 * sub)]

        def rows_of(self, ref, j):
            return ref.at[pl.ds(j * self.size, self.size), :]

        def send(self, src, dst, send_sem, recv_sem, to):
            pltpu.make_async_remote_copy(
                src_ref=src, dst_ref=dst, send_sem=send_sem, recv_sem=recv_sem, device_id=to, device_id_type=MESH
            ).start()

        def wait(self, sem, rows):
            pltpu.make_async_copy(self.some(rows), self.some(rows), sem).wait()

        def piece_sem(self, j, which):
            return self.sem.at[4 + 5 * j + which]

        def a(self):
            for p in range(4):
                self.send(self.piece(theirs[p]), self.recv_a(p), self.sem.at[0], self.sem.at[1], (my_b, twin))

        def p(self, j):
            if j == 0:
                self.wait(self.sem.at[1], 4 * self.n)
            for p in range(4):
                add_into(self.rows_of(self.piece(own[p]), j), self.rows_of(self.recv_a(p), j), self.size)

        def b(self, j):
            for i in range(2):
                src = self.rows_of(self.piece(own[i]), j)
                self.send(src, self.recv(i, j), self.sem.at[0], self.piece_sem(j, 0), (my_b, my_w + first))

        def c(self, j):
            self.wait(self.piece_sem(j, 0), 2 * self.size)
            for i in range(2):
                mine = self.rows_of(self.piece(own[2 + i]), j)
                add_into(mine, self.recv(i, j), self.size)
                if i == 0:
                    self.send(mine, self.recv(2, j), self.sem.at[0], self.piece_sem(j, 1), (my_b, my_w + second))

        def d(self, j):
            self.wait(self.piece_sem(j, 1), self.size)
            final, mine, other = self.final(j), self.rows_of(self.piece(own[3]), j), self.recv(2, j)

            def body(i):
                at = pl.ds(pl.multiple_of(i * 32, 32), 32)
                final[at, :] = mine[at, :] + other[at, :]

            loop(self.size // 32, body)

            @pl.when(outer)
            def _():
                to = (1 + my_b // 2, my_w)
                self.send(final, self.recv(3, j), self.sem.at[2], self.piece_sem(j, 2), to)

        def e(self, j):
            @pl.when(inner)
            def _():
                self.wait(self.piece_sem(j, 2), self.size)
                add_into(self.final(j), self.recv(3, j), self.size)
                to = (3 - my_b, my_w)
                self.send(self.final(j), self.recv(4, j), self.piece_sem(j, 4), self.piece_sem(j, 3), to)

        def f(self, j):
            @pl.when(inner)
            def _():
                self.wait(self.piece_sem(j, 4), self.size)
                self.wait(self.piece_sem(j, 3), self.size)
                add_into(self.final(j), self.recv(4, j), self.size)
                to = (3 * (my_b - 1), my_w)
                self.send(self.final(j), self.recv(3, j), self.sem.at[2], self.piece_sem(j, 2), to)

        def g(self, j):
            dst = self.out.at[pl.ds(j * self.size, self.size), :]

            @pl.when(outer)
            def _():
                self.wait(self.piece_sem(j, 2), self.size)
                pltpu.make_async_copy(self.recv(3, j), dst, self.sem.at[3]).start()

            @pl.when(inner)
            def _():
                pltpu.make_async_copy(self.final(j), dst, self.sem.at[3]).start()

        def release(self):
            self.wait(self.sem.at[0], 7 * self.n)

        def close(self):
            self.wait(self.sem.at[2], self.n)
            self.wait(self.sem.at[3], self.n)

    def block(ref, index, n):
        begin, size = n
        return ref.at[pl.ds((index // 4) * T + begin, size), pl.ds((index % 4) * C, C)]

    def make_heads():
        def recv(index, j):
            return recv_h.at[index, pl.ds(j * (H // PIECES["H"]), H // PIECES["H"]), :]

        def recv_a(p):
            return gs.at[pl.ds(p * H, H), pl.ds(0, HB)]

        def some(n):
            return wh.at[pl.ds(0, n // H)] if n % H == 0 else wh.at[0, pl.ds(0, n), :]

        return Reduce(0, lambda s: wh.at[s], some, recv_a, recv, lambda j: recv(2, j), H, PIECES["H"], gh_out)

    def make_spatial(l):
        n = 9 * C // wide
        sub = PIECES[f"S{l}"]
        size = n // sub

        def recv(index, j):
            if l == 1 or index < 2:
                return recv_s.at[4 + index, pl.ds(j * size, size), :]
            third, begin = j * size // 192, j * size % 192
            if index == 2:
                return block(zc, 5 + third, (begin, size))
            return slc.at[pl.ds((index - 3) * 192 + begin, size), pl.ds(third * C, C)]

        def piece(s):
            return gs.at[pl.ds(pl.multiple_of(s * n, 64), n), :]

        return Reduce(
            1 + l, piece, lambda n: gs.at[pl.ds(0, n), :], lambda p: recv_s.at[p], recv, lambda j: recv(2, j), n, sub, gs_out.at[l]
        )

    def make_tall(kind, held, l, recv_a, recv, final, sub, out):
        def rows_of(j):
            return (j * (T // sub), T // sub)

        return Reduce(
            kind,
            lambda s: held.at[tall(s), :],
            lambda n: held.at[pl.ds(0, n), :],
            recv_a,
            lambda index, j: recv(index, rows_of(j)),
            lambda j: final(rows_of(j)),
            T, sub, out.at[l],
        )

    def shared_a(p):
        return block(entry.at[2], p, (0, T))

    def recv_a_reduce1(p):
        return act.at[1, p // 2, pl.ds((p % 2) * T, T), :]

    def recv_expand1(index, n):
        return block(entry.at[2], 4 + index, n) if index < 3 else recv_e.at[index - 3, pl.ds(*n), :]

    def recv_expand0(index, n):
        return block(entry.at[2], 4 + index, n) if index < 3 else zb.at[1, pl.ds((index - 3) * T + n[0], n[1]), :]

    def recv_reduce1(index, n):
        if index < 2:
            return slc.at[pl.ds(index * T + n[0], n[1]), pl.ds(3 * C, C)]
        return block(entry.at[2], 7, n) if index == 2 else recv_r.at[index - 3, pl.ds(*n), :]

    def recv_reduce0(index, n):
        return block(zc, index, n)

    table = {"H": make_heads(), "S1": make_spatial(1), "S0": make_spatial(0)}
    table["E1"] = make_tall(4, ger, 1, shared_a, recv_expand1, lambda n: recv_e.at[2, pl.ds(*n), :], PIECES["E1"], ge_out)
    table["E0"] = make_tall(3, ger, 0, shared_a, recv_expand0, lambda n: slb.at[1, pl.ds(*n), :], PIECES["E0"], ge_out)
    table["R1"] = make_tall(5, wr, 1, recv_a_reduce1, recv_reduce1, lambda n: recv_reduce1(2, n), PIECES["R1"], gr_out)
    table["R0"] = make_tall(6, we, 0, shared_a, recv_reduce0, lambda n: recv_reduce0(2, n), PIECES["R0"], gr_out)

    def input_grad(q):
        lanes = slice(q * Q, (q + 1) * Q)
        for m in range(2):
            taps_f[0, span(m), 0:Q] = dot(dred[span(m), :], wr[lanes, :], NT)

        def body(i):
            at = pl.ds(pl.multiple_of(i * CH, CH), CH)
            dexp[at, lanes] = (taps_f[0, at, 0:Q] + wide_f[at, lanes]).astype(BF16)

        loop(M // CH, body)

    by_number = [None] + [table[name] for name in ("H", "E1", "S1", "R1", "E0", "S0", "R0")]

    def point(place):
        for entry_code in AGENDA.get(place, ()):
            item, step, piece_index = entry_code // 100, entry_code // 10 % 10, entry_code % 10
            if item == 8:
                input_grad(piece_index)
                continue
            reduce = by_number[item]
            todo = (None, reduce.p, reduce.b, reduce.c, reduce.d, reduce.e, reduce.f, reduce.g)[step]
            for j in range(reduce.sub) if piece_index == 9 else (piece_index,):
                todo(j)

    spill_zc = pltpu.make_async_copy(zc, zc_far, out_sem.at[2])
    spill_slc = pltpu.make_async_copy(slc, slc_far, out_sem.at[3])
    back_zc = pltpu.make_async_copy(zc_far, zc, out_sem.at[2])
    back_slc = pltpu.make_async_copy(slc_far, slc, out_sem.at[3])
    ggm_ref[...] = jnp.zeros_like(ggm_ref)
    gsm_ref[...] = jnp.zeros_like(gsm_ref)
    ggo_ref[...] = jnp.zeros_like(ggo_ref)
    gso_ref[...] = jnp.zeros_like(gso_ref)
    load_act.wait()
    for copy in load_small:
        copy.wait()

    for l in range(2):
        load_wr(l).wait()

        def reduce_in(m):
            mid_f[span(m), :] = dot(entry[l, span(m), :], wr[...])
            if l == 0:
                pl.when(m == 0)(lambda: pl.semaphore_wait(barrier, wide + batch - 2))
            mid_stats(0, m, FWD if l == 0 else W4)

        loop(2, reduce_in)
        if l == 0:
            load_wr(1).start()
            load_cot.wait()
            load_wh.wait()
            load_thr.wait()
            cot_t[...] = cot[...].T
        heads(4 * l)
        loop(2, lambda m: sum_middle(0, m, FWD if l == 0 else W4))
        heads(4 * l + 1)
        load_ws(l).wait()

        def conv_own(m):
            def store(at, value):
                act[l, 1, at, :] = value

            mid_forward(0, l, 0, m, FWD if l == 0 else W4, za, sla, store, gia)
            halo_start([act.at[l, r] for r in range(3)], m)
            for c in range(3):
                taps_f[c, span(m), :] = dot(act[l, 1, span(m), :], ws[(3 + c) * C : (4 + c) * C, :])

        loop(2, conv_own)
        halo_pass([act.at[l, r] for r in range(3)])

        def conv_rest(m):
            halo_wait([act.at[l, r] for r in range(3)], m)
            for c in range(3):
                taps_f[c, span(m), :] += dot(act[l, 0, span(m), :], ws[c * C : (c + 1) * C, :]) + dot(
                    act[l, 2, span(m), :], ws[(6 + c) * C : (7 + c) * C, :]
                )

            def body(i):
                at = chunk(m, i)
                mid_f[at, :] = taps_f[1, at, :] + shifted(taps_f[0, at, :], 1) + shifted(taps_f[2, at, :], -1)

            loop(rows // CH, body)
            mid_stats(1, m, W4)

        loop(2, conv_rest)
        if l == 0:
            load_ws(1).start()
        heads(4 * l + 2)
        loop(2, lambda m: sum_middle(1, m, W4))
        heads(4 * l + 3)
        load_we(l).wait()

        def expand(m):
            def store(at, value):
                actb[l, at, :] = value

            mid_forward(1, l, 1, m, W4, zb, slb, store, gib)
            for q in range(4):
                lanes = slice(q * Q, (q + 1) * Q)
                wide_f[span(m), lanes] = dot(actb[l, span(m), :], we[lanes, :], NT)

                def body(i, c):
                    z = wide_f[chunk(m, i), lanes]
                    zw = z * along(valid_ref[chunk(m, i), :], Q)
                    return c[0] + fold8(zw), c[1] + fold8(zw * z)

                first, second = lax.fori_loop(0, rows // CH, body, (zero(Q), zero(Q)), unroll=4)
                pack(2, m, 0, q * Q, Q, first)
                pack(2, m, 1, q * Q, Q, second)
            sum_start(2, m, Q)

        loop(2, expand)
        if l == 0:
            load_we(1).start()
        loop(2, lambda m: sum_middle(2, m, Q))

        def output(m):
            total = sum_end(2, m, Q)
            rn = along(count[m, 0:1, :], Q)
            for q in range(4):
                lanes = slice(q * Q, (q + 1) * Q)
                mean = total[q : q + 1] * rn
                inv = lax.rsqrt(total[4 + q : 5 + q] * rn - mean * mean + EPS)
                gain = go_ref[l : l + 1, lanes]
                shift = so_ref[l : l + 1, lanes]
                gic[l, m, 0:1, lanes] = gain * inv

                def body(i, c):
                    at = chunk(m, i)
                    v = along(valid_ref[at, :], Q)
                    zhat = (wide_f[at, lanes] - mean) * inv
                    kept = pl.ds(pl.multiple_of(q * M + m * rows + i * CH, CH), CH)
                    below = entry[l, at, lanes].astype(F32)
                    if l == 1:
                        below = below + ger[kept, :].astype(F32)
                    before = gain * zhat + shift + below
                    s = sigmoid(before)
                    value = before * s * v
                    slope = s * (1.0 + before * (1.0 - s)) * v
                    zc[at, lanes] = zhat.astype(BF16)
                    slc[at, lanes] = slope.astype(BF16)
                    low = value.astype(BF16)
                    entry[l + 1, at, lanes] = low
                    if l == 0:
                        ger[kept, :] = (value - low.astype(F32)).astype(BF16)
                        return c
                    d = thr[at, lanes].astype(F32) * slope
                    wide_f[at, lanes] = d
                    return c[0] + fold8(d), c[1] + fold8(d * zhat)

                if l == 0:
                    lax.fori_loop(0, rows // CH, body, 0, unroll=4)
                else:
                    first, second = lax.fori_loop(0, rows // CH, body, (zero(Q), zero(Q)), unroll=4)
                    pack(0, m, 0, q * Q, Q, first)
                    pack(0, m, 1, q * Q, Q, second)
            if l == 1:
                sum_start(0, m, Q)

        if l == 1:
            spill_zc.wait()
            spill_slc.wait()
        loop(2, output)
        if l == 0:
            spill_zc.start()
            spill_slc.start()

    store_small = [
        pltpu.make_async_copy(src, dst, out_sem.at[4 + i])
        for i, (src, dst) in enumerate(
            ((ggm_ref, ggm_out), (gsm_ref, gsm_out), (ggo_ref, ggo_out), (gso_ref, gso_out))
        )
    ]
    store_y = pltpu.make_async_copy(entry.at[2], y_out, out_sem.at[0])
    store_y.start()
    back_slc.start()
    grad_heads(False)
    loop(2, lambda m: sum_middle(0, m, Q))
    table["H"].a()
    grad_heads(True)
    store_y.wait()
    point(100)

    for l in (1, 0):
        if l == 0:
            load_we(0).wait()

        def back_out(m):
            total = sum_end(0, m, Q)
            rn = along(count[m, 0:1, :], Q)
            for q in range(4):
                lanes = slice(q * Q, (q + 1) * Q)
                sd, sz = total[q : q + 1], total[4 + q : 5 + q]
                gso_ref[l : l + 1, lanes] += sd
                ggo_ref[l : l + 1, lanes] += sz
                sd, sz = sd * rn, sz * rn
                gi = gic[l, m, 0:1, lanes]

                def body(i):
                    at = chunk(m, i)
                    v = along(valid_ref[at, :], Q)
                    zhat = zc[at, lanes].astype(F32)
                    dexp[at, lanes] = (v * gi * (wide_f[at, lanes] - (sd + zhat * sz))).astype(BF16)

                loop(rows // CH, body)
            mid_f[span(m), :] = dot(dexp[span(m), :], we[...])
            mid_back_sums(1, l, m, zb, slb)

        loop(2, back_out)
        if l == 1:
            load_we(0).start()
            back_zc.start()
        point(100 * l + 1)
        if l == 0:
            table["E1"].release()
        grad_tall(ger, dexp, actb[l], False)
        loop(2, lambda m: sum_middle(1, m, W4))
        point(100 * l + 2)
        table[f"E{l}"].a()
        grad_tall(ger, dexp, actb[l], True)
        point(100 * l + 3)
        if l == 0:
            load_ws(0).wait()

        grad_rows = [dcv.at[0], dcs.at[:, pl.ds(C, C)], dcv.at[1]]

        def back_conv(m):
            def store(at, value):
                low = value.astype(BF16)
                dcs[at, C : 2 * C] = low
                dcs[at, 0:C] = shifted(value, -1).astype(BF16)
                dcs[at, 2 * C : 3 * C] = shifted(value, 1).astype(BF16)

            mid_back(1, l, 1, m, zb, gib, store)
            halo_start(grad_rows, m)
            for c in range(3):
                taps_f[c, span(m), :] = dot(dcs[span(m), C : 2 * C], ws[(3 + c) * C : (4 + c) * C, :], NT)

        loop(2, back_conv)
        halo_pass(grad_rows)
        point(100 * l + 4)
        if l == 0:
            table["S1"].release()
        grad_spatial(l, 1)
        point(100 * l + 5)

        def back_rest(m):
            halo_wait(grad_rows, m)
            for c in range(3):
                taps_f[c, span(m), :] += dot(dcv[0, span(m), :], ws[(6 + c) * C : (7 + c) * C, :], NT) + dot(
                    dcv[1, span(m), :], ws[c * C : (c + 1) * C, :], NT
                )

            def body(i):
                at = chunk(m, i)
                mid_f[at, :] = taps_f[1, at, :] + shifted(taps_f[0, at, :], -1) + shifted(taps_f[2, at, :], 1)

            loop(rows // CH, body)
            mid_back_sums(2, l, m, za, sla)

        loop(2, back_rest)
        if l == 1:
            load_ws(0).start()
        point(100 * l + 6)
        grad_spatial(l, 0)
        if l == 0:
            grad_spatial(l, 2)
            table["S0"].a()
        loop(2, lambda m: sum_middle(2, m, W4))
        point(100 * l + 7)
        if l == 0:
            table["R1"].release()
            load_wr(0).start()
        if l == 1:
            grad_spatial(l, 2)
            table["S1"].a()
        point(100 * l + 8)
        if l == 0:
            load_wr(0).wait()

        if l == 1:
            back_zc.wait()
            back_slc.wait()

        def back_in(m):
            def store(at, value):
                dred[at, :] = value.astype(BF16)

            mid_back(2, l, 0, m, za, gia, store)
            for q in range(4 if l == 1 else 0):
                lanes = slice(q * Q, (q + 1) * Q)
                taps_f[0, span(m), 0:Q] = dot(dred[span(m), :], wr[lanes, :], NT)

                def body(i, c):
                    at = chunk(m, i)
                    d = (taps_f[0, at, 0:Q] + wide_f[at, lanes]) * slc[at, lanes].astype(F32)
                    wide_f[at, lanes] = d
                    return c[0] + fold8(d), c[1] + fold8(d * zc[at, lanes].astype(F32))

                first, second = lax.fori_loop(0, rows // CH, body, (zero(Q), zero(Q)), unroll=4)
                pack(0, m, 0, q * Q, Q, first)
                pack(0, m, 1, q * Q, Q, second)
            if l == 1:
                sum_start(0, m, Q)

        loop(2, back_in)
        if l == 1:
            point(109)
            grad_tall(wr, entry.at[1], dred[...], False)
            loop(2, lambda m: sum_middle(0, m, Q))
            point(110)
            table["R1"].a()
            grad_tall(wr, entry.at[1], dred[...], True)
            point(111)
        else:
            grad_tall(we, entry.at[0], dred[...], False)
            table["R0"].a()
            grad_tall(we, entry.at[0], dred[...], True)
            for copy in store_small:
                copy.start()
            point(9)

    for copy in store_small:
        copy.wait()
    store_dx = pltpu.make_async_copy(dexp, dx_out, out_sem.at[1])
    store_dx.start()
    store_dx.wait()
    for name in ("H", "E0", "S0", "R0"):
        table[name].release()
    for item in table.values():
        item.close()


def run_block(act, thr, cot, valid, w_reduce, w_spatial, w_expand, w_heads, gm, sm, go, so):
    wide, batch = lax.axis_size("wide"), lax.axis_size("batch")
    M, D = act.shape
    C = w_reduce.shape[2]
    H = w_heads.shape[0]
    rows = M // 2
    Q = D // 4
    hbm = pl.BlockSpec(memory_space=pl.ANY)
    V, DMA = pltpu.VMEM, pltpu.SemaphoreType.DMA
    scratch = [
        V((D, C), BF16), V((9 * C, C), BF16), V((D, C), BF16), V((D // HB, H, HB), BF16),
        V((3, M, D), BF16), V((M, D), F32), V((M, D), BF16),
        V((M, H), BF16), V((H, M), BF16),
        V((2, 3, M, C), BF16), V((2, M, C), BF16), V((2, M, C), BF16),
        V((2, M, C), BF16), V((2, M, C), BF16), V((2, M, C), BF16),
        V((M, D), BF16), V((M, D), BF16),
        V((M, C), F32), V((3, M, C), F32),
        V((2, M, C), BF16), V((M, 3 * C), BF16), V((M, C), BF16),
        V((2, 2, 8, C), F32), V((2, 2, 8, C), F32), V((2, 2, 8, D), F32), V((2, 8, 128), F32),
        V((3, 2, 8, Q), F32), V((3, 2, 8, Q), F32),
        V((3, 2, wide, 8, Q), F32), V((3, 2, batch, 8, Q), F32),
        V((D, C), BF16), V((9 * C, C), BF16),
        V((5, H, HB), BF16), V((9, 9 * C // wide, C), BF16), V((3, 256, C), BF16), V((2, 256, C), BF16),
        V((rows, C), BF16),
        V((2, 2, C), F32), V((2, 2, C), F32), V((2, D), F32), V((2, D), F32), V((M, 128), F32),
        V((2, 2, C), F32), V((2, 2, C), F32), V((2, D), F32), V((2, D), F32),
        DMA((12,)), DMA((3, 2)), DMA((3, 2)), DMA((3, 2)), DMA((3, 2)),
        DMA((2, 2)), DMA((2, 2)), DMA, DMA, DMA((8,)), DMA((sum(4 + 5 * k for k in PIECES.values()),)),
    ]
    shape = jax.ShapeDtypeStruct
    return pl.pallas_call(
        functools.partial(block_kernel, (wide, batch, rows, D, C, H)),
        out_shape=[
            shape((M, D), BF16), shape((M, D), BF16),
            shape((2, D // wide, C), BF16), shape((2, 9 * C // wide, C), BF16), shape((2, D // wide, C), BF16), shape((H, D // wide), BF16),
            shape((2, 2, C), F32), shape((2, 2, C), F32), shape((2, D), F32), shape((2, D), F32),
            shape((M, D), BF16), shape((M, D), BF16),
        ],
        in_specs=[hbm] * 12,
        out_specs=[hbm] * 12,
        scratch_shapes=scratch,
        compiler_params=pltpu.CompilerParams(
            collective_id=7, has_side_effects=True, vmem_limit_bytes=VMEM_BYTES
        ),
    )(act, thr, cot, valid, w_reduce, w_spatial, w_expand, w_heads, gm, sm, go, so)


def finish_kernel(n, *refs):
    ins, outs, held, wide, sems, out_sems = refs[:n], refs[n : 2 * n], refs[2 * n : 3 * n], refs[3 * n : -2], refs[-2], refs[-1]
    loads = [pltpu.make_async_copy(ins[i], held[i], sems.at[i]) for i in range(n)]
    for copy in loads:
        copy.start()
    stores = []
    w = 0
    for i in range(n):
        loads[i].wait()
        src = held[i]
        if ins[i].dtype != outs[i].dtype:
            src = wide[w]
            w += 1
            rows = 64
            if len(src.shape) == 2:
                def body(r, src=src, i=i):
                    at = pl.ds(pl.multiple_of(r * rows, rows), rows)
                    src[at, :] = held[i][at, :].astype(F32)

                loop(src.shape[0] // rows, body)
            else:
                for l in range(src.shape[0]):
                    def body(r, src=src, i=i, l=l):
                        at = pl.ds(pl.multiple_of(r * rows, rows), rows)
                        src[l, at, :] = held[i][l, at, :].astype(F32)

                    loop(src.shape[1] // rows, body)
        stores.append(pltpu.make_async_copy(src, outs[i], out_sems.at[i]))
        stores[-1].start()
    for copy in stores:
        copy.wait()


def finish(*arrays):
    hbm = pl.BlockSpec(memory_space=pl.ANY)
    n = len(arrays)
    widened = [a.dtype == BF16 and 2 <= i < 6 for i, a in enumerate(arrays)]
    out = [jax.ShapeDtypeStruct(a.shape, F32 if w else a.dtype) for a, w in zip(arrays, widened)]
    scratch = [pltpu.VMEM(a.shape, a.dtype) for a in arrays]
    scratch += [pltpu.VMEM(a.shape, F32) for a, w in zip(arrays, widened) if w]
    return pl.pallas_call(
        functools.partial(finish_kernel, n),
        out_shape=out,
        in_specs=[hbm] * n,
        out_specs=[hbm] * n,
        scratch_shapes=scratch + [pltpu.SemaphoreType.DMA((n,)), pltpu.SemaphoreType.DMA((n,))],
        compiler_params=pltpu.CompilerParams(vmem_limit_bytes=VMEM_BYTES),
    )(*arrays)


def shards_rows(
    activations, bucket_ids, thresholds, head_cot, w_reduce, w_spatial, w_expand,
    gain_mid, shift_mid, gain_out, shift_out, w_heads,
):
    micro, images, pixels, D = activations.shape
    M = micro * images * pixels
    L, _, C = w_reduce.shape
    H = head_cot.shape[-1]
    wide = lax.axis_size("wide")
    positions = lax.axis_index("wide") * pixels + jnp.arange(pixels, dtype=jnp.int32)
    valid = jnp.broadcast_to(frame_mask(bucket_ids, positions).reshape(M, 1), (M, 128))
    y, dx, gr, gs, ge, gh, ggm, gsm, ggo, gso, _, _ = run_block(
        activations.reshape(M, D), thresholds.reshape(M, D), head_cot.reshape(M, H), valid,
        w_reduce, w_spatial, w_expand, w_heads,
        gain_mid, shift_mid, gain_out, shift_out,
    )
    y, dx, gr, gs, ge, gh, ggm, gsm, ggo, gso = finish(y, dx, gr, gs, ge, gh, ggm, gsm, ggo, gso)

    return (
        y.reshape(activations.shape),
        dx.reshape(activations.shape),
        gr,
        gs,
        ge,
        ggm,
        gsm,
        ggo,
        gso,
        gh,
    )


def solution(mesh):
    placed = (
        P(None, "batch", "wide", None),
        P(None, "batch"),
        P(None, "batch", "wide", None),
        P(None, "batch", "wide", None),
        P(),
        P(),
        P(),
        P(),
        P(),
        P(),
        P(),
        P(),
    )
    def split(*arrays):
        micro, images, pixels, features = arrays[0].shape
        whole_rows = pixels == FRAME and FRAME == lax.axis_size("wide") and lax.axis_size("batch") == 4
        fits = micro == 2 and images * pixels == 256 and features == 2048 and arrays[4].shape[2] == 512
        return (shards_rows if whole_rows and fits else shards)(*arrays)

    return jax.shard_map(
        split,
        mesh=mesh,
        in_specs=placed,
        out_specs=(
            P(None, "batch", "wide", None),
            P(None, "batch", "wide", None),
            P(None, "wide", None),
            P(None, "wide", None),
            P(None, "wide", None),
            P(),
            P(),
            P(),
            P(),
            P(None, "wide"),
        ),
        check_vma=False,
    )
```

```python
import functools

import jax
import jax.numpy as jnp
from jax import lax
from jax.experimental import pallas as pl
from jax.experimental.pallas import tpu as pltpu
from jax.sharding import PartitionSpec as P

HEAD = 256
TASKS = 3
FRAME = 8


EPS = 1e-05
SHARP = 8.0
FLOOR = 0.25
ROW_TABLE = (8, 8, 7, 6, 8, 5, 7, 8)
COL_TABLE = (8, 7, 8, 8, 6, 8, 7, 5)


def silu_slope(values):
    gate_val = jax.nn.sigmoid(values)
    return gate_val * (1.0 + values * (1.0 - gate_val))


def frame_mask(buckets, positions):
    bucket_kinds = jnp.arange(len(ROW_TABLE), dtype=jnp.int32)
    onehot = (buckets[..., None] == bucket_kinds).astype(jnp.int32)
    heights = jnp.sum(onehot * jnp.array(ROW_TABLE, dtype=jnp.int32), -1)
    widths = jnp.sum(onehot * jnp.array(COL_TABLE, dtype=jnp.int32), -1)
    rowpos = positions // FRAME
    colpos = positions % FRAME
    inside = (rowpos < heights[..., None]) & (colpos < widths[..., None])
    return inside.astype(jnp.float32)


def unfold_taps(images):
    padded = jnp.pad(images, ((0, 0), (1, 1), (1, 1), (0, 0)))
    pieces = [
        padded[:, row_off : row_off + FRAME, col_off : col_off + FRAME, :]
        for row_off in range(3)
        for col_off in range(3)
    ]
    return jnp.concatenate(pieces, -1)


def fold_taps(columns, channels):
    total_sum = jnp.zeros(columns.shape[:-1] + (channels,), columns.dtype)
    for tap_index in range(9):
        row_off, col_off = divmod(tap_index, 3)
        tap_part = columns[..., tap_index * channels : (tap_index + 1) * channels]
        padded = jnp.pad(tap_part, ((0, 0), (1, 1), (1, 1), (0, 0)))
        total_sum = (
            total_sum
            + padded[:, 2 - row_off : 2 - row_off + FRAME, 2 - col_off : 2 - col_off + FRAME, :]
        )
    return total_sum


def sum_kernel(wide, batch, x_ref, o_ref, near, far, part, near_send, near_recv, far_send, far_recv):
    my_w = lax.axis_index("wide")
    my_b = lax.axis_index("batch")
    barrier = pltpu.get_barrier_semaphore()
    for step in range(1, wide):
        pl.semaphore_signal(
            barrier, inc=1, device_id=(my_b, lax.rem(my_w + step, wide)), device_id_type=pl.DeviceIdType.MESH
        )
    for step in range(1, batch):
        pl.semaphore_signal(
            barrier, inc=1, device_id=(lax.rem(my_b + step, batch), my_w), device_id_type=pl.DeviceIdType.MESH
        )
    pl.semaphore_wait(barrier, wide + batch - 2)

    def exchange(src, slots, send, recv, count, me, target):
        copies = []
        for step in range(1, count):
            copy = pltpu.make_async_remote_copy(
                src_ref=src,
                dst_ref=slots.at[me],
                send_sem=send.at[step],
                recv_sem=recv.at[step],
                device_id=target(lax.rem(me + step, count)),
                device_id_type=pl.DeviceIdType.MESH,
            )
            copy.start()
            copies.append(copy)
        slots[me] = src[...]
        for copy in copies:
            copy.wait()
        total = slots[0]
        for index in range(1, count):
            total = total + slots[index]
        return total

    part[...] = exchange(x_ref, near, near_send, near_recv, wide, my_w, lambda w: (my_b, w))
    o_ref[...] = exchange(part, far, far_send, far_recv, batch, my_b, lambda b: (b, my_w))


def sum_all(values):
    wide, batch = lax.axis_size("wide"), lax.axis_size("batch")
    block = values.shape
    return pl.pallas_call(
        functools.partial(sum_kernel, wide, batch),
        out_shape=jax.ShapeDtypeStruct(block, jnp.float32),
        in_specs=[pl.BlockSpec(memory_space=pltpu.VMEM)],
        out_specs=pl.BlockSpec(memory_space=pltpu.VMEM),
        scratch_shapes=[
            pltpu.VMEM((wide,) + block, jnp.float32),
            pltpu.VMEM((batch,) + block, jnp.float32),
            pltpu.VMEM(block, jnp.float32),
            pltpu.SemaphoreType.DMA((wide,)),
            pltpu.SemaphoreType.DMA((wide,)),
            pltpu.SemaphoreType.DMA((batch,)),
            pltpu.SemaphoreType.DMA((batch,)),
        ],
        compiler_params=pltpu.CompilerParams(collective_id=block[-1] // 512, has_side_effects=True),
    )(values)


def batch_norm(values, valid_rows, scale_vec, offset_vec):
    weighted = values * valid_rows[..., None]
    sum_first = jnp.sum(weighted, 1)
    sum_second = jnp.sum(weighted * values, 1)
    counts = jnp.sum(valid_rows, 1)
    count_row = jnp.broadcast_to(counts[:, None], sum_first.shape)
    summed = sum_all(jnp.concatenate([sum_first, sum_second, count_row, jnp.zeros_like(sum_first)], 0))
    sum_first, sum_second, counts = summed[0:2], summed[2:4], summed[4:6, 0]
    mean_val = sum_first / counts[:, None]
    spread = sum_second / counts[:, None] - mean_val * mean_val
    inv_std = lax.rsqrt(spread + EPS)
    normed = (values - mean_val[:, None, :]) * inv_std[:, None, :]
    return (normed, scale_vec * normed + offset_vec, inv_std, counts)


def norm_back(grad_out, normed, inv_std, counts, valid_rows, scale_vec):
    sum_grad = jnp.sum(grad_out, 1)
    sum_prod = jnp.sum(grad_out * normed, 1)
    summed = sum_all(jnp.concatenate([sum_grad, sum_prod, sum_grad, sum_prod], 0))
    sum_grad, sum_prod = summed[0:2], summed[2:4]
    centered = (
        grad_out - (sum_grad[:, None, :] + normed * sum_prod[:, None, :]) / counts[:, None, None]
    )
    grad_in = valid_rows[..., None] * scale_vec * inv_std[:, None, :] * centered
    return (grad_in, jnp.sum(sum_prod, 0), jnp.sum(sum_grad, 0))


def forward_layer(layer_in, pix_valid, img_valid, params, layout):
    w_in, w_mid, w_out, scale_a, offset_a, scale_b, offset_b, scale_c, offset_c = params
    groups, per_lane, local_imgs = layout
    span_len = layer_in.shape[0]
    channels = w_in.shape[1]
    entry_low = layer_in.astype(jnp.bfloat16)
    reduced = jnp.einsum("mrd,dc->mrc", entry_low, w_in, preferred_element_type=jnp.float32)
    normed_a, bn_a, inv_a, counts = batch_norm(reduced, pix_valid, scale_a, offset_a)
    act_a = (jax.nn.silu(bn_a) * pix_valid[..., None]).astype(jnp.bfloat16)
    arrived = lax.all_to_all(
        act_a.reshape(span_len, groups, per_lane, channels),
        "wide",
        split_axis=1,
        concat_axis=2,
        tiled=True,
    )
    count_imgs = arrived.shape[1]
    images = arrived.reshape(span_len * count_imgs, FRAME, FRAME, channels)
    columns = unfold_taps(images).reshape(span_len, count_imgs, FRAME * FRAME, 9 * channels)
    conv_out = jnp.einsum("mkpc,co->mkpo", columns, w_mid, preferred_element_type=jnp.float32)
    taps_saved, conv_out = (columns, conv_out)
    taps_saved = taps_saved.reshape(span_len, -1, taps_saved.shape[-1])
    conv_out = conv_out.reshape(span_len, -1, channels)
    normed_b, bn_b, inv_b, unused_counts = batch_norm(conv_out, img_valid, scale_b, offset_b)
    act_b = (jax.nn.silu(bn_b) * img_valid[..., None]).astype(jnp.bfloat16)
    returned = lax.all_to_all(
        act_b.reshape(span_len, local_imgs, FRAME * FRAME, channels),
        "wide",
        split_axis=2,
        concat_axis=1,
        tiled=True,
    ).reshape(span_len, -1, channels)
    expanded = jnp.einsum("mrc,oc->mro", returned, w_out, preferred_element_type=jnp.float32)
    normed_c, bn_c, inv_c, unused_again = batch_norm(expanded, pix_valid, scale_c, offset_c)
    before = bn_c + layer_in
    result = jax.nn.silu(before) * pix_valid[..., None]
    saved = (
        entry_low,
        normed_a,
        bn_a,
        inv_a,
        taps_saved,
        normed_b,
        bn_b,
        inv_b,
        returned,
        normed_c,
        before,
        inv_c,
        counts,
    )
    return (result, saved)


def backward_layer(incoming, saved, pix_valid, img_valid, params, layout):
    w_in, w_mid, w_out, scale_a, offset_a, scale_b, offset_b, scale_c, offset_c = params
    groups, per_lane, local_imgs = layout
    (
        entry_low,
        normed_a,
        bn_a,
        inv_a,
        taps_saved,
        normed_b,
        bn_b,
        inv_b,
        returned,
        normed_c,
        before,
        inv_c,
        counts,
    ) = saved
    span_len = incoming.shape[0]
    channels = w_in.shape[1]
    grad_pre = incoming * pix_valid[..., None] * silu_slope(before)
    grad_c, scale_gc, offset_gc = norm_back(grad_pre, normed_c, inv_c, counts, pix_valid, scale_c)
    grad_c_low = grad_c.astype(jnp.bfloat16)
    g_out = jnp.einsum("mro,mrc->oc", grad_c_low, returned, preferred_element_type=jnp.float32)
    d_returned = jnp.einsum(
        "mro,oc->mrc", grad_c_low, w_out, preferred_element_type=jnp.float32
    ).astype(jnp.bfloat16)
    d_images = lax.all_to_all(
        d_returned.reshape(span_len, groups, per_lane, channels),
        "wide",
        split_axis=1,
        concat_axis=2,
        tiled=True,
    ).reshape(span_len, -1, channels)
    d_bn_b = d_images.astype(jnp.float32) * img_valid[..., None] * silu_slope(bn_b)
    grad_b, scale_gb, offset_gb = norm_back(d_bn_b, normed_b, inv_b, counts, img_valid, scale_b)
    grad_b_low = grad_b.astype(jnp.bfloat16)
    g_mid = jnp.einsum("mrk,mro->ko", taps_saved, grad_b_low, preferred_element_type=jnp.float32)
    d_columns = jnp.einsum("mro,ko->mrk", grad_b_low, w_mid, preferred_element_type=jnp.float32)
    d_act = fold_taps(
        d_columns.reshape(span_len * local_imgs, FRAME, FRAME, 9 * channels), channels
    )
    d_act = d_act.astype(jnp.bfloat16).reshape(span_len, local_imgs, FRAME * FRAME, channels)
    d_pixels = lax.all_to_all(d_act, "wide", split_axis=2, concat_axis=1, tiled=True).reshape(
        span_len, -1, channels
    )
    d_bn_a = d_pixels.astype(jnp.float32) * pix_valid[..., None] * silu_slope(bn_a)
    grad_a, scale_ga, offset_ga = norm_back(d_bn_a, normed_a, inv_a, counts, pix_valid, scale_a)
    grad_a_low = grad_a.astype(jnp.bfloat16)
    g_in = jnp.einsum("mrd,mrc->dc", entry_low, grad_a_low, preferred_element_type=jnp.float32)
    d_entry = jnp.einsum("mrc,dc->mrd", grad_a_low, w_in, preferred_element_type=jnp.float32)
    return (
        d_entry + grad_pre,
        (g_in, g_mid, g_out),
        (scale_ga, offset_ga, scale_gb, offset_gb, scale_gc, offset_gc),
    )


def grad_drop(task_values, limits):
    task_total = task_values[0]
    magnitude = jnp.abs(task_values[0])
    for task_index in range(1, len(task_values)):
        task_total = task_total + task_values[task_index]
        magnitude = magnitude + jnp.abs(task_values[task_index])
    keep_ratio = 0.5 * (1.0 + task_total / jnp.maximum(magnitude, FLOOR))
    upward = jax.nn.sigmoid(SHARP * (keep_ratio - limits))
    downward = jax.nn.sigmoid(SHARP * (limits - keep_ratio))
    merged = jnp.zeros_like(task_total)
    for task_value in task_values:
        merged = merged + jnp.where(task_value > 0, upward, downward) * task_value
    return merged


def add_tuples(left, right):
    return tuple((left_item + right_item for left_item, right_item in zip(left, right)))


def shards(
    activations,
    bucket_ids,
    thresholds,
    head_cot,
    w_reduce,
    w_spatial,
    w_expand,
    gain_mid,
    shift_mid,
    gain_out,
    shift_out,
    w_heads,
):
    micro_total, groups, per_lane, features = activations.shape
    lane_count = lax.axis_size("wide")
    local_imgs = groups // lane_count
    lane_index = lax.axis_index("wide")
    layout = (groups, per_lane, local_imgs)
    pix_positions = lane_index * per_lane + jnp.arange(per_lane, dtype=jnp.int32)
    pix_valid_all = frame_mask(bucket_ids, pix_positions).reshape(micro_total, -1)
    own_ids = lax.dynamic_slice_in_dim(bucket_ids, lane_index * local_imgs, local_imgs, 1)
    img_valid_all = frame_mask(own_ids, jnp.arange(FRAME * FRAME, dtype=jnp.int32)).reshape(
        micro_total, -1
    )
    layer_total = w_reduce.shape[0]
    head_width = head_cot.shape[-1]
    layer_params = [
        (
            w_reduce[layer_index],
            w_spatial[layer_index],
            w_expand[layer_index],
            gain_mid[layer_index, 0],
            shift_mid[layer_index, 0],
            gain_mid[layer_index, 1],
            shift_mid[layer_index, 1],
            gain_out[layer_index],
            shift_out[layer_index],
        )
        for layer_index in range(layer_total)
    ]
    spans = [(0, micro_total)]
    weight_acc = [None] * layer_total
    norm_acc = [None] * layer_total
    heads_acc = jnp.zeros((features, head_width), jnp.float32)
    outs_y = []
    outs_dx = []
    for span_at, span_len in spans:

        def take_span(array):
            return lax.slice_in_dim(array, span_at, span_at + span_len, axis=0)

        pix_valid = take_span(pix_valid_all)
        img_valid = take_span(img_valid_all)
        carried = take_span(activations).reshape(span_len, -1, features).astype(jnp.float32)
        saved_layers = []
        for layer_index in range(layer_total):
            carried, saved = forward_layer(
                carried, pix_valid, img_valid, layer_params[layer_index], layout
            )
            saved_layers.append(saved)
        result_low = carried.astype(jnp.bfloat16)
        outs_y.append(result_low.reshape(span_len, groups, per_lane, features))
        head_grads = take_span(head_cot).reshape(span_len, -1, head_width)
        heads_acc = heads_acc + jnp.einsum(
            "mrd,mrh->dh", result_low, head_grads, preferred_element_type=jnp.float32
        )
        task_values = [
            jnp.einsum(
                "mrh,hd->mrd",
                head_grads[..., task_index * HEAD : (task_index + 1) * HEAD],
                w_heads[task_index * HEAD : (task_index + 1) * HEAD],
                preferred_element_type=jnp.float32,
            )
            for task_index in range(TASKS)
        ]
        limits = take_span(thresholds).reshape(span_len, -1, features).astype(jnp.float32)
        incoming = grad_drop(task_values, limits)
        for layer_index in reversed(range(layer_total)):
            incoming, weight_parts, norm_parts = backward_layer(
                incoming,
                saved_layers[layer_index],
                pix_valid,
                img_valid,
                layer_params[layer_index],
                layout,
            )
            if weight_acc[layer_index] is None:
                weight_acc[layer_index] = weight_parts
                norm_acc[layer_index] = norm_parts
            else:
                weight_acc[layer_index] = add_tuples(weight_acc[layer_index], weight_parts)
                norm_acc[layer_index] = add_tuples(norm_acc[layer_index], norm_parts)
        outs_dx.append(incoming.astype(jnp.bfloat16).reshape(span_len, groups, per_lane, features))
    stack_in = jnp.stack([layer_acc[0] for layer_acc in weight_acc])
    stack_mid = jnp.stack([layer_acc[1] for layer_acc in weight_acc])
    stack_out = jnp.stack([layer_acc[2] for layer_acc in weight_acc])
    shard_in, shard_mid, shard_out, shard_heads = (
        lax.psum_scatter(
            stack_in.astype(jnp.bfloat16), "wide", scatter_dimension=1, tiled=True
        ).astype(jnp.float32),
        lax.psum_scatter(
            stack_mid.astype(jnp.bfloat16), "wide", scatter_dimension=1, tiled=True
        ).astype(jnp.float32),
        lax.psum_scatter(
            stack_out.astype(jnp.bfloat16), "wide", scatter_dimension=1, tiled=True
        ).astype(jnp.float32),
        lax.psum_scatter(
            heads_acc[None].astype(jnp.bfloat16), "wide", scatter_dimension=1, tiled=True
        ).astype(jnp.float32),
    )
    shard_in, shard_mid, shard_out, shard_heads = (
        lax.psum(shard_in.astype(jnp.bfloat16), "batch").astype(jnp.float32),
        lax.psum(shard_mid.astype(jnp.bfloat16), "batch").astype(jnp.float32),
        lax.psum(shard_out.astype(jnp.bfloat16), "batch").astype(jnp.float32),
        lax.psum(shard_heads.astype(jnp.bfloat16), "batch").astype(jnp.float32),
    )
    g_gain_mid = jnp.stack([jnp.stack([layer_norm[0], layer_norm[2]]) for layer_norm in norm_acc])
    g_shift_mid = jnp.stack([jnp.stack([layer_norm[1], layer_norm[3]]) for layer_norm in norm_acc])
    g_gain_out = jnp.stack([layer_norm[4] for layer_norm in norm_acc])
    g_shift_out = jnp.stack([layer_norm[5] for layer_norm in norm_acc])
    return (
        jnp.concatenate(outs_y, 0),
        jnp.concatenate(outs_dx, 0),
        shard_in,
        shard_mid,
        shard_out,
        g_gain_mid,
        g_shift_mid,
        g_gain_out,
        g_shift_out,
        shard_heads[0].T,
    )


MESH = pl.DeviceIdType.MESH
F32, BF16 = jnp.float32, jnp.bfloat16
NN = (((1,), (0,)), ((), ()))
NT = (((1,), (1,)), ((), ()))
TN = (((0,), (0,)), ((), ()))
CH = 16
HB = 256

VMEM_BYTES = 63 * 1024 * 1024
PIECES = {"H": 4, "S0": 6, "S1": 3, "E0": 2, "E1": 2, "R1": 2, "R0": 4}
AGENDA = {
    101: (110, 120, 111, 121),
    102: (112, 122),
    103: (113,),
    104: (130, 123, 219),
    106: (220, 131, 221),
    107: (132,),
    108: (133, 230),
    109: (310, 140, 231, 320),
    110: (311, 141, 240),
    111: (321, 312, 241, 150),
    1: (322,),
    2: (142, 410, 151, 330, 143),
    3: (250, 331, 332, 251, 340),
    4: (519, 341, 152, 342, 529),
    5: (269, 350, 411),
    6: (270, 530, 153, 429, 360),
    7: (
        351, 169, 540, 430, 610, 620, 611, 612, 431, 352, 361, 613, 621, 550, 440, 614, 630, 370, 531, 441, 631,
        622, 271,
    ),
    8: (623, 450, 362, 640, 615, 624, 541, 560, 451, 632, 625, 460, 650, 641),
    9: (
        633, 170, 642, 461, 651, 551, 634, 710, 711, 720, 635, 721, 712, 643, 660, 811, 652, 644, 661, 470, 722,
        810, 730, 713, 723, 645, 561, 653, 371, 372, 171, 172, 731, 812, 740, 732, 654, 662, 663, 655, 733, 741,
        742, 664, 750, 743, 751, 665, 752, 760, 753, 471, 670, 761, 579, 671, 672, 673, 173, 813, 674, 675, 762,
        763, 779,
    ),
}


def dot(left, right, dims=NN):
    return lax.dot_general(left, right, dims, preferred_element_type=F32)


def along(column, lanes):
    return column if lanes == 128 else jnp.concatenate([column] * (lanes // 128), axis=1)


def sigmoid(v):
    return 0.5 * jnp.tanh(0.5 * v) + 0.5


def fold8(block):
    total = block[0:8]
    for at in range(8, block.shape[0], 8):
        total = total + block[at : at + 8]
    return total


def shifted(block, by):
    rows, lanes = block.shape
    grouped = block.reshape(rows // FRAME, FRAME, lanes)
    pixel = lax.broadcasted_iota(jnp.int32, grouped.shape, 1)
    moved = pltpu.roll(grouped, by % FRAME, 1)
    keep = pixel > 0 if by == 1 else pixel < FRAME - 1
    return jnp.where(keep, moved, 0.0).reshape(rows, lanes)


def loop(n, body, start=0):
    def step(i, c):
        body(i)
        return c

    lax.fori_loop(start, n, step, 0, unroll=4 if n % 4 == 0 and n >= 8 else 1)


def block_kernel(
    dims,
    act_in, thr_in, cot_in, bucket_ref, wr_in, ws_in, we_in, wh_in, gm_in, sm_in, go_in, so_in,
    y_out, dx_out, gr_out, gs_out, ge_out, gh_out, ggm_out, gsm_out, ggo_out, gso_out, zc_far, slc_far,
    wr, ws, we, wh, entry, wide_f, thr, cot, cot_t, act, za, sla, actb, zb, slb, zc, slc,
    mid_f, taps_f, dcv, dcs, dred, gia, gib, gic, count, pay, part, near, far,
    ger, gs, recv_h, recv_s, recv_e, recv_r, relay,
    gm_ref, sm_ref, go_ref, so_ref, valid_ref, ggm_ref, gsm_ref, ggo_ref, gso_ref,
    load_sem, near_send, near_recv, far_send, far_recv, halo_send, halo_recv, relay_send, relay_recv,
    out_sem, rs_sem,
):
    wide, batch, rows, D, C, H = dims
    my_w = lax.axis_index("wide")
    my_b = lax.axis_index("batch")
    Q = D // 4
    M = 2 * rows
    dexp = thr

    def span(m):
        return pl.ds(pl.multiple_of(m * rows, rows), rows)

    def chunk(m, i):
        return pl.ds(pl.multiple_of(m * rows + i * CH, CH), CH)

    def load(src, dst, index):
        return pltpu.make_async_copy(src, dst, load_sem.at[index])

    def load_wr(l):
        return load(wr_in.at[l], wr, 0)

    def load_ws(l):
        return load(ws_in.at[l], ws, 1)

    def load_we(l):
        return load(we_in.at[l], we, 2)

    load_act = load(act_in, entry.at[0], 3)
    load_wh = load(wh, wh, 4)
    load_thr = load(thr_in, thr, 5)
    load_cot = load(cot_in, cot, 6)
    load_small = [
        load(src, dst, 7 + i)
        for i, (src, dst) in enumerate(
            ((gm_in, gm_ref), (sm_in, sm_ref), (go_in, go_ref), (so_in, so_ref))
        )
    ]
    load_act.start()
    load_wr(0).start()
    for copy in load_small:
        copy.start()

    pixel = lax.broadcasted_iota(jnp.int32, (FRAME, 128), 0)

    def mark_valid(image):
        kind = bucket_ref[image // (rows // FRAME), lax.rem(image, rows // FRAME)]
        height, width = jnp.int32(ROW_TABLE[0]), jnp.int32(COL_TABLE[0])
        for index in range(1, len(ROW_TABLE)):
            height = jnp.where(kind == index, ROW_TABLE[index], height)
            width = jnp.where(kind == index, COL_TABLE[index], width)
        limit = jnp.where(my_w < height, width, 0)
        valid_ref[pl.ds(pl.multiple_of(image * FRAME, FRAME), FRAME), :] = (pixel < limit).astype(F32)

    loop(M // FRAME, mark_valid)

    for side in (0, 2):
        for l in range(2):
            act[l, side] = jnp.zeros(act.shape[2:], BF16)
        dcv[side // 2] = jnp.zeros(dcv.shape[1:], BF16)

    barrier = pltpu.get_barrier_semaphore()
    for step in range(1, wide):
        pl.semaphore_signal(barrier, inc=1, device_id=(my_b, lax.rem(my_w + step, wide)), device_id_type=MESH)
    for step in range(1, batch):
        pl.semaphore_signal(barrier, inc=1, device_id=(lax.rem(my_b + step, batch), my_w), device_id_type=MESH)

    def near_copy(k, m, step, lanes):
        return pltpu.make_async_remote_copy(
            src_ref=pay.at[k, m, :, pl.ds(0, lanes)],
            dst_ref=near.at[k, m, my_w, :, pl.ds(0, lanes)],
            send_sem=near_send.at[k, m],
            recv_sem=near_recv.at[k, m],
            device_id=(my_b, lax.rem(my_w + step, wide)),
            device_id_type=MESH,
        )

    def far_copy(k, m, step, lanes):
        return pltpu.make_async_remote_copy(
            src_ref=part.at[k, m, :, pl.ds(0, lanes)],
            dst_ref=far.at[k, m, my_b, :, pl.ds(0, lanes)],
            send_sem=far_send.at[k, m],
            recv_sem=far_recv.at[k, m],
            device_id=(lax.rem(my_b + step, batch), my_w),
            device_id_type=MESH,
        )

    def whole_sum(block, *sems):
        for sem in sems:
            pltpu.make_async_copy(block, block, sem).wait()

    def sum_start(k, m, lanes):
        for step in range(1, wide):
            near_copy(k, m, step, lanes).start()
        near[k, m, my_w, :, 0:lanes] = pay[k, m, :, 0:lanes]

    def sum_middle(k, m, lanes):
        whole_sum(near.at[k, m, pl.ds(0, wide - 1), :, pl.ds(0, lanes)], near_send.at[k, m], near_recv.at[k, m])
        total = near[k, m, 0, :, 0:lanes]
        for index in range(1, wide):
            total = total + near[k, m, index, :, 0:lanes]
        part[k, m, :, 0:lanes] = total
        for step in range(1, batch):
            far_copy(k, m, step, lanes).start()
        far[k, m, my_b, :, 0:lanes] = total

    def sum_end(k, m, lanes):
        whole_sum(far.at[k, m, pl.ds(0, batch - 1), :, pl.ds(0, lanes)], far_send.at[k, m], far_recv.at[k, m])
        total = far[k, m, 0, :, 0:lanes]
        for index in range(1, batch):
            total = total + far[k, m, index, :, 0:lanes]
        return total

    def pack(k, m, which, at, width, sums):
        row = jnp.sum(sums, 0, keepdims=True)
        for j in range(row.shape[1] // width):
            index = which * 4 + at // width + j
            pay[k, m, index : index + 1, 0:width] = row[:, j * width : (j + 1) * width]

    def unpack_mid(total, which):
        return jnp.concatenate([total[which * 4 + j : which * 4 + j + 1, 0 : C // 4] for j in range(4)], axis=1)

    W4 = C // 4
    FWD = 2 * W4

    def zero(width):
        return jnp.zeros((8, width), F32)

    def mid_stats(k, m, lanes):
        def body(i, c):
            z = mid_f[chunk(m, i), :]
            v = valid_ref[chunk(m, i), :]
            zw = z * along(v, C)
            return c[0] + fold8(zw), c[1] + fold8(zw * z), c[2] + fold8(v)

        first, second, seen = lax.fori_loop(0, rows // CH, body, (zero(C), zero(C), zero(128)), unroll=4)
        pack(k, m, 0, 0, W4, first)
        pack(k, m, 1, 0, W4, second)
        if lanes == FWD:
            pay[k, m, :, W4:FWD] = jnp.broadcast_to(jnp.sum(seen, 0, keepdims=True), (8, W4))
        sum_start(k, m, lanes)

    def mid_forward(k, l, which, m, lanes, zhat_ref, slope_ref, store, gi_ref):
        total = sum_end(k, m, lanes)
        if lanes == FWD:
            count[m] = jnp.broadcast_to(1.0 / total[0:1, W4:FWD], (8, 128))
        rn = along(count[m, 0:1, :], C)
        mean = unpack_mid(total, 0) * rn
        inv = lax.rsqrt(unpack_mid(total, 1) * rn - mean * mean + EPS)
        gain = gm_ref[l, which : which + 1, :]
        shift = sm_ref[l, which : which + 1, :]
        gi_ref[l, m, 0:1, :] = gain * inv

        def body(i):
            at = chunk(m, i)
            v = along(valid_ref[at, :], C)
            zhat = (mid_f[at, :] - mean) * inv
            value = gain * zhat + shift
            s = sigmoid(value)
            zhat_ref[l, at, :] = zhat.astype(BF16)
            slope_ref[l, at, :] = (s * (1.0 + value * (1.0 - s)) * v).astype(BF16)
            store(at, (value * s * v).astype(BF16))

        loop(rows // CH, body)

    def mid_back_sums(k, l, m, zhat_ref, slope_ref):
        def body(i, c):
            at = chunk(m, i)
            d = mid_f[at, :].astype(BF16).astype(F32) * slope_ref[l, at, :].astype(F32)
            mid_f[at, :] = d
            return c[0] + fold8(d), c[1] + fold8(d * zhat_ref[l, at, :].astype(F32))

        first, second = lax.fori_loop(0, rows // CH, body, (zero(C), zero(C)), unroll=4)
        pack(k, m, 0, 0, W4, first)
        pack(k, m, 1, 0, W4, second)
        sum_start(k, m, W4)

    def mid_back(k, l, which, m, zhat_ref, gi_ref, store):
        total = sum_end(k, m, W4)
        sd, sz = unpack_mid(total, 0), unpack_mid(total, 1)
        gsm_ref[l, which : which + 1, :] += sd
        ggm_ref[l, which : which + 1, :] += sz
        rn = along(count[m, 0:1, :], C)
        sd, sz = sd * rn, sz * rn
        gi = gi_ref[l, m, 0:1, :]

        def body(i):
            at = chunk(m, i)
            v = along(valid_ref[at, :], C)
            zhat = zhat_ref[l, at, :].astype(F32)
            store(at, v * gi * (mid_f[at, :] - (sd + zhat * sz)))

        loop(rows // CH, body)

    low, high = wide // 2 - 1, wide // 2

    def halo(buffers, m, down):
        side = 0 if down else 1
        return pltpu.make_async_remote_copy(
            src_ref=buffers[1].at[span(m), :],
            dst_ref=buffers[0 if down else 2].at[span(m), :],
            send_sem=halo_send.at[m, side],
            recv_sem=halo_recv.at[m, side],
            device_id=(my_b, my_w + 1 if down else my_w - 1),
            device_id_type=MESH,
        )

    def halo_out(buffers, down):
        side = 0 if down else 1
        return pltpu.make_async_remote_copy(
            src_ref=buffers[1].at[span(1), :],
            dst_ref=relay,
            send_sem=halo_send.at[1, side],
            recv_sem=relay_recv,
            device_id=(my_b, wide - 1 if down else 0),
            device_id_type=MESH,
        )

    def halo_on(buffers, down):
        side = 0 if down else 1
        return pltpu.make_async_remote_copy(
            src_ref=relay,
            dst_ref=buffers[0 if down else 2].at[span(1), :],
            send_sem=relay_send,
            recv_sem=halo_recv.at[1, side],
            device_id=(my_b, high if down else low),
            device_id_type=MESH,
        )

    def halo_start(buffers, m):
        around_down = (my_w == low) & (m == 1)
        around_up = (my_w == high) & (m == 1)

        @pl.when((my_w < wide - 1) & jnp.logical_not(around_down))
        def _():
            halo(buffers, m, True).start()

        @pl.when(around_down)
        def _():
            halo_out(buffers, True).start()

        @pl.when((my_w > 0) & jnp.logical_not(around_up))
        def _():
            halo(buffers, m, False).start()

        @pl.when(around_up)
        def _():
            halo_out(buffers, False).start()

    def halo_pass(buffers):
        @pl.when(my_w == wide - 1)
        def _():
            halo_out(buffers, True).wait_recv()
            halo_on(buffers, True).start()

        @pl.when(my_w == 0)
        def _():
            halo_out(buffers, False).wait_recv()
            halo_on(buffers, False).start()

    def halo_wait(buffers, m):
        @pl.when(my_w < wide - 1)
        def _():
            halo(buffers, m, True).wait_send()
            halo(buffers, m, False).wait_recv()

        @pl.when(my_w > 0)
        def _():
            halo(buffers, m, False).wait_send()
            halo(buffers, m, True).wait_recv()

        @pl.when((m == 1) & ((my_w == 0) | (my_w == wide - 1)))
        def _():
            halo_on(buffers, True).wait_send()

    def heads(j):
        cols = pl.ds(pl.multiple_of(j * HB, HB), HB)
        for t in range(TASKS):
            taps_f[t, :, 0:HB] = dot(cot[:, t * HEAD : (t + 1) * HEAD], wh[j, t * HEAD : (t + 1) * HEAD, :])

        def body(i):
            at = pl.ds(pl.multiple_of(i * CH, CH), CH)
            values = [taps_f[t, at, 0:HB] for t in range(TASKS)]
            total = values[0] + values[1] + values[2]
            size = jnp.abs(values[0]) + jnp.abs(values[1]) + jnp.abs(values[2])
            keep = 0.5 * (1.0 + total / jnp.maximum(size, FLOOR))
            offset = SHARP * (keep - thr[at, cols].astype(F32))
            up = sigmoid(offset)
            down = 1.0 - up
            merged = jnp.zeros_like(total)
            for value in values:
                merged = merged + jnp.where(value > 0, up, down) * value
            thr[at, cols] = merged.astype(BF16)

        loop(2 * rows // CH, body)

    T = 256
    core, my_x, my_y = lax.rem(my_w, 2), lax.rem(my_w // 2, 2), my_w // 4
    to_core, to_x, to_y = 1 - 2 * core, 2 - 4 * my_x, 4 - 8 * my_y
    first = to_x * (1 - core) + to_y * core
    second = to_x * core + to_y * (1 - core)
    twin = my_w + to_core
    own = [my_w + to_x + to_y, my_w + first, my_w + second, my_w]
    theirs = [twin + to_x + to_y, twin + second, twin + first, twin]
    inner = (my_b == 1) | (my_b == 2)
    outer = (my_b == 0) | (my_b == 3)

    def tall(s):
        return pl.ds(pl.multiple_of(s * T, T), T)

    def grad_tall(held, lhs, rhs, mine):
        def body(i):
            s = 2 * i + (core if mine else 1 - core)
            held[tall(s), :] = dot(lhs[:, tall(s)], rhs, TN).astype(BF16)

        loop(wide // 2, body)

    def grad_heads(mine):
        def body(i):
            s = 2 * i + (core if mine else 1 - core)
            wh[s] = dot(cot_t[...], entry[2, :, tall(s)]).astype(BF16)

        loop(wide // 2, body)

    def grad_spatial(l, row_offset):
        def body(half):
            product = dot(act[l, row_offset, :, tall(half)], dcs[...], TN).astype(BF16)
            for c in range(3):
                base = pl.multiple_of((3 * row_offset + c) * C + half * T, T)
                gs[pl.ds(base, T), :] = product[:, c * C : (c + 1) * C]

        loop(C // T, body)

    def add_into(dst, src, n):
        step = 32

        def body(i):
            at = pl.ds(pl.multiple_of(i * step, step), step)
            dst[at, :] = dst[at, :] + src[at, :]

        loop(n // step, body)

    class Reduce:
        def __init__(self, kind, piece, some, recv_a, recv, final, n, sub, out):
            self.kind, self.piece, self.some, self.recv_a, self.recv, self.final = kind, piece, some, recv_a, recv, final
            self.n, self.sub, self.out = n, sub, out
            self.size = n // sub
            self.sem = rs_sem.at[pl.ds(sum(4 + 5 * k for k in list(PIECES.values())[:kind]), 4 + 5 * sub)]

        def rows_of(self, ref, j):
            return ref.at[pl.ds(j * self.size, self.size), :]

        def send(self, src, dst, send_sem, recv_sem, to):
            pltpu.make_async_remote_copy(
                src_ref=src, dst_ref=dst, send_sem=send_sem, recv_sem=recv_sem, device_id=to, device_id_type=MESH
            ).start()

        def wait(self, sem, rows):
            pltpu.make_async_copy(self.some(rows), self.some(rows), sem).wait()

        def piece_sem(self, j, which):
            return self.sem.at[4 + 5 * j + which]

        def a(self, parts=(0, 1, 2, 3)):
            for p in parts:
                self.send(self.piece(theirs[p]), self.recv_a(p), self.sem.at[0], self.sem.at[1], (my_b, twin))

        def p(self, j):
            if j == 0:
                self.wait(self.sem.at[1], 4 * self.n)
            for p in range(4):
                add_into(self.rows_of(self.piece(own[p]), j), self.rows_of(self.recv_a(p), j), self.size)

        def b(self, j):
            for i in range(2):
                src = self.rows_of(self.piece(own[i]), j)
                self.send(src, self.recv(i, j), self.sem.at[0], self.piece_sem(j, 0), (my_b, my_w + first))

        def c(self, j):
            self.wait(self.piece_sem(j, 0), 2 * self.size)
            for i in range(2):
                mine = self.rows_of(self.piece(own[2 + i]), j)
                add_into(mine, self.recv(i, j), self.size)
                if i == 0:
                    self.send(mine, self.recv(2, j), self.sem.at[0], self.piece_sem(j, 1), (my_b, my_w + second))

        def d(self, j):
            self.wait(self.piece_sem(j, 1), self.size)
            final, mine, other = self.final(j), self.rows_of(self.piece(own[3]), j), self.recv(2, j)

            def body(i):
                at = pl.ds(pl.multiple_of(i * 32, 32), 32)
                final[at, :] = mine[at, :] + other[at, :]

            loop(self.size // 32, body)

            @pl.when(outer)
            def _():
                to = (1 + my_b // 2, my_w)
                self.send(final, self.recv(3, j), self.sem.at[2], self.piece_sem(j, 2), to)

        def e(self, j):
            @pl.when(inner)
            def _():
                self.wait(self.piece_sem(j, 2), self.size)
                add_into(self.final(j), self.recv(3, j), self.size)
                to = (3 - my_b, my_w)
                self.send(self.final(j), self.recv(4, j), self.piece_sem(j, 4), self.piece_sem(j, 3), to)

        def f(self, j):
            @pl.when(inner)
            def _():
                self.wait(self.piece_sem(j, 4), self.size)
                self.wait(self.piece_sem(j, 3), self.size)
                add_into(self.final(j), self.recv(4, j), self.size)
                to = (3 * (my_b - 1), my_w)
                self.send(self.final(j), self.recv(3, j), self.sem.at[2], self.piece_sem(j, 2), to)

        def g(self, j):
            dst = self.out.at[pl.ds(j * self.size, self.size), :]

            @pl.when(outer)
            def _():
                self.wait(self.piece_sem(j, 2), self.size)
                pltpu.make_async_copy(self.recv(3, j), dst, self.sem.at[3]).start()

            @pl.when(inner)
            def _():
                pltpu.make_async_copy(self.final(j), dst, self.sem.at[3]).start()

        def release(self):
            self.wait(self.sem.at[0], 7 * self.n)

        def close(self):
            self.wait(self.sem.at[2], self.n)
            self.wait(self.sem.at[3], self.n)

    def block(ref, index, n):
        begin, size = n
        return ref.at[pl.ds((index // 4) * T + begin, size), pl.ds((index % 4) * C, C)]

    def make_heads():
        def recv(index, j):
            return recv_h.at[index, pl.ds(j * (H // PIECES["H"]), H // PIECES["H"]), :]

        def recv_a(p):
            return gs.at[pl.ds(p * H, H), pl.ds(0, HB)]

        def some(n):
            return wh.at[pl.ds(0, n // H)] if n % H == 0 else wh.at[0, pl.ds(0, n), :]

        return Reduce(0, lambda s: wh.at[s], some, recv_a, recv, lambda j: recv(2, j), H, PIECES["H"], gh_out)

    def make_spatial(l):
        n = 9 * C // wide
        sub = PIECES[f"S{l}"]
        size = n // sub

        def recv(index, j):
            if l == 1 or index < 2:
                return recv_s.at[4 + index, pl.ds(j * size, size), :]
            third, begin = j * size // 192, j * size % 192
            if index == 2:
                return block(zc, 5 + third, (begin, size))
            return slc.at[pl.ds((index - 3) * 192 + begin, size), pl.ds(third * C, C)]

        def piece(s):
            return gs.at[pl.ds(pl.multiple_of(s * n, 64), n), :]

        return Reduce(
            1 + l, piece, lambda n: gs.at[pl.ds(0, n), :], lambda p: recv_s.at[p], recv, lambda j: recv(2, j), n, sub, gs_out.at[l]
        )

    def make_tall(kind, held, l, recv_a, recv, final, sub, out):
        def rows_of(j):
            return (j * (T // sub), T // sub)

        return Reduce(
            kind,
            lambda s: held.at[tall(s), :],
            lambda n: held.at[pl.ds(0, n), :],
            recv_a,
            lambda index, j: recv(index, rows_of(j)),
            lambda j: final(rows_of(j)),
            T, sub, out.at[l],
        )

    def shared_a(p):
        return block(entry.at[2], p, (0, T))

    def recv_a_reduce1(p):
        return act.at[1, p // 2, pl.ds((p % 2) * T, T), :]

    def recv_expand1(index, n):
        return block(entry.at[2], 4 + index, n) if index < 3 else recv_e.at[index - 3, pl.ds(*n), :]

    def recv_expand0(index, n):
        return block(entry.at[2], 4 + index, n) if index < 3 else zb.at[1, pl.ds((index - 3) * T + n[0], n[1]), :]

    def recv_reduce1(index, n):
        if index < 2:
            return slc.at[pl.ds(index * T + n[0], n[1]), pl.ds(3 * C, C)]
        return block(entry.at[2], 7, n) if index == 2 else recv_r.at[index - 3, pl.ds(*n), :]

    def recv_reduce0(index, n):
        return block(zc, index, n)

    table = {"H": make_heads(), "S1": make_spatial(1), "S0": make_spatial(0)}
    table["E1"] = make_tall(4, ger, 1, shared_a, recv_expand1, lambda n: recv_e.at[2, pl.ds(*n), :], PIECES["E1"], ge_out)
    table["E0"] = make_tall(3, ger, 0, shared_a, recv_expand0, lambda n: slb.at[1, pl.ds(*n), :], PIECES["E0"], ge_out)
    table["R1"] = make_tall(5, wr, 1, recv_a_reduce1, recv_reduce1, lambda n: recv_reduce1(2, n), PIECES["R1"], gr_out)
    table["R0"] = make_tall(6, we, 0, shared_a, recv_reduce0, lambda n: recv_reduce0(2, n), PIECES["R0"], gr_out)

    def input_grad(q):
        lanes = slice(q * Q, (q + 1) * Q)
        for m in range(2):
            taps_f[0, span(m), 0:Q] = dot(dred[span(m), :], wr[lanes, :], NT)

        def body(i):
            at = pl.ds(pl.multiple_of(i * CH, CH), CH)
            dexp[at, lanes] = (taps_f[0, at, 0:Q] + wide_f[at, lanes]).astype(BF16)

        loop(M // CH, body)
        pltpu.make_async_copy(dexp.at[:, lanes], dx_out.at[:, lanes], out_sem.at[1]).start()

    by_number = [None] + [table[name] for name in ("H", "E1", "S1", "R1", "E0", "S0", "R0")]

    def point(place):
        for entry_code in AGENDA.get(place, ()):
            item, step, piece_index = entry_code // 100, entry_code // 10 % 10, entry_code % 10
            if item == 8:
                input_grad(piece_index)
                continue
            reduce = by_number[item]
            todo = (None, reduce.p, reduce.b, reduce.c, reduce.d, reduce.e, reduce.f, reduce.g)[step]
            for j in range(reduce.sub) if piece_index == 9 else (piece_index,):
                todo(j)

    spill_zc = pltpu.make_async_copy(zc, zc_far, out_sem.at[2])
    spill_slc = pltpu.make_async_copy(slc, slc_far, out_sem.at[3])
    back_zc = pltpu.make_async_copy(zc_far, zc, out_sem.at[2])
    back_slc = pltpu.make_async_copy(slc_far, slc, out_sem.at[3])
    ggm_ref[...] = jnp.zeros_like(ggm_ref)
    gsm_ref[...] = jnp.zeros_like(gsm_ref)
    ggo_ref[...] = jnp.zeros_like(ggo_ref)
    gso_ref[...] = jnp.zeros_like(gso_ref)
    load_act.wait()
    for copy in load_small:
        copy.wait()

    for l in range(2):
        load_wr(l).wait()
        if l == 0:
            load_cot.start()
            for j in range(D // HB):
                load(wh_in.at[:, pl.ds(j * HB, HB)], wh.at[j], 4).start()
            load_thr.start()
            load_ws(0).start()
            load_we(0).start()

        def reduce_in(m):
            mid_f[span(m), :] = dot(entry[l, span(m), :], wr[...])
            if l == 0:
                pl.when(m == 0)(lambda: pl.semaphore_wait(barrier, wide + batch - 2))
            mid_stats(0, m, FWD if l == 0 else W4)

        loop(2, reduce_in)
        if l == 0:
            load_wr(1).start()
            load_cot.wait()
            load_wh.wait()
            load_thr.wait()
            cot_t[...] = cot[...].T
        heads(4 * l)
        loop(2, lambda m: sum_middle(0, m, FWD if l == 0 else W4))
        heads(4 * l + 1)
        load_ws(l).wait()

        def conv_own(m):
            def store(at, value):
                act[l, 1, at, :] = value

            mid_forward(0, l, 0, m, FWD if l == 0 else W4, za, sla, store, gia)
            halo_start([act.at[l, r] for r in range(3)], m)
            for c in range(3):
                taps_f[c, span(m), :] = dot(act[l, 1, span(m), :], ws[(3 + c) * C : (4 + c) * C, :])

        loop(2, conv_own)
        halo_pass([act.at[l, r] for r in range(3)])

        def conv_rest(m):
            halo_wait([act.at[l, r] for r in range(3)], m)
            for c in range(3):
                taps_f[c, span(m), :] += dot(act[l, 0, span(m), :], ws[c * C : (c + 1) * C, :]) + dot(
                    act[l, 2, span(m), :], ws[(6 + c) * C : (7 + c) * C, :]
                )

            def body(i):
                at = chunk(m, i)
                mid_f[at, :] = taps_f[1, at, :] + shifted(taps_f[0, at, :], 1) + shifted(taps_f[2, at, :], -1)

            loop(rows // CH, body)
            mid_stats(1, m, W4)

        loop(2, conv_rest)
        if l == 0:
            load_ws(1).start()
        heads(4 * l + 2)
        loop(2, lambda m: sum_middle(1, m, W4))
        heads(4 * l + 3)
        load_we(l).wait()

        def expand(m):
            def store(at, value):
                actb[l, at, :] = value

            mid_forward(1, l, 1, m, W4, zb, slb, store, gib)
            for q in range(4):
                lanes = slice(q * Q, (q + 1) * Q)
                wide_f[span(m), lanes] = dot(actb[l, span(m), :], we[lanes, :], NT)

                def body(i, c):
                    z = wide_f[chunk(m, i), lanes]
                    zw = z * along(valid_ref[chunk(m, i), :], Q)
                    return c[0] + fold8(zw), c[1] + fold8(zw * z)

                first, second = lax.fori_loop(0, rows // CH, body, (zero(Q), zero(Q)), unroll=4)
                pack(2, m, 0, q * Q, Q, first)
                pack(2, m, 1, q * Q, Q, second)
            sum_start(2, m, Q)

        loop(2, expand)
        if l == 0:
            load_we(1).start()
        loop(2, lambda m: sum_middle(2, m, Q))

        def output(m):
            total = sum_end(2, m, Q)
            rn = along(count[m, 0:1, :], Q)
            for q in range(4):
                lanes = slice(q * Q, (q + 1) * Q)
                mean = total[q : q + 1] * rn
                inv = lax.rsqrt(total[4 + q : 5 + q] * rn - mean * mean + EPS)
                gain = go_ref[l : l + 1, lanes]
                shift = so_ref[l : l + 1, lanes]
                gic[l, m, 0:1, lanes] = gain * inv

                def body(i, c):
                    at = chunk(m, i)
                    v = along(valid_ref[at, :], Q)
                    zhat = (wide_f[at, lanes] - mean) * inv
                    kept = pl.ds(pl.multiple_of(q * M + m * rows + i * CH, CH), CH)
                    below = entry[l, at, lanes].astype(F32)
                    if l == 1:
                        below = below + ger[kept, :].astype(F32)
                    before = gain * zhat + shift + below
                    s = sigmoid(before)
                    value = before * s * v
                    slope = s * (1.0 + before * (1.0 - s)) * v
                    zc[at, lanes] = zhat.astype(BF16)
                    slc[at, lanes] = slope.astype(BF16)
                    low = value.astype(BF16)
                    entry[l + 1, at, lanes] = low
                    if l == 0:
                        ger[kept, :] = (value - low.astype(F32)).astype(BF16)
                        return c
                    d = thr[at, lanes].astype(F32) * slope
                    wide_f[at, lanes] = d
                    return c[0] + fold8(d), c[1] + fold8(d * zhat)

                if l == 0:
                    lax.fori_loop(0, rows // CH, body, 0, unroll=4)
                else:
                    first, second = lax.fori_loop(0, rows // CH, body, (zero(Q), zero(Q)), unroll=4)
                    pack(0, m, 0, q * Q, Q, first)
                    pack(0, m, 1, q * Q, Q, second)
            if l == 1:
                sum_start(0, m, Q)

        if l == 1:
            spill_zc.wait()
            spill_slc.wait()
        loop(2, output)
        if l == 0:
            spill_zc.start()
            spill_slc.start()

    store_small = [
        pltpu.make_async_copy(src, dst, out_sem.at[4 + i])
        for i, (src, dst) in enumerate(
            ((ggm_ref, ggm_out), (gsm_ref, gsm_out), (ggo_ref, ggo_out), (gso_ref, gso_out))
        )
    ]
    store_y = pltpu.make_async_copy(entry.at[2], y_out, out_sem.at[0])
    store_y.start()
    back_slc.start()
    grad_heads(False)
    table["H"].a()
    loop(2, lambda m: sum_middle(0, m, Q))
    grad_heads(True)
    store_y.wait()
    point(100)

    for l in (1, 0):
        if l == 0:
            load_we(0).wait()

        def back_out(m):
            total = sum_end(0, m, Q)
            rn = along(count[m, 0:1, :], Q)
            for q in range(4):
                lanes = slice(q * Q, (q + 1) * Q)
                sd, sz = total[q : q + 1], total[4 + q : 5 + q]
                gso_ref[l : l + 1, lanes] += sd
                ggo_ref[l : l + 1, lanes] += sz
                sd, sz = sd * rn, sz * rn
                gi = gic[l, m, 0:1, lanes]

                def body(i):
                    at = chunk(m, i)
                    v = along(valid_ref[at, :], Q)
                    zhat = zc[at, lanes].astype(F32)
                    dexp[at, lanes] = (v * gi * (wide_f[at, lanes] - (sd + zhat * sz))).astype(BF16)

                loop(rows // CH, body)
            mid_f[span(m), :] = dot(dexp[span(m), :], we[...])
            mid_back_sums(1, l, m, zb, slb)

        loop(2, back_out)
        if l == 1:
            load_we(0).start()
            back_zc.start()
        point(100 * l + 1)
        if l == 0:
            table["E1"].release()
        grad_tall(ger, dexp, actb[l], False)
        loop(2, lambda m: sum_middle(1, m, W4))
        point(100 * l + 2)
        table[f"E{l}"].a()
        grad_tall(ger, dexp, actb[l], True)
        point(100 * l + 3)
        if l == 0:
            load_ws(0).wait()

        grad_rows = [dcv.at[0], dcs.at[:, pl.ds(C, C)], dcv.at[1]]

        def back_conv(m):
            def store(at, value):
                low = value.astype(BF16)
                dcs[at, C : 2 * C] = low
                dcs[at, 0:C] = shifted(value, -1).astype(BF16)
                dcs[at, 2 * C : 3 * C] = shifted(value, 1).astype(BF16)

            mid_back(1, l, 1, m, zb, gib, store)
            halo_start(grad_rows, m)
            for c in range(3):
                taps_f[c, span(m), :] = dot(dcs[span(m), C : 2 * C], ws[(3 + c) * C : (4 + c) * C, :], NT)

        loop(2, back_conv)
        halo_pass(grad_rows)
        point(100 * l + 4)
        if l == 0:
            table["S1"].release()
        grad_spatial(l, 1)
        point(100 * l + 5)

        def back_rest(m):
            halo_wait(grad_rows, m)
            for c in range(3):
                taps_f[c, span(m), :] += dot(dcv[0, span(m), :], ws[(6 + c) * C : (7 + c) * C, :], NT) + dot(
                    dcv[1, span(m), :], ws[c * C : (c + 1) * C, :], NT
                )

            def body(i):
                at = chunk(m, i)
                mid_f[at, :] = taps_f[1, at, :] + shifted(taps_f[0, at, :], -1) + shifted(taps_f[2, at, :], 1)

            loop(rows // CH, body)
            mid_back_sums(2, l, m, za, sla)

        loop(2, back_rest)
        if l == 1:
            load_ws(0).start()
        point(100 * l + 6)
        grad_spatial(l, 0)
        if l == 0:
            grad_spatial(l, 2)
            table["S0"].a()
        loop(2, lambda m: sum_middle(2, m, W4))
        point(100 * l + 7)
        if l == 0:
            table["R1"].release()
            load_wr(0).start()
        if l == 1:
            grad_spatial(l, 2)
            table["S1"].a()
        point(100 * l + 8)
        if l == 0:
            load_wr(0).wait()

        if l == 1:
            back_zc.wait()
            back_slc.wait()

        def back_in(m):
            def store(at, value):
                dred[at, :] = value.astype(BF16)

            mid_back(2, l, 0, m, za, gia, store)
            for q in range(4 if l == 1 else 0):
                lanes = slice(q * Q, (q + 1) * Q)
                taps_f[0, span(m), 0:Q] = dot(dred[span(m), :], wr[lanes, :], NT)

                def body(i, c):
                    at = chunk(m, i)
                    d = (taps_f[0, at, 0:Q] + wide_f[at, lanes]) * slc[at, lanes].astype(F32)
                    wide_f[at, lanes] = d
                    return c[0] + fold8(d), c[1] + fold8(d * zc[at, lanes].astype(F32))

                first, second = lax.fori_loop(0, rows // CH, body, (zero(Q), zero(Q)), unroll=4)
                pack(0, m, 0, q * Q, Q, first)
                pack(0, m, 1, q * Q, Q, second)
            if l == 1:
                sum_start(0, m, Q)

        loop(2, back_in)
        if l == 1:
            point(109)
            grad_tall(wr, entry.at[1], dred[...], False)
            loop(2, lambda m: sum_middle(0, m, Q))
            point(110)
            table["R1"].a()
            grad_tall(wr, entry.at[1], dred[...], True)
            point(111)
        else:
            for p in range(4):
                we[tall(theirs[p]), :] = dot(entry[0, :, tall(theirs[p])], dred[...], TN).astype(BF16)
                table["R0"].a((p,))
            grad_tall(we, entry.at[0], dred[...], True)
            for copy in store_small:
                copy.start()
            point(9)

    for copy in store_small:
        copy.wait()
    pltpu.make_async_copy(dexp, dx_out, out_sem.at[1]).wait()
    for name in ("H", "E0", "S0", "R0"):
        table[name].release()
    for item in table.values():
        item.close()


def run_block(act, thr, cot, buckets, w_reduce, w_spatial, w_expand, w_heads, gm, sm, go, so):
    wide, batch = lax.axis_size("wide"), lax.axis_size("batch")
    M, D = act.shape
    C = w_reduce.shape[2]
    H = w_heads.shape[0]
    rows = M // 2
    Q = D // 4
    hbm = pl.BlockSpec(memory_space=pl.ANY)
    V, DMA = pltpu.VMEM, pltpu.SemaphoreType.DMA
    scratch = [
        V((D, C), BF16), V((9 * C, C), BF16), V((D, C), BF16), V((D // HB, H, HB), BF16),
        V((3, M, D), BF16), V((M, D), F32), V((M, D), BF16),
        V((M, H), BF16), V((H, M), BF16),
        V((2, 3, M, C), BF16), V((2, M, C), BF16), V((2, M, C), BF16),
        V((2, M, C), BF16), V((2, M, C), BF16), V((2, M, C), BF16),
        V((M, D), BF16), V((M, D), BF16),
        V((M, C), F32), V((3, M, C), F32),
        V((2, M, C), BF16), V((M, 3 * C), BF16), V((M, C), BF16),
        V((2, 2, 8, C), F32), V((2, 2, 8, C), F32), V((2, 2, 8, D), F32), V((2, 8, 128), F32),
        V((3, 2, 8, Q), F32), V((3, 2, 8, Q), F32),
        V((3, 2, wide, 8, Q), F32), V((3, 2, batch, 8, Q), F32),
        V((D, C), BF16), V((9 * C, C), BF16),
        V((5, H, HB), BF16), V((9, 9 * C // wide, C), BF16), V((3, 256, C), BF16), V((2, 256, C), BF16),
        V((rows, C), BF16),
        V((2, 2, C), F32), V((2, 2, C), F32), V((2, D), F32), V((2, D), F32), V((M, 128), F32),
        V((2, 2, C), F32), V((2, 2, C), F32), V((2, D), F32), V((2, D), F32),
        DMA((12,)), DMA((3, 2)), DMA((3, 2)), DMA((3, 2)), DMA((3, 2)),
        DMA((2, 2)), DMA((2, 2)), DMA, DMA, DMA((8,)), DMA((sum(4 + 5 * k for k in PIECES.values()),)),
    ]
    shape = jax.ShapeDtypeStruct
    return pl.pallas_call(
        functools.partial(block_kernel, (wide, batch, rows, D, C, H)),
        out_shape=[
            shape((M, D), BF16), shape((M, D), BF16),
            shape((2, D // wide, C), BF16), shape((2, 9 * C // wide, C), BF16), shape((2, D // wide, C), BF16), shape((H, D // wide), BF16),
            shape((2, 2, C), F32), shape((2, 2, C), F32), shape((2, D), F32), shape((2, D), F32),
            shape((M, D), BF16), shape((M, D), BF16),
        ],
        in_specs=[hbm] * 3 + [pl.BlockSpec(memory_space=pltpu.SMEM)] + [hbm] * 8,
        out_specs=[hbm] * 12,
        scratch_shapes=scratch,
        compiler_params=pltpu.CompilerParams(
            collective_id=7, has_side_effects=True, vmem_limit_bytes=VMEM_BYTES
        ),
    )(act, thr, cot, buckets, w_reduce, w_spatial, w_expand, w_heads, gm, sm, go, so)


def finish_kernel(n, *refs):
    ins, outs, held, wide, sems, out_sems = refs[:n], refs[n : 2 * n], refs[2 * n : 3 * n], refs[3 * n : -2], refs[-2], refs[-1]
    loads = [pltpu.make_async_copy(ins[i], held[i], sems.at[i]) for i in range(n)]
    for copy in loads:
        copy.start()
    stores = []
    w = 0
    for i in range(n):
        loads[i].wait()
        src = held[i]
        if ins[i].dtype != outs[i].dtype:
            src = wide[w]
            w += 1
            rows = 64
            if len(src.shape) == 2:
                def body(r, src=src, i=i):
                    at = pl.ds(pl.multiple_of(r * rows, rows), rows)
                    src[at, :] = held[i][at, :].astype(F32)

                loop(src.shape[0] // rows, body)
            else:
                for l in range(src.shape[0]):
                    def body(r, src=src, i=i, l=l):
                        at = pl.ds(pl.multiple_of(r * rows, rows), rows)
                        src[l, at, :] = held[i][l, at, :].astype(F32)

                    loop(src.shape[1] // rows, body)
        stores.append(pltpu.make_async_copy(src, outs[i], out_sems.at[i]))
        stores[-1].start()
    for copy in stores:
        copy.wait()


def finish(*arrays):
    hbm = pl.BlockSpec(memory_space=pl.ANY)
    n = len(arrays)
    widened = [a.dtype == BF16 and 2 <= i < 6 for i, a in enumerate(arrays)]
    out = [jax.ShapeDtypeStruct(a.shape, F32 if w else a.dtype) for a, w in zip(arrays, widened)]
    scratch = [pltpu.VMEM(a.shape, a.dtype) for a in arrays]
    scratch += [pltpu.VMEM(a.shape, F32) for a, w in zip(arrays, widened) if w]
    return pl.pallas_call(
        functools.partial(finish_kernel, n),
        out_shape=out,
        in_specs=[hbm] * n,
        out_specs=[hbm] * n,
        scratch_shapes=scratch + [pltpu.SemaphoreType.DMA((n,)), pltpu.SemaphoreType.DMA((n,))],
        compiler_params=pltpu.CompilerParams(vmem_limit_bytes=VMEM_BYTES),
    )(*arrays)


def shards_rows(
    activations, bucket_ids, thresholds, head_cot, w_reduce, w_spatial, w_expand,
    gain_mid, shift_mid, gain_out, shift_out, w_heads,
):
    micro, images, pixels, D = activations.shape
    M = micro * images * pixels
    L, _, C = w_reduce.shape
    H = head_cot.shape[-1]
    y, dx, gr, gs, ge, gh, ggm, gsm, ggo, gso, _, _ = run_block(
        activations.reshape(M, D), thresholds.reshape(M, D), head_cot.reshape(M, H), bucket_ids,
        w_reduce, w_spatial, w_expand, w_heads,
        gain_mid, shift_mid, gain_out, shift_out,
    )
    y, dx, gr, gs, ge, gh, ggm, gsm, ggo, gso = finish(y, dx, gr, gs, ge, gh, ggm, gsm, ggo, gso)

    return (
        y.reshape(activations.shape),
        dx.reshape(activations.shape),
        gr,
        gs,
        ge,
        ggm,
        gsm,
        ggo,
        gso,
        gh,
    )


def solution(mesh):
    placed = (
        P(None, "batch", "wide", None),
        P(None, "batch"),
        P(None, "batch", "wide", None),
        P(None, "batch", "wide", None),
        P(),
        P(),
        P(),
        P(),
        P(),
        P(),
        P(),
        P(),
    )
    def split(*arrays):
        micro, images, pixels, features = arrays[0].shape
        whole_rows = pixels == FRAME and FRAME == lax.axis_size("wide") and lax.axis_size("batch") == 4
        fits = micro == 2 and images * pixels == 256 and features == 2048 and arrays[4].shape[2] == 512
        return (shards_rows if whole_rows and fits else shards)(*arrays)

    return jax.shard_map(
        split,
        mesh=mesh,
        in_specs=placed,
        out_specs=(
            P(None, "batch", "wide", None),
            P(None, "batch", "wide", None),
            P(None, "wide", None),
            P(None, "wide", None),
            P(None, "wide", None),
            P(),
            P(),
            P(),
            P(),
            P(None, "wide"),
        ),
        check_vma=False,
    )
```

```python
import functools

import jax
import jax.numpy as jnp
from jax import lax
from jax.experimental import pallas as pl
from jax.experimental.pallas import tpu as pltpu
from jax.sharding import PartitionSpec as P

HEAD = 256
TASKS = 3
FRAME = 8


EPS = 1e-05
SHARP = 8.0
FLOOR = 0.25
ROW_TABLE = (8, 8, 7, 6, 8, 5, 7, 8)
COL_TABLE = (8, 7, 8, 8, 6, 8, 7, 5)


def silu_slope(values):
    gate_val = jax.nn.sigmoid(values)
    return gate_val * (1.0 + values * (1.0 - gate_val))


def frame_mask(buckets, positions):
    bucket_kinds = jnp.arange(len(ROW_TABLE), dtype=jnp.int32)
    onehot = (buckets[..., None] == bucket_kinds).astype(jnp.int32)
    heights = jnp.sum(onehot * jnp.array(ROW_TABLE, dtype=jnp.int32), -1)
    widths = jnp.sum(onehot * jnp.array(COL_TABLE, dtype=jnp.int32), -1)
    rowpos = positions // FRAME
    colpos = positions % FRAME
    inside = (rowpos < heights[..., None]) & (colpos < widths[..., None])
    return inside.astype(jnp.float32)


def unfold_taps(images):
    padded = jnp.pad(images, ((0, 0), (1, 1), (1, 1), (0, 0)))
    pieces = [
        padded[:, row_off : row_off + FRAME, col_off : col_off + FRAME, :]
        for row_off in range(3)
        for col_off in range(3)
    ]
    return jnp.concatenate(pieces, -1)


def fold_taps(columns, channels):
    total_sum = jnp.zeros(columns.shape[:-1] + (channels,), columns.dtype)
    for tap_index in range(9):
        row_off, col_off = divmod(tap_index, 3)
        tap_part = columns[..., tap_index * channels : (tap_index + 1) * channels]
        padded = jnp.pad(tap_part, ((0, 0), (1, 1), (1, 1), (0, 0)))
        total_sum = (
            total_sum
            + padded[:, 2 - row_off : 2 - row_off + FRAME, 2 - col_off : 2 - col_off + FRAME, :]
        )
    return total_sum


def sum_kernel(wide, batch, x_ref, o_ref, near, far, part, near_send, near_recv, far_send, far_recv):
    my_w = lax.axis_index("wide")
    my_b = lax.axis_index("batch")
    barrier = pltpu.get_barrier_semaphore()
    for step in range(1, wide):
        pl.semaphore_signal(
            barrier, inc=1, device_id=(my_b, lax.rem(my_w + step, wide)), device_id_type=pl.DeviceIdType.MESH
        )
    for step in range(1, batch):
        pl.semaphore_signal(
            barrier, inc=1, device_id=(lax.rem(my_b + step, batch), my_w), device_id_type=pl.DeviceIdType.MESH
        )
    pl.semaphore_wait(barrier, wide + batch - 2)

    def exchange(src, slots, send, recv, count, me, target):
        copies = []
        for step in range(1, count):
            copy = pltpu.make_async_remote_copy(
                src_ref=src,
                dst_ref=slots.at[me],
                send_sem=send.at[step],
                recv_sem=recv.at[step],
                device_id=target(lax.rem(me + step, count)),
                device_id_type=pl.DeviceIdType.MESH,
            )
            copy.start()
            copies.append(copy)
        slots[me] = src[...]
        for copy in copies:
            copy.wait()
        total = slots[0]
        for index in range(1, count):
            total = total + slots[index]
        return total

    part[...] = exchange(x_ref, near, near_send, near_recv, wide, my_w, lambda w: (my_b, w))
    o_ref[...] = exchange(part, far, far_send, far_recv, batch, my_b, lambda b: (b, my_w))


def sum_all(values):
    wide, batch = lax.axis_size("wide"), lax.axis_size("batch")
    block = values.shape
    return pl.pallas_call(
        functools.partial(sum_kernel, wide, batch),
        out_shape=jax.ShapeDtypeStruct(block, jnp.float32),
        in_specs=[pl.BlockSpec(memory_space=pltpu.VMEM)],
        out_specs=pl.BlockSpec(memory_space=pltpu.VMEM),
        scratch_shapes=[
            pltpu.VMEM((wide,) + block, jnp.float32),
            pltpu.VMEM((batch,) + block, jnp.float32),
            pltpu.VMEM(block, jnp.float32),
            pltpu.SemaphoreType.DMA((wide,)),
            pltpu.SemaphoreType.DMA((wide,)),
            pltpu.SemaphoreType.DMA((batch,)),
            pltpu.SemaphoreType.DMA((batch,)),
        ],
        compiler_params=pltpu.CompilerParams(collective_id=block[-1] // 512, has_side_effects=True),
    )(values)


def batch_norm(values, valid_rows, scale_vec, offset_vec):
    weighted = values * valid_rows[..., None]
    sum_first = jnp.sum(weighted, 1)
    sum_second = jnp.sum(weighted * values, 1)
    counts = jnp.sum(valid_rows, 1)
    count_row = jnp.broadcast_to(counts[:, None], sum_first.shape)
    summed = sum_all(jnp.concatenate([sum_first, sum_second, count_row, jnp.zeros_like(sum_first)], 0))
    sum_first, sum_second, counts = summed[0:2], summed[2:4], summed[4:6, 0]
    mean_val = sum_first / counts[:, None]
    spread = sum_second / counts[:, None] - mean_val * mean_val
    inv_std = lax.rsqrt(spread + EPS)
    normed = (values - mean_val[:, None, :]) * inv_std[:, None, :]
    return (normed, scale_vec * normed + offset_vec, inv_std, counts)


def norm_back(grad_out, normed, inv_std, counts, valid_rows, scale_vec):
    sum_grad = jnp.sum(grad_out, 1)
    sum_prod = jnp.sum(grad_out * normed, 1)
    summed = sum_all(jnp.concatenate([sum_grad, sum_prod, sum_grad, sum_prod], 0))
    sum_grad, sum_prod = summed[0:2], summed[2:4]
    centered = (
        grad_out - (sum_grad[:, None, :] + normed * sum_prod[:, None, :]) / counts[:, None, None]
    )
    grad_in = valid_rows[..., None] * scale_vec * inv_std[:, None, :] * centered
    return (grad_in, jnp.sum(sum_prod, 0), jnp.sum(sum_grad, 0))


def forward_layer(layer_in, pix_valid, img_valid, params, layout):
    w_in, w_mid, w_out, scale_a, offset_a, scale_b, offset_b, scale_c, offset_c = params
    groups, per_lane, local_imgs = layout
    span_len = layer_in.shape[0]
    channels = w_in.shape[1]
    entry_low = layer_in.astype(jnp.bfloat16)
    reduced = jnp.einsum("mrd,dc->mrc", entry_low, w_in, preferred_element_type=jnp.float32)
    normed_a, bn_a, inv_a, counts = batch_norm(reduced, pix_valid, scale_a, offset_a)
    act_a = (jax.nn.silu(bn_a) * pix_valid[..., None]).astype(jnp.bfloat16)
    arrived = lax.all_to_all(
        act_a.reshape(span_len, groups, per_lane, channels),
        "wide",
        split_axis=1,
        concat_axis=2,
        tiled=True,
    )
    count_imgs = arrived.shape[1]
    images = arrived.reshape(span_len * count_imgs, FRAME, FRAME, channels)
    columns = unfold_taps(images).reshape(span_len, count_imgs, FRAME * FRAME, 9 * channels)
    conv_out = jnp.einsum("mkpc,co->mkpo", columns, w_mid, preferred_element_type=jnp.float32)
    taps_saved, conv_out = (columns, conv_out)
    taps_saved = taps_saved.reshape(span_len, -1, taps_saved.shape[-1])
    conv_out = conv_out.reshape(span_len, -1, channels)
    normed_b, bn_b, inv_b, unused_counts = batch_norm(conv_out, img_valid, scale_b, offset_b)
    act_b = (jax.nn.silu(bn_b) * img_valid[..., None]).astype(jnp.bfloat16)
    returned = lax.all_to_all(
        act_b.reshape(span_len, local_imgs, FRAME * FRAME, channels),
        "wide",
        split_axis=2,
        concat_axis=1,
        tiled=True,
    ).reshape(span_len, -1, channels)
    expanded = jnp.einsum("mrc,oc->mro", returned, w_out, preferred_element_type=jnp.float32)
    normed_c, bn_c, inv_c, unused_again = batch_norm(expanded, pix_valid, scale_c, offset_c)
    before = bn_c + layer_in
    result = jax.nn.silu(before) * pix_valid[..., None]
    saved = (
        entry_low,
        normed_a,
        bn_a,
        inv_a,
        taps_saved,
        normed_b,
        bn_b,
        inv_b,
        returned,
        normed_c,
        before,
        inv_c,
        counts,
    )
    return (result, saved)


def backward_layer(incoming, saved, pix_valid, img_valid, params, layout):
    w_in, w_mid, w_out, scale_a, offset_a, scale_b, offset_b, scale_c, offset_c = params
    groups, per_lane, local_imgs = layout
    (
        entry_low,
        normed_a,
        bn_a,
        inv_a,
        taps_saved,
        normed_b,
        bn_b,
        inv_b,
        returned,
        normed_c,
        before,
        inv_c,
        counts,
    ) = saved
    span_len = incoming.shape[0]
    channels = w_in.shape[1]
    grad_pre = incoming * pix_valid[..., None] * silu_slope(before)
    grad_c, scale_gc, offset_gc = norm_back(grad_pre, normed_c, inv_c, counts, pix_valid, scale_c)
    grad_c_low = grad_c.astype(jnp.bfloat16)
    g_out = jnp.einsum("mro,mrc->oc", grad_c_low, returned, preferred_element_type=jnp.float32)
    d_returned = jnp.einsum(
        "mro,oc->mrc", grad_c_low, w_out, preferred_element_type=jnp.float32
    ).astype(jnp.bfloat16)
    d_images = lax.all_to_all(
        d_returned.reshape(span_len, groups, per_lane, channels),
        "wide",
        split_axis=1,
        concat_axis=2,
        tiled=True,
    ).reshape(span_len, -1, channels)
    d_bn_b = d_images.astype(jnp.float32) * img_valid[..., None] * silu_slope(bn_b)
    grad_b, scale_gb, offset_gb = norm_back(d_bn_b, normed_b, inv_b, counts, img_valid, scale_b)
    grad_b_low = grad_b.astype(jnp.bfloat16)
    g_mid = jnp.einsum("mrk,mro->ko", taps_saved, grad_b_low, preferred_element_type=jnp.float32)
    d_columns = jnp.einsum("mro,ko->mrk", grad_b_low, w_mid, preferred_element_type=jnp.float32)
    d_act = fold_taps(
        d_columns.reshape(span_len * local_imgs, FRAME, FRAME, 9 * channels), channels
    )
    d_act = d_act.astype(jnp.bfloat16).reshape(span_len, local_imgs, FRAME * FRAME, channels)
    d_pixels = lax.all_to_all(d_act, "wide", split_axis=2, concat_axis=1, tiled=True).reshape(
        span_len, -1, channels
    )
    d_bn_a = d_pixels.astype(jnp.float32) * pix_valid[..., None] * silu_slope(bn_a)
    grad_a, scale_ga, offset_ga = norm_back(d_bn_a, normed_a, inv_a, counts, pix_valid, scale_a)
    grad_a_low = grad_a.astype(jnp.bfloat16)
    g_in = jnp.einsum("mrd,mrc->dc", entry_low, grad_a_low, preferred_element_type=jnp.float32)
    d_entry = jnp.einsum("mrc,dc->mrd", grad_a_low, w_in, preferred_element_type=jnp.float32)
    return (
        d_entry + grad_pre,
        (g_in, g_mid, g_out),
        (scale_ga, offset_ga, scale_gb, offset_gb, scale_gc, offset_gc),
    )


def grad_drop(task_values, limits):
    task_total = task_values[0]
    magnitude = jnp.abs(task_values[0])
    for task_index in range(1, len(task_values)):
        task_total = task_total + task_values[task_index]
        magnitude = magnitude + jnp.abs(task_values[task_index])
    keep_ratio = 0.5 * (1.0 + task_total / jnp.maximum(magnitude, FLOOR))
    upward = jax.nn.sigmoid(SHARP * (keep_ratio - limits))
    downward = jax.nn.sigmoid(SHARP * (limits - keep_ratio))
    merged = jnp.zeros_like(task_total)
    for task_value in task_values:
        merged = merged + jnp.where(task_value > 0, upward, downward) * task_value
    return merged


def add_tuples(left, right):
    return tuple((left_item + right_item for left_item, right_item in zip(left, right)))


def shards(
    activations,
    bucket_ids,
    thresholds,
    head_cot,
    w_reduce,
    w_spatial,
    w_expand,
    gain_mid,
    shift_mid,
    gain_out,
    shift_out,
    w_heads,
):
    micro_total, groups, per_lane, features = activations.shape
    lane_count = lax.axis_size("wide")
    local_imgs = groups // lane_count
    lane_index = lax.axis_index("wide")
    layout = (groups, per_lane, local_imgs)
    pix_positions = lane_index * per_lane + jnp.arange(per_lane, dtype=jnp.int32)
    pix_valid_all = frame_mask(bucket_ids, pix_positions).reshape(micro_total, -1)
    own_ids = lax.dynamic_slice_in_dim(bucket_ids, lane_index * local_imgs, local_imgs, 1)
    img_valid_all = frame_mask(own_ids, jnp.arange(FRAME * FRAME, dtype=jnp.int32)).reshape(
        micro_total, -1
    )
    layer_total = w_reduce.shape[0]
    head_width = head_cot.shape[-1]
    layer_params = [
        (
            w_reduce[layer_index],
            w_spatial[layer_index],
            w_expand[layer_index],
            gain_mid[layer_index, 0],
            shift_mid[layer_index, 0],
            gain_mid[layer_index, 1],
            shift_mid[layer_index, 1],
            gain_out[layer_index],
            shift_out[layer_index],
        )
        for layer_index in range(layer_total)
    ]
    spans = [(0, micro_total)]
    weight_acc = [None] * layer_total
    norm_acc = [None] * layer_total
    heads_acc = jnp.zeros((features, head_width), jnp.float32)
    outs_y = []
    outs_dx = []
    for span_at, span_len in spans:

        def take_span(array):
            return lax.slice_in_dim(array, span_at, span_at + span_len, axis=0)

        pix_valid = take_span(pix_valid_all)
        img_valid = take_span(img_valid_all)
        carried = take_span(activations).reshape(span_len, -1, features).astype(jnp.float32)
        saved_layers = []
        for layer_index in range(layer_total):
            carried, saved = forward_layer(
                carried, pix_valid, img_valid, layer_params[layer_index], layout
            )
            saved_layers.append(saved)
        result_low = carried.astype(jnp.bfloat16)
        outs_y.append(result_low.reshape(span_len, groups, per_lane, features))
        head_grads = take_span(head_cot).reshape(span_len, -1, head_width)
        heads_acc = heads_acc + jnp.einsum(
            "mrd,mrh->dh", result_low, head_grads, preferred_element_type=jnp.float32
        )
        task_values = [
            jnp.einsum(
                "mrh,hd->mrd",
                head_grads[..., task_index * HEAD : (task_index + 1) * HEAD],
                w_heads[task_index * HEAD : (task_index + 1) * HEAD],
                preferred_element_type=jnp.float32,
            )
            for task_index in range(TASKS)
        ]
        limits = take_span(thresholds).reshape(span_len, -1, features).astype(jnp.float32)
        incoming = grad_drop(task_values, limits)
        for layer_index in reversed(range(layer_total)):
            incoming, weight_parts, norm_parts = backward_layer(
                incoming,
                saved_layers[layer_index],
                pix_valid,
                img_valid,
                layer_params[layer_index],
                layout,
            )
            if weight_acc[layer_index] is None:
                weight_acc[layer_index] = weight_parts
                norm_acc[layer_index] = norm_parts
            else:
                weight_acc[layer_index] = add_tuples(weight_acc[layer_index], weight_parts)
                norm_acc[layer_index] = add_tuples(norm_acc[layer_index], norm_parts)
        outs_dx.append(incoming.astype(jnp.bfloat16).reshape(span_len, groups, per_lane, features))
    stack_in = jnp.stack([layer_acc[0] for layer_acc in weight_acc])
    stack_mid = jnp.stack([layer_acc[1] for layer_acc in weight_acc])
    stack_out = jnp.stack([layer_acc[2] for layer_acc in weight_acc])
    shard_in, shard_mid, shard_out, shard_heads = (
        lax.psum_scatter(
            stack_in.astype(jnp.bfloat16), "wide", scatter_dimension=1, tiled=True
        ).astype(jnp.float32),
        lax.psum_scatter(
            stack_mid.astype(jnp.bfloat16), "wide", scatter_dimension=1, tiled=True
        ).astype(jnp.float32),
        lax.psum_scatter(
            stack_out.astype(jnp.bfloat16), "wide", scatter_dimension=1, tiled=True
        ).astype(jnp.float32),
        lax.psum_scatter(
            heads_acc[None].astype(jnp.bfloat16), "wide", scatter_dimension=1, tiled=True
        ).astype(jnp.float32),
    )
    shard_in, shard_mid, shard_out, shard_heads = (
        lax.psum(shard_in.astype(jnp.bfloat16), "batch").astype(jnp.float32),
        lax.psum(shard_mid.astype(jnp.bfloat16), "batch").astype(jnp.float32),
        lax.psum(shard_out.astype(jnp.bfloat16), "batch").astype(jnp.float32),
        lax.psum(shard_heads.astype(jnp.bfloat16), "batch").astype(jnp.float32),
    )
    g_gain_mid = jnp.stack([jnp.stack([layer_norm[0], layer_norm[2]]) for layer_norm in norm_acc])
    g_shift_mid = jnp.stack([jnp.stack([layer_norm[1], layer_norm[3]]) for layer_norm in norm_acc])
    g_gain_out = jnp.stack([layer_norm[4] for layer_norm in norm_acc])
    g_shift_out = jnp.stack([layer_norm[5] for layer_norm in norm_acc])
    return (
        jnp.concatenate(outs_y, 0),
        jnp.concatenate(outs_dx, 0),
        shard_in,
        shard_mid,
        shard_out,
        g_gain_mid,
        g_shift_mid,
        g_gain_out,
        g_shift_out,
        shard_heads[0].T,
    )


MESH = pl.DeviceIdType.MESH
F32, BF16 = jnp.float32, jnp.bfloat16
NN = (((1,), (0,)), ((), ()))
NT = (((1,), (1,)), ((), ()))
TN = (((0,), (0,)), ((), ()))
CH = 16
HB = 256

VMEM_BYTES = 63 * 1024 * 1024
PIECES = {"H": 4, "S0": 6, "S1": 3, "E0": 2, "E1": 2, "R1": 2, "R0": 8}
AGENDA = {
    101: (110, 120, 111, 121),
    102: (112, 122),
    103: (113,),
    104: (130, 123, 219),
    106: (220, 131, 221),
    107: (132,),
    108: (133, 230),
    109: (310, 140, 231, 320),
    110: (311, 141, 240),
    111: (321, 312, 241, 150),
    1: (322,),
    2: (142, 410, 151, 330, 143),
    3: (250, 331, 332, 251, 340),
    4: (519, 341, 152, 342, 529),
    5: (269, 350, 411),
    6: (270, 530, 153, 429, 360),
    7: (
        351, 169, 540, 430, 610, 620, 611, 612, 431, 352, 361, 613, 621, 550, 440, 614, 630, 370, 531, 441, 631,
        622, 271,
    ),
    8: (623, 450, 362, 640, 615, 624, 541, 560, 451, 632, 625, 460, 650, 641),
    9: (
        633, 170, 642, 461, 651, 551, 634, 710, 711, 712, 713, 720, 721, 635, 722, 723, 714, 715, 643, 660, 811,
        652, 644, 661, 470, 724, 725, 810, 730, 731, 716, 717, 726, 727, 645, 561, 653, 371, 372, 171, 172, 732,
        733, 812, 740, 741, 734, 735, 654, 662, 663, 655, 736, 737, 742, 743, 744, 745, 664, 750, 751, 746, 747,
        752, 753, 665, 754, 755, 760, 761, 756, 757, 471, 670, 762, 763, 579, 671, 672, 673, 173, 813, 674, 675,
        764, 765, 766, 767, 779,
    ),
}


def dot(left, right, dims=NN):
    return lax.dot_general(left, right, dims, preferred_element_type=F32)


def along(column, lanes):
    return column if lanes == 128 else jnp.concatenate([column] * (lanes // 128), axis=1)


def sigmoid(v):
    return 0.5 * jnp.tanh(0.5 * v) + 0.5


def fold8(block):
    total = block[0:8]
    for at in range(8, block.shape[0], 8):
        total = total + block[at : at + 8]
    return total


def shifted(block, by):
    rows, lanes = block.shape
    grouped = block.reshape(rows // FRAME, FRAME, lanes)
    pixel = lax.broadcasted_iota(jnp.int32, grouped.shape, 1)
    moved = pltpu.roll(grouped, by % FRAME, 1)
    keep = pixel > 0 if by == 1 else pixel < FRAME - 1
    return jnp.where(keep, moved, 0.0).reshape(rows, lanes)


def loop(n, body, start=0):
    def step(i, c):
        body(i)
        return c

    lax.fori_loop(start, n, step, 0, unroll=4 if n % 4 == 0 and n >= 8 else 1)


def block_kernel(
    dims,
    act_in, thr_in, cot_in, bucket_ref, wr_in, ws_in, we_in, wh_in, gm_in, sm_in, go_in, so_in,
    y_out, dx_out, gr_out, gs_out, ge_out, gh_out, ggm_out, gsm_out, ggo_out, gso_out, zc_far, slc_far,
    wr, ws, we, wh, entry, wide_f, thr, cot, cot_t, act, za, sla, actb, zb, slb, zc, slc,
    mid_f, taps_f, dcv, dcs, dred, gia, gib, gic, count, pay, part, near, far,
    ger, gs, recv_h, recv_s, recv_e, recv_r, relay,
    gm_ref, sm_ref, go_ref, so_ref, valid_ref, ggm_ref, gsm_ref, ggo_ref, gso_ref,
    load_sem, near_send, near_recv, far_send, far_recv, halo_send, halo_recv, relay_send, relay_recv,
    out_sem, rs_sem,
):
    wide, batch, rows, D, C, H = dims
    my_w = lax.axis_index("wide")
    my_b = lax.axis_index("batch")
    Q = D // 4
    M = 2 * rows
    dexp = thr

    def span(m):
        return pl.ds(pl.multiple_of(m * rows, rows), rows)

    def chunk(m, i):
        return pl.ds(pl.multiple_of(m * rows + i * CH, CH), CH)

    def load(src, dst, index):
        return pltpu.make_async_copy(src, dst, load_sem.at[index])

    def load_wr(l):
        return load(wr_in.at[l], wr, 0)

    def load_ws(l):
        return load(ws_in.at[l], ws, 1)

    def load_we(l):
        return load(we_in.at[l], we, 2)

    load_act = load(act_in, entry.at[0], 3)
    load_wh = load(wh, wh, 4)
    load_thr = load(thr_in, thr, 5)
    load_cot = load(cot_in, cot, 6)
    load_small = [
        load(src, dst, 7 + i)
        for i, (src, dst) in enumerate(
            ((gm_in, gm_ref), (sm_in, sm_ref), (go_in, go_ref), (so_in, so_ref))
        )
    ]
    load_act.start()
    load_wr(0).start()
    for copy in load_small:
        copy.start()

    pixel = lax.broadcasted_iota(jnp.int32, (FRAME, 128), 0)

    def mark_valid(image):
        kind = bucket_ref[image // (rows // FRAME), lax.rem(image, rows // FRAME)]
        height, width = jnp.int32(ROW_TABLE[0]), jnp.int32(COL_TABLE[0])
        for index in range(1, len(ROW_TABLE)):
            height = jnp.where(kind == index, ROW_TABLE[index], height)
            width = jnp.where(kind == index, COL_TABLE[index], width)
        limit = jnp.where(my_w < height, width, 0)
        valid_ref[pl.ds(pl.multiple_of(image * FRAME, FRAME), FRAME), :] = (pixel < limit).astype(F32)

    loop(M // FRAME, mark_valid)

    for side in (0, 2):
        for l in range(2):
            act[l, side] = jnp.zeros(act.shape[2:], BF16)
        dcv[side // 2] = jnp.zeros(dcv.shape[1:], BF16)

    barrier = pltpu.get_barrier_semaphore()
    for step in range(1, wide):
        pl.semaphore_signal(barrier, inc=1, device_id=(my_b, lax.rem(my_w + step, wide)), device_id_type=MESH)
    for step in range(1, batch):
        pl.semaphore_signal(barrier, inc=1, device_id=(lax.rem(my_b + step, batch), my_w), device_id_type=MESH)

    def near_copy(k, m, step, lanes):
        return pltpu.make_async_remote_copy(
            src_ref=pay.at[k, m, :, pl.ds(0, lanes)],
            dst_ref=near.at[k, m, my_w, :, pl.ds(0, lanes)],
            send_sem=near_send.at[k, m],
            recv_sem=near_recv.at[k, m],
            device_id=(my_b, lax.rem(my_w + step, wide)),
            device_id_type=MESH,
        )

    def far_copy(k, m, step, lanes):
        return pltpu.make_async_remote_copy(
            src_ref=part.at[k, m, :, pl.ds(0, lanes)],
            dst_ref=far.at[k, m, my_b, :, pl.ds(0, lanes)],
            send_sem=far_send.at[k, m],
            recv_sem=far_recv.at[k, m],
            device_id=(lax.rem(my_b + step, batch), my_w),
            device_id_type=MESH,
        )

    def whole_sum(block, *sems):
        for sem in sems:
            pltpu.make_async_copy(block, block, sem).wait()

    def sum_start(k, m, lanes):
        for step in range(1, wide):
            near_copy(k, m, step, lanes).start()
        near[k, m, my_w, :, 0:lanes] = pay[k, m, :, 0:lanes]

    def sum_middle(k, m, lanes):
        whole_sum(near.at[k, m, pl.ds(0, wide - 1), :, pl.ds(0, lanes)], near_send.at[k, m], near_recv.at[k, m])
        total = near[k, m, 0, :, 0:lanes]
        for index in range(1, wide):
            total = total + near[k, m, index, :, 0:lanes]
        part[k, m, :, 0:lanes] = total
        for step in range(1, batch):
            far_copy(k, m, step, lanes).start()
        far[k, m, my_b, :, 0:lanes] = total

    def sum_end(k, m, lanes):
        whole_sum(far.at[k, m, pl.ds(0, batch - 1), :, pl.ds(0, lanes)], far_send.at[k, m], far_recv.at[k, m])
        total = far[k, m, 0, :, 0:lanes]
        for index in range(1, batch):
            total = total + far[k, m, index, :, 0:lanes]
        return total

    def pack(k, m, which, at, width, sums):
        row = jnp.sum(sums, 0, keepdims=True)
        for j in range(row.shape[1] // width):
            index = which * 4 + at // width + j
            pay[k, m, index : index + 1, 0:width] = row[:, j * width : (j + 1) * width]

    def unpack_mid(total, which):
        return jnp.concatenate([total[which * 4 + j : which * 4 + j + 1, 0 : C // 4] for j in range(4)], axis=1)

    W4 = C // 4
    FWD = 2 * W4

    def zero(width):
        return jnp.zeros((8, width), F32)

    def mid_stats(k, m, lanes):
        def body(i, c):
            z = mid_f[chunk(m, i), :]
            v = valid_ref[chunk(m, i), :]
            zw = z * along(v, C)
            return c[0] + fold8(zw), c[1] + fold8(zw * z), c[2] + fold8(v)

        first, second, seen = lax.fori_loop(0, rows // CH, body, (zero(C), zero(C), zero(128)), unroll=4)
        pack(k, m, 0, 0, W4, first)
        pack(k, m, 1, 0, W4, second)
        if lanes == FWD:
            pay[k, m, :, W4:FWD] = jnp.broadcast_to(jnp.sum(seen, 0, keepdims=True), (8, W4))
        sum_start(k, m, lanes)

    def mid_forward(k, l, which, m, lanes, zhat_ref, slope_ref, store, gi_ref):
        total = sum_end(k, m, lanes)
        if lanes == FWD:
            count[m] = jnp.broadcast_to(1.0 / total[0:1, W4:FWD], (8, 128))
        rn = along(count[m, 0:1, :], C)
        mean = unpack_mid(total, 0) * rn
        inv = lax.rsqrt(unpack_mid(total, 1) * rn - mean * mean + EPS)
        gain = gm_ref[l, which : which + 1, :]
        shift = sm_ref[l, which : which + 1, :]
        gi_ref[l, m, 0:1, :] = gain * inv

        def body(i):
            at = chunk(m, i)
            v = along(valid_ref[at, :], C)
            zhat = (mid_f[at, :] - mean) * inv
            value = gain * zhat + shift
            s = sigmoid(value)
            zhat_ref[l, at, :] = zhat.astype(BF16)
            slope_ref[l, at, :] = (s * (1.0 + value * (1.0 - s)) * v).astype(BF16)
            store(at, (value * s * v).astype(BF16))

        loop(rows // CH, body)

    def mid_back_sums(k, l, m, zhat_ref, slope_ref):
        def body(i, c):
            at = chunk(m, i)
            d = mid_f[at, :].astype(BF16).astype(F32) * slope_ref[l, at, :].astype(F32)
            mid_f[at, :] = d
            return c[0] + fold8(d), c[1] + fold8(d * zhat_ref[l, at, :].astype(F32))

        first, second = lax.fori_loop(0, rows // CH, body, (zero(C), zero(C)), unroll=4)
        pack(k, m, 0, 0, W4, first)
        pack(k, m, 1, 0, W4, second)
        sum_start(k, m, W4)

    def mid_back(k, l, which, m, zhat_ref, gi_ref, store):
        total = sum_end(k, m, W4)
        sd, sz = unpack_mid(total, 0), unpack_mid(total, 1)
        gsm_ref[l, which : which + 1, :] += sd
        ggm_ref[l, which : which + 1, :] += sz
        rn = along(count[m, 0:1, :], C)
        sd, sz = sd * rn, sz * rn
        gi = gi_ref[l, m, 0:1, :]

        def body(i):
            at = chunk(m, i)
            v = along(valid_ref[at, :], C)
            zhat = zhat_ref[l, at, :].astype(F32)
            store(at, v * gi * (mid_f[at, :] - (sd + zhat * sz)))

        loop(rows // CH, body)

    low, high = wide // 2 - 1, wide // 2

    def halo(buffers, m, down):
        side = 0 if down else 1
        return pltpu.make_async_remote_copy(
            src_ref=buffers[1].at[span(m), :],
            dst_ref=buffers[0 if down else 2].at[span(m), :],
            send_sem=halo_send.at[m, side],
            recv_sem=halo_recv.at[m, side],
            device_id=(my_b, my_w + 1 if down else my_w - 1),
            device_id_type=MESH,
        )

    def halo_out(buffers, down):
        side = 0 if down else 1
        return pltpu.make_async_remote_copy(
            src_ref=buffers[1].at[span(1), :],
            dst_ref=relay,
            send_sem=halo_send.at[1, side],
            recv_sem=relay_recv,
            device_id=(my_b, wide - 1 if down else 0),
            device_id_type=MESH,
        )

    def halo_on(buffers, down):
        side = 0 if down else 1
        return pltpu.make_async_remote_copy(
            src_ref=relay,
            dst_ref=buffers[0 if down else 2].at[span(1), :],
            send_sem=relay_send,
            recv_sem=halo_recv.at[1, side],
            device_id=(my_b, high if down else low),
            device_id_type=MESH,
        )

    def halo_start(buffers, m):
        around_down = (my_w == low) & (m == 1)
        around_up = (my_w == high) & (m == 1)

        @pl.when((my_w < wide - 1) & jnp.logical_not(around_down))
        def _():
            halo(buffers, m, True).start()

        @pl.when(around_down)
        def _():
            halo_out(buffers, True).start()

        @pl.when((my_w > 0) & jnp.logical_not(around_up))
        def _():
            halo(buffers, m, False).start()

        @pl.when(around_up)
        def _():
            halo_out(buffers, False).start()

    def halo_pass(buffers):
        @pl.when(my_w == wide - 1)
        def _():
            halo_out(buffers, True).wait_recv()
            halo_on(buffers, True).start()

        @pl.when(my_w == 0)
        def _():
            halo_out(buffers, False).wait_recv()
            halo_on(buffers, False).start()

    def halo_wait(buffers, m):
        @pl.when(my_w < wide - 1)
        def _():
            halo(buffers, m, True).wait_send()
            halo(buffers, m, False).wait_recv()

        @pl.when(my_w > 0)
        def _():
            halo(buffers, m, False).wait_send()
            halo(buffers, m, True).wait_recv()

        @pl.when((m == 1) & ((my_w == 0) | (my_w == wide - 1)))
        def _():
            halo_on(buffers, True).wait_send()

    def heads(j):
        cols = pl.ds(pl.multiple_of(j * HB, HB), HB)
        for t in range(TASKS):
            taps_f[t, :, 0:HB] = dot(cot[:, t * HEAD : (t + 1) * HEAD], wh[j, t * HEAD : (t + 1) * HEAD, :])

        def body(i):
            at = pl.ds(pl.multiple_of(i * CH, CH), CH)
            values = [taps_f[t, at, 0:HB] for t in range(TASKS)]
            total = values[0] + values[1] + values[2]
            size = jnp.abs(values[0]) + jnp.abs(values[1]) + jnp.abs(values[2])
            keep = 0.5 * (1.0 + total / jnp.maximum(size, FLOOR))
            offset = SHARP * (keep - thr[at, cols].astype(F32))
            up = sigmoid(offset)
            down = 1.0 - up
            merged = jnp.zeros_like(total)
            for value in values:
                merged = merged + jnp.where(value > 0, up, down) * value
            thr[at, cols] = merged.astype(BF16)

        loop(2 * rows // CH, body)

    T = 256
    core, my_x, my_y = lax.rem(my_w, 2), lax.rem(my_w // 2, 2), my_w // 4
    to_core, to_x, to_y = 1 - 2 * core, 2 - 4 * my_x, 4 - 8 * my_y
    first = to_x * (1 - core) + to_y * core
    second = to_x * core + to_y * (1 - core)
    twin = my_w + to_core
    own = [my_w + to_x + to_y, my_w + first, my_w + second, my_w]
    theirs = [twin + to_x + to_y, twin + second, twin + first, twin]
    inner = (my_b == 1) | (my_b == 2)
    outer = (my_b == 0) | (my_b == 3)

    def tall(s):
        return pl.ds(pl.multiple_of(s * T, T), T)

    def grad_tall(held, lhs, rhs, mine):
        def body(i):
            s = 2 * i + (core if mine else 1 - core)
            held[tall(s), :] = dot(lhs[:, tall(s)], rhs, TN).astype(BF16)

        loop(wide // 2, body)

    def grad_heads(mine):
        def body(i):
            s = 2 * i + (core if mine else 1 - core)
            wh[s] = dot(cot_t[...], entry[2, :, tall(s)]).astype(BF16)

        loop(wide // 2, body)

    def grad_spatial(l, row_offset):
        def body(half):
            product = dot(act[l, row_offset, :, tall(half)], dcs[...], TN).astype(BF16)
            for c in range(3):
                base = pl.multiple_of((3 * row_offset + c) * C + half * T, T)
                gs[pl.ds(base, T), :] = product[:, c * C : (c + 1) * C]

        loop(C // T, body)

    def add_into(dst, src, n):
        step = 32

        def body(i):
            at = pl.ds(pl.multiple_of(i * step, step), step)
            dst[at, :] = dst[at, :] + src[at, :]

        loop(n // step, body)

    class Reduce:
        def __init__(self, kind, piece, some, recv_a, recv, final, n, sub, out):
            self.kind, self.piece, self.some, self.recv_a, self.recv, self.final = kind, piece, some, recv_a, recv, final
            self.n, self.sub, self.out = n, sub, out
            self.size = n // sub
            self.sem = rs_sem.at[pl.ds(sum(4 + 5 * k for k in list(PIECES.values())[:kind]), 4 + 5 * sub)]

        def rows_of(self, ref, j):
            return ref.at[pl.ds(j * self.size, self.size), :]

        def send(self, src, dst, send_sem, recv_sem, to):
            pltpu.make_async_remote_copy(
                src_ref=src, dst_ref=dst, send_sem=send_sem, recv_sem=recv_sem, device_id=to, device_id_type=MESH
            ).start()

        def wait(self, sem, rows):
            pltpu.make_async_copy(self.some(rows), self.some(rows), sem).wait()

        def piece_sem(self, j, which):
            return self.sem.at[4 + 5 * j + which]

        def a(self, parts=(0, 1, 2, 3)):
            for p in parts:
                self.send(self.piece(theirs[p]), self.recv_a(p), self.sem.at[0], self.sem.at[1], (my_b, twin))

        def p(self, j):
            if j == 0:
                self.wait(self.sem.at[1], 4 * self.n)
            for p in range(4):
                add_into(self.rows_of(self.piece(own[p]), j), self.rows_of(self.recv_a(p), j), self.size)

        def b(self, j):
            for i in range(2):
                src = self.rows_of(self.piece(own[i]), j)
                self.send(src, self.recv(i, j), self.sem.at[0], self.piece_sem(j, 0), (my_b, my_w + first))

        def c(self, j):
            self.wait(self.piece_sem(j, 0), 2 * self.size)
            for i in range(2):
                mine = self.rows_of(self.piece(own[2 + i]), j)
                add_into(mine, self.recv(i, j), self.size)
                if i == 0:
                    self.send(mine, self.recv(2, j), self.sem.at[0], self.piece_sem(j, 1), (my_b, my_w + second))

        def d(self, j):
            self.wait(self.piece_sem(j, 1), self.size)
            final, mine, other = self.final(j), self.rows_of(self.piece(own[3]), j), self.recv(2, j)

            def body(i):
                at = pl.ds(pl.multiple_of(i * 32, 32), 32)
                final[at, :] = mine[at, :] + other[at, :]

            loop(self.size // 32, body)

            @pl.when(outer)
            def _():
                to = (1 + my_b // 2, my_w)
                self.send(final, self.recv(3, j), self.sem.at[2], self.piece_sem(j, 2), to)

        def e(self, j):
            @pl.when(inner)
            def _():
                self.wait(self.piece_sem(j, 2), self.size)
                add_into(self.final(j), self.recv(3, j), self.size)
                to = (3 - my_b, my_w)
                self.send(self.final(j), self.recv(4, j), self.piece_sem(j, 4), self.piece_sem(j, 3), to)

        def f(self, j):
            @pl.when(inner)
            def _():
                self.wait(self.piece_sem(j, 4), self.size)
                self.wait(self.piece_sem(j, 3), self.size)
                add_into(self.final(j), self.recv(4, j), self.size)
                to = (3 * (my_b - 1), my_w)
                self.send(self.final(j), self.recv(3, j), self.sem.at[2], self.piece_sem(j, 2), to)

        def g(self, j):
            dst = self.out.at[pl.ds(j * self.size, self.size), :]

            @pl.when(outer)
            def _():
                self.wait(self.piece_sem(j, 2), self.size)
                pltpu.make_async_copy(self.recv(3, j), dst, self.sem.at[3]).start()

            @pl.when(inner)
            def _():
                pltpu.make_async_copy(self.final(j), dst, self.sem.at[3]).start()

        def release(self):
            self.wait(self.sem.at[0], 7 * self.n)

        def close(self):
            self.wait(self.sem.at[2], self.n)
            self.wait(self.sem.at[3], self.n)

    def block(ref, index, n):
        begin, size = n
        return ref.at[pl.ds((index // 4) * T + begin, size), pl.ds((index % 4) * C, C)]

    def make_heads():
        def recv(index, j):
            return recv_h.at[index, pl.ds(j * (H // PIECES["H"]), H // PIECES["H"]), :]

        def recv_a(p):
            return gs.at[pl.ds(p * H, H), pl.ds(0, HB)]

        def some(n):
            return wh.at[pl.ds(0, n // H)] if n % H == 0 else wh.at[0, pl.ds(0, n), :]

        return Reduce(0, lambda s: wh.at[s], some, recv_a, recv, lambda j: recv(2, j), H, PIECES["H"], gh_out)

    def make_spatial(l):
        n = 9 * C // wide
        sub = PIECES[f"S{l}"]
        size = n // sub

        def recv(index, j):
            if l == 1 or index < 2:
                return recv_s.at[4 + index, pl.ds(j * size, size), :]
            third, begin = j * size // 192, j * size % 192
            if index == 2:
                return block(zc, 5 + third, (begin, size))
            return slc.at[pl.ds((index - 3) * 192 + begin, size), pl.ds(third * C, C)]

        def piece(s):
            return gs.at[pl.ds(pl.multiple_of(s * n, 64), n), :]

        return Reduce(
            1 + l, piece, lambda n: gs.at[pl.ds(0, n), :], lambda p: recv_s.at[p], recv, lambda j: recv(2, j), n, sub, gs_out.at[l]
        )

    def make_tall(kind, held, l, recv_a, recv, final, sub, out):
        def rows_of(j):
            return (j * (T // sub), T // sub)

        return Reduce(
            kind,
            lambda s: held.at[tall(s), :],
            lambda n: held.at[pl.ds(0, n), :],
            recv_a,
            lambda index, j: recv(index, rows_of(j)),
            lambda j: final(rows_of(j)),
            T, sub, out.at[l],
        )

    def shared_a(p):
        return block(entry.at[2], p, (0, T))

    def recv_a_reduce1(p):
        return act.at[1, p // 2, pl.ds((p % 2) * T, T), :]

    def recv_expand1(index, n):
        return block(entry.at[2], 4 + index, n) if index < 3 else recv_e.at[index - 3, pl.ds(*n), :]

    def recv_expand0(index, n):
        return block(entry.at[2], 4 + index, n) if index < 3 else zb.at[1, pl.ds((index - 3) * T + n[0], n[1]), :]

    def recv_reduce1(index, n):
        if index < 2:
            return slc.at[pl.ds(index * T + n[0], n[1]), pl.ds(3 * C, C)]
        return block(entry.at[2], 7, n) if index == 2 else recv_r.at[index - 3, pl.ds(*n), :]

    def recv_reduce0(index, n):
        return block(zc, index, n)

    table = {"H": make_heads(), "S1": make_spatial(1), "S0": make_spatial(0)}
    table["E1"] = make_tall(4, ger, 1, shared_a, recv_expand1, lambda n: recv_e.at[2, pl.ds(*n), :], PIECES["E1"], ge_out)
    table["E0"] = make_tall(3, ger, 0, shared_a, recv_expand0, lambda n: slb.at[1, pl.ds(*n), :], PIECES["E0"], ge_out)
    table["R1"] = make_tall(5, wr, 1, recv_a_reduce1, recv_reduce1, lambda n: recv_reduce1(2, n), PIECES["R1"], gr_out)
    table["R0"] = make_tall(6, we, 0, shared_a, recv_reduce0, lambda n: recv_reduce0(2, n), PIECES["R0"], gr_out)

    def input_grad(q):
        lanes = slice(q * Q, (q + 1) * Q)
        for m in range(2):
            taps_f[0, span(m), 0:Q] = dot(dred[span(m), :], wr[lanes, :], NT)

        def body(i):
            at = pl.ds(pl.multiple_of(i * CH, CH), CH)
            dexp[at, lanes] = (taps_f[0, at, 0:Q] + wide_f[at, lanes]).astype(BF16)

        loop(M // CH, body)
        pltpu.make_async_copy(dexp.at[:, lanes], dx_out.at[:, lanes], out_sem.at[1]).start()

    by_number = [None] + [table[name] for name in ("H", "E1", "S1", "R1", "E0", "S0", "R0")]

    def point(place):
        for entry_code in AGENDA.get(place, ()):
            item, step, piece_index = entry_code // 100, entry_code // 10 % 10, entry_code % 10
            if item == 8:
                input_grad(piece_index)
                continue
            reduce = by_number[item]
            todo = (None, reduce.p, reduce.b, reduce.c, reduce.d, reduce.e, reduce.f, reduce.g)[step]
            for j in range(reduce.sub) if piece_index == 9 else (piece_index,):
                todo(j)

    spill_zc = pltpu.make_async_copy(zc, zc_far, out_sem.at[2])
    spill_slc = pltpu.make_async_copy(slc, slc_far, out_sem.at[3])
    back_zc = pltpu.make_async_copy(zc_far, zc, out_sem.at[2])
    back_slc = pltpu.make_async_copy(slc_far, slc, out_sem.at[3])
    ggm_ref[...] = jnp.zeros_like(ggm_ref)
    gsm_ref[...] = jnp.zeros_like(gsm_ref)
    ggo_ref[...] = jnp.zeros_like(ggo_ref)
    gso_ref[...] = jnp.zeros_like(gso_ref)
    load_act.wait()
    for copy in load_small:
        copy.wait()

    for l in range(2):
        load_wr(l).wait()
        if l == 0:
            load_cot.start()
            for j in range(D // HB):
                load(wh_in.at[:, pl.ds(j * HB, HB)], wh.at[j], 4).start()
            load_thr.start()
            load_ws(0).start()
            load_we(0).start()

        def reduce_in(m):
            mid_f[span(m), :] = dot(entry[l, span(m), :], wr[...])
            if l == 0:
                pl.when(m == 0)(lambda: pl.semaphore_wait(barrier, wide + batch - 2))
            mid_stats(0, m, FWD if l == 0 else W4)

        loop(2, reduce_in)
        if l == 0:
            load_wr(1).start()
            load_cot.wait()
            load_wh.wait()
            load_thr.wait()
            cot_t[...] = cot[...].T
        heads(4 * l)
        loop(2, lambda m: sum_middle(0, m, FWD if l == 0 else W4))
        heads(4 * l + 1)
        load_ws(l).wait()

        def conv_own(m):
            def store(at, value):
                act[l, 1, at, :] = value

            mid_forward(0, l, 0, m, FWD if l == 0 else W4, za, sla, store, gia)
            halo_start([act.at[l, r] for r in range(3)], m)
            for c in range(3):
                taps_f[c, span(m), :] = dot(act[l, 1, span(m), :], ws[(3 + c) * C : (4 + c) * C, :])

        loop(2, conv_own)
        halo_pass([act.at[l, r] for r in range(3)])

        def conv_rest(m):
            halo_wait([act.at[l, r] for r in range(3)], m)
            for c in range(3):
                taps_f[c, span(m), :] += dot(act[l, 0, span(m), :], ws[c * C : (c + 1) * C, :]) + dot(
                    act[l, 2, span(m), :], ws[(6 + c) * C : (7 + c) * C, :]
                )

            def body(i):
                at = chunk(m, i)
                mid_f[at, :] = taps_f[1, at, :] + shifted(taps_f[0, at, :], 1) + shifted(taps_f[2, at, :], -1)

            loop(rows // CH, body)
            mid_stats(1, m, W4)

        loop(2, conv_rest)
        if l == 0:
            load_ws(1).start()
        heads(4 * l + 2)
        loop(2, lambda m: sum_middle(1, m, W4))
        heads(4 * l + 3)
        load_we(l).wait()

        def expand(m):
            def store(at, value):
                actb[l, at, :] = value

            mid_forward(1, l, 1, m, W4, zb, slb, store, gib)
            for q in range(4):
                lanes = slice(q * Q, (q + 1) * Q)
                wide_f[span(m), lanes] = dot(actb[l, span(m), :], we[lanes, :], NT)

                def body(i, c):
                    z = wide_f[chunk(m, i), lanes]
                    zw = z * along(valid_ref[chunk(m, i), :], Q)
                    return c[0] + fold8(zw), c[1] + fold8(zw * z)

                first, second = lax.fori_loop(0, rows // CH, body, (zero(Q), zero(Q)), unroll=4)
                pack(2, m, 0, q * Q, Q, first)
                pack(2, m, 1, q * Q, Q, second)
            sum_start(2, m, Q)

        loop(2, expand)
        if l == 0:
            load_we(1).start()
        loop(2, lambda m: sum_middle(2, m, Q))

        def output(m):
            total = sum_end(2, m, Q)
            rn = along(count[m, 0:1, :], Q)
            for q in range(4):
                lanes = slice(q * Q, (q + 1) * Q)
                mean = total[q : q + 1] * rn
                inv = lax.rsqrt(total[4 + q : 5 + q] * rn - mean * mean + EPS)
                gain = go_ref[l : l + 1, lanes]
                shift = so_ref[l : l + 1, lanes]
                gic[l, m, 0:1, lanes] = gain * inv

                def body(i, c):
                    at = chunk(m, i)
                    v = along(valid_ref[at, :], Q)
                    zhat = (wide_f[at, lanes] - mean) * inv
                    kept = pl.ds(pl.multiple_of(q * M + m * rows + i * CH, CH), CH)
                    below = entry[l, at, lanes].astype(F32)
                    if l == 1:
                        below = below + ger[kept, :].astype(F32)
                    before = gain * zhat + shift + below
                    s = sigmoid(before)
                    value = before * s * v
                    slope = s * (1.0 + before * (1.0 - s)) * v
                    zc[at, lanes] = zhat.astype(BF16)
                    slc[at, lanes] = slope.astype(BF16)
                    low = value.astype(BF16)
                    entry[l + 1, at, lanes] = low
                    if l == 0:
                        ger[kept, :] = (value - low.astype(F32)).astype(BF16)
                        return c
                    d = thr[at, lanes].astype(F32) * slope
                    wide_f[at, lanes] = d
                    return c[0] + fold8(d), c[1] + fold8(d * zhat)

                if l == 0:
                    lax.fori_loop(0, rows // CH, body, 0, unroll=4)
                else:
                    first, second = lax.fori_loop(0, rows // CH, body, (zero(Q), zero(Q)), unroll=4)
                    pack(0, m, 0, q * Q, Q, first)
                    pack(0, m, 1, q * Q, Q, second)
            if l == 1:
                sum_start(0, m, Q)

        if l == 1:
            spill_zc.wait()
            spill_slc.wait()
        loop(2, output)
        if l == 0:
            spill_zc.start()
            spill_slc.start()

    store_small = [
        pltpu.make_async_copy(src, dst, out_sem.at[4 + i])
        for i, (src, dst) in enumerate(
            ((ggm_ref, ggm_out), (gsm_ref, gsm_out), (ggo_ref, ggo_out), (gso_ref, gso_out))
        )
    ]
    store_y = pltpu.make_async_copy(entry.at[2], y_out, out_sem.at[0])
    store_y.start()
    back_slc.start()
    grad_heads(False)
    table["H"].a()
    loop(2, lambda m: sum_middle(0, m, Q))
    grad_heads(True)
    store_y.wait()
    point(100)

    for l in (1, 0):
        if l == 0:
            load_we(0).wait()

        def back_out(m):
            total = sum_end(0, m, Q)
            rn = along(count[m, 0:1, :], Q)
            for q in range(4):
                lanes = slice(q * Q, (q + 1) * Q)
                sd, sz = total[q : q + 1], total[4 + q : 5 + q]
                gso_ref[l : l + 1, lanes] += sd
                ggo_ref[l : l + 1, lanes] += sz
                sd, sz = sd * rn, sz * rn
                gi = gic[l, m, 0:1, lanes]

                def body(i):
                    at = chunk(m, i)
                    v = along(valid_ref[at, :], Q)
                    zhat = zc[at, lanes].astype(F32)
                    dexp[at, lanes] = (v * gi * (wide_f[at, lanes] - (sd + zhat * sz))).astype(BF16)

                loop(rows // CH, body)
            mid_f[span(m), :] = dot(dexp[span(m), :], we[...])
            mid_back_sums(1, l, m, zb, slb)

        loop(2, back_out)
        if l == 1:
            load_we(0).start()
            back_zc.start()
        point(100 * l + 1)
        if l == 0:
            table["E1"].release()
        grad_tall(ger, dexp, actb[l], False)
        loop(2, lambda m: sum_middle(1, m, W4))
        point(100 * l + 2)
        table[f"E{l}"].a()
        grad_tall(ger, dexp, actb[l], True)
        point(100 * l + 3)
        if l == 0:
            load_ws(0).wait()

        grad_rows = [dcv.at[0], dcs.at[:, pl.ds(C, C)], dcv.at[1]]

        def back_conv(m):
            def store(at, value):
                low = value.astype(BF16)
                dcs[at, C : 2 * C] = low
                dcs[at, 0:C] = shifted(value, -1).astype(BF16)
                dcs[at, 2 * C : 3 * C] = shifted(value, 1).astype(BF16)

            mid_back(1, l, 1, m, zb, gib, store)
            halo_start(grad_rows, m)
            for c in range(3):
                taps_f[c, span(m), :] = dot(dcs[span(m), C : 2 * C], ws[(3 + c) * C : (4 + c) * C, :], NT)

        loop(2, back_conv)
        halo_pass(grad_rows)
        point(100 * l + 4)
        if l == 0:
            table["S1"].release()
        grad_spatial(l, 1)
        point(100 * l + 5)

        def back_rest(m):
            halo_wait(grad_rows, m)
            for c in range(3):
                taps_f[c, span(m), :] += dot(dcv[0, span(m), :], ws[(6 + c) * C : (7 + c) * C, :], NT) + dot(
                    dcv[1, span(m), :], ws[c * C : (c + 1) * C, :], NT
                )

            def body(i):
                at = chunk(m, i)
                mid_f[at, :] = taps_f[1, at, :] + shifted(taps_f[0, at, :], -1) + shifted(taps_f[2, at, :], 1)

            loop(rows // CH, body)
            mid_back_sums(2, l, m, za, sla)

        loop(2, back_rest)
        if l == 1:
            load_ws(0).start()
        point(100 * l + 6)
        grad_spatial(l, 0)
        if l == 0:
            grad_spatial(l, 2)
            table["S0"].a()
        loop(2, lambda m: sum_middle(2, m, W4))
        point(100 * l + 7)
        if l == 0:
            table["R1"].release()
            load_wr(0).start()
        if l == 1:
            grad_spatial(l, 2)
            table["S1"].a()
        point(100 * l + 8)
        if l == 0:
            load_wr(0).wait()

        if l == 1:
            back_zc.wait()
            back_slc.wait()

        def back_in(m):
            def store(at, value):
                dred[at, :] = value.astype(BF16)

            mid_back(2, l, 0, m, za, gia, store)
            for q in range(4 if l == 1 else 0):
                lanes = slice(q * Q, (q + 1) * Q)
                taps_f[0, span(m), 0:Q] = dot(dred[span(m), :], wr[lanes, :], NT)

                def body(i, c):
                    at = chunk(m, i)
                    d = (taps_f[0, at, 0:Q] + wide_f[at, lanes]) * slc[at, lanes].astype(F32)
                    wide_f[at, lanes] = d
                    return c[0] + fold8(d), c[1] + fold8(d * zc[at, lanes].astype(F32))

                first, second = lax.fori_loop(0, rows // CH, body, (zero(Q), zero(Q)), unroll=4)
                pack(0, m, 0, q * Q, Q, first)
                pack(0, m, 1, q * Q, Q, second)
            if l == 1:
                sum_start(0, m, Q)

        loop(2, back_in)
        if l == 1:
            point(109)
            grad_tall(wr, entry.at[1], dred[...], False)
            loop(2, lambda m: sum_middle(0, m, Q))
            point(110)
            table["R1"].a()
            grad_tall(wr, entry.at[1], dred[...], True)
            point(111)
        else:
            for p in range(4):
                we[tall(theirs[p]), :] = dot(entry[0, :, tall(theirs[p])], dred[...], TN).astype(BF16)
                table["R0"].a((p,))
            grad_tall(we, entry.at[0], dred[...], True)
            for copy in store_small:
                copy.start()
            point(9)

    for copy in store_small:
        copy.wait()
    pltpu.make_async_copy(dexp, dx_out, out_sem.at[1]).wait()
    for name in ("H", "E0", "S0", "R0"):
        table[name].release()
    for item in table.values():
        item.close()


def run_block(act, thr, cot, buckets, w_reduce, w_spatial, w_expand, w_heads, gm, sm, go, so):
    wide, batch = lax.axis_size("wide"), lax.axis_size("batch")
    M, D = act.shape
    C = w_reduce.shape[2]
    H = w_heads.shape[0]
    rows = M // 2
    Q = D // 4
    hbm = pl.BlockSpec(memory_space=pl.ANY)
    V, DMA = pltpu.VMEM, pltpu.SemaphoreType.DMA
    scratch = [
        V((D, C), BF16), V((9 * C, C), BF16), V((D, C), BF16), V((D // HB, H, HB), BF16),
        V((3, M, D), BF16), V((M, D), F32), V((M, D), BF16),
        V((M, H), BF16), V((H, M), BF16),
        V((2, 3, M, C), BF16), V((2, M, C), BF16), V((2, M, C), BF16),
        V((2, M, C), BF16), V((2, M, C), BF16), V((2, M, C), BF16),
        V((M, D), BF16), V((M, D), BF16),
        V((M, C), F32), V((3, M, C), F32),
        V((2, M, C), BF16), V((M, 3 * C), BF16), V((M, C), BF16),
        V((2, 2, 8, C), F32), V((2, 2, 8, C), F32), V((2, 2, 8, D), F32), V((2, 8, 128), F32),
        V((3, 2, 8, Q), F32), V((3, 2, 8, Q), F32),
        V((3, 2, wide, 8, Q), F32), V((3, 2, batch, 8, Q), F32),
        V((D, C), BF16), V((9 * C, C), BF16),
        V((5, H, HB), BF16), V((9, 9 * C // wide, C), BF16), V((3, 256, C), BF16), V((2, 256, C), BF16),
        V((rows, C), BF16),
        V((2, 2, C), F32), V((2, 2, C), F32), V((2, D), F32), V((2, D), F32), V((M, 128), F32),
        V((2, 2, C), F32), V((2, 2, C), F32), V((2, D), F32), V((2, D), F32),
        DMA((12,)), DMA((3, 2)), DMA((3, 2)), DMA((3, 2)), DMA((3, 2)),
        DMA((2, 2)), DMA((2, 2)), DMA, DMA, DMA((8,)), DMA((sum(4 + 5 * k for k in PIECES.values()),)),
    ]
    shape = jax.ShapeDtypeStruct
    return pl.pallas_call(
        functools.partial(block_kernel, (wide, batch, rows, D, C, H)),
        out_shape=[
            shape((M, D), BF16), shape((M, D), BF16),
            shape((2, D // wide, C), BF16), shape((2, 9 * C // wide, C), BF16), shape((2, D // wide, C), BF16), shape((H, D // wide), BF16),
            shape((2, 2, C), F32), shape((2, 2, C), F32), shape((2, D), F32), shape((2, D), F32),
            shape((M, D), BF16), shape((M, D), BF16),
        ],
        in_specs=[hbm] * 3 + [pl.BlockSpec(memory_space=pltpu.SMEM)] + [hbm] * 8,
        out_specs=[hbm] * 12,
        scratch_shapes=scratch,
        compiler_params=pltpu.CompilerParams(
            collective_id=7, has_side_effects=True, vmem_limit_bytes=VMEM_BYTES
        ),
    )(act, thr, cot, buckets, w_reduce, w_spatial, w_expand, w_heads, gm, sm, go, so)


def finish_kernel(n, *refs):
    ins, outs, held, wide, sems, out_sems = refs[:n], refs[n : 2 * n], refs[2 * n : 3 * n], refs[3 * n : -2], refs[-2], refs[-1]
    loads = [pltpu.make_async_copy(ins[i], held[i], sems.at[i]) for i in range(n)]
    for copy in loads:
        copy.start()
    stores = []
    w = 0
    for i in range(n):
        loads[i].wait()
        src = held[i]
        if ins[i].dtype != outs[i].dtype:
            src = wide[w]
            w += 1
            rows = 64
            if len(src.shape) == 2:
                def body(r, src=src, i=i):
                    at = pl.ds(pl.multiple_of(r * rows, rows), rows)
                    src[at, :] = held[i][at, :].astype(F32)

                loop(src.shape[0] // rows, body)
            else:
                for l in range(src.shape[0]):
                    def body(r, src=src, i=i, l=l):
                        at = pl.ds(pl.multiple_of(r * rows, rows), rows)
                        src[l, at, :] = held[i][l, at, :].astype(F32)

                    loop(src.shape[1] // rows, body)
        stores.append(pltpu.make_async_copy(src, outs[i], out_sems.at[i]))
        stores[-1].start()
    for copy in stores:
        copy.wait()


def finish(*arrays):
    hbm = pl.BlockSpec(memory_space=pl.ANY)
    n = len(arrays)
    widened = [a.dtype == BF16 and 2 <= i < 6 for i, a in enumerate(arrays)]
    out = [jax.ShapeDtypeStruct(a.shape, F32 if w else a.dtype) for a, w in zip(arrays, widened)]
    scratch = [pltpu.VMEM(a.shape, a.dtype) for a in arrays]
    scratch += [pltpu.VMEM(a.shape, F32) for a, w in zip(arrays, widened) if w]
    return pl.pallas_call(
        functools.partial(finish_kernel, n),
        out_shape=out,
        in_specs=[hbm] * n,
        out_specs=[hbm] * n,
        scratch_shapes=scratch + [pltpu.SemaphoreType.DMA((n,)), pltpu.SemaphoreType.DMA((n,))],
        compiler_params=pltpu.CompilerParams(vmem_limit_bytes=VMEM_BYTES),
    )(*arrays)


def shards_rows(
    activations, bucket_ids, thresholds, head_cot, w_reduce, w_spatial, w_expand,
    gain_mid, shift_mid, gain_out, shift_out, w_heads,
):
    micro, images, pixels, D = activations.shape
    M = micro * images * pixels
    L, _, C = w_reduce.shape
    H = head_cot.shape[-1]
    y, dx, gr, gs, ge, gh, ggm, gsm, ggo, gso, _, _ = run_block(
        activations.reshape(M, D), thresholds.reshape(M, D), head_cot.reshape(M, H), bucket_ids,
        w_reduce, w_spatial, w_expand, w_heads,
        gain_mid, shift_mid, gain_out, shift_out,
    )
    y, dx, gr, gs, ge, gh, ggm, gsm, ggo, gso = finish(y, dx, gr, gs, ge, gh, ggm, gsm, ggo, gso)

    return (
        y.reshape(activations.shape),
        dx.reshape(activations.shape),
        gr,
        gs,
        ge,
        ggm,
        gsm,
        ggo,
        gso,
        gh,
    )


def solution(mesh):
    placed = (
        P(None, "batch", "wide", None),
        P(None, "batch"),
        P(None, "batch", "wide", None),
        P(None, "batch", "wide", None),
        P(),
        P(),
        P(),
        P(),
        P(),
        P(),
        P(),
        P(),
    )
    def split(*arrays):
        micro, images, pixels, features = arrays[0].shape
        whole_rows = pixels == FRAME and FRAME == lax.axis_size("wide") and lax.axis_size("batch") == 4
        fits = micro == 2 and images * pixels == 256 and features == 2048 and arrays[4].shape[2] == 512
        return (shards_rows if whole_rows and fits else shards)(*arrays)

    return jax.shard_map(
        split,
        mesh=mesh,
        in_specs=placed,
        out_specs=(
            P(None, "batch", "wide", None),
            P(None, "batch", "wide", None),
            P(None, "wide", None),
            P(None, "wide", None),
            P(None, "wide", None),
            P(),
            P(),
            P(),
            P(),
            P(None, "wide"),
        ),
        check_vma=False,
    )
```
